32 devices in a mesh: groups: 2 (over y), frame: 4 (over z), head: 2 (over x), rep: 2 (over core).
Axes of the slice: x: 2, y: 2, z: 4, core: 2. Of those that a mesh axis runs over, the one named last changes fastest.
Arguments:
- latents: bfloat16 [4096, 1536], P(('groups', 'frame')), parts along dimension 0, may hold values from -6 to 6
- modulation: float32 [6, 1536], P('groups'), parts along dimension 0, may hold values from -3 to 3
- key_cache: bfloat16 [4096, 1024], P(('groups', 'frame'), ('head', 'rep')), parts along dimension 0, may hold values from -310 to 310
- value_cache: bfloat16 [4096, 1024], P(('groups', 'frame'), ('head', 'rep')), parts along dimension 0, may hold values from -5 to 5
- block_worker: int32 [32], P(('groups', 'frame')), parts along dimension 0, may hold values from -1 to 3, as said below
- query_weight: bfloat16 [1536, 1024], P(None, ('head', 'rep')), may hold values from -0.3125 to 0.3125
- key_weight: bfloat16 [1536, 1024], P(None, ('head', 'rep')), may hold values from -0.15625 to 0.15625
- value_weight: bfloat16 [1536, 1024], P(None, ('head', 'rep')), may hold values from -0.15625 to 0.15625
- out_weight: bfloat16 [1024, 1536], P(('head', 'rep')), may hold values from -0.75 to 0.75
Outputs:
- update: float32 [4096, 1536], P(('groups', 'frame', 'head', 'rep')), parts along dimension 0
The draws below stay inside these ranges and needn't reach their ends.
There are 2 independent parts, one for each index of `groups`. The reference program is written for one: setup_inputs(seed, part) draws one part's arguments, and reference() takes and returns one part's arrays. A program takes and returns all parts, laid end to end along the dimension named above; an argument that names none is the same for every part. Nothing has to cross between parts.
Inputs may be any that keep to these rules, and one draw needn't show every extreme that they name: `block_worker`: exactly 4 blocks hold a worker number; each number 0 to 3 is held by exactly one block, the other blocks hold -1.
All inputs are finite; a program needn't handle non-finite values.
Results may differ from the reference program's by a relative error of at most 0.0095.
The reference program's roundings to bfloat16 on the way count: a program that leaves them out, or rounds other values in their place, can miss the bound.
Values may be sent and summed in bfloat16 or wider, within the bound.
No kernel may reach another device: no remote copies, remote signals or barrier semaphores. Data moves between devices by JAX's collectives and lax.ppermute only.
A program may use at most 64 MiB of HBM per device.

```python
import jax
import jax.numpy as jnp
from jax import lax

D = 1536
HEADS = 8
HD = 128
ROWS = 128
NBLK = 16
TOKENS = 2048
N_FRAME = 4


def draw_key_cache(key, part):
    key = jax.random.fold_in(key, 5)
    base_key = jax.random.fold_in(key, 0)
    normal = jnp.clip(jax.random.normal(base_key, (TOKENS, HEADS * HD), jnp.float32), -5.0, 5.0)
    return normal.astype(jnp.bfloat16)


def draw_block_worker(key, part):
    key = jax.random.fold_in(key, 9)
    bias_key, full_key, noise_key, order_key = jax.random.split(key, 4)
    per_device = NBLK // N_FRAME
    bias = jax.random.randint(bias_key, (N_FRAME,), 0, 4, dtype=jnp.int32)
    full = jax.random.randint(full_key, (), 0, N_FRAME, dtype=jnp.int32)
    bias = jnp.where(jnp.arange(N_FRAME, dtype=jnp.int32) == full, 8, bias)
    block_ids = jnp.arange(NBLK, dtype=jnp.int32)
    noise = jax.random.randint(noise_key, (NBLK,), 0, 4096, dtype=jnp.int32)
    priority = (jnp.repeat(bias, per_device) * 4096 + noise) * NBLK + block_ids
    ranking = jnp.argsort(jnp.argsort(-priority)).astype(jnp.int32)
    chosen = ranking < N_FRAME
    second = jax.random.randint(order_key, (NBLK,), 0, 4096, dtype=jnp.int32) * NBLK + block_ids
    second = jnp.where(chosen, second, 4096 * NBLK + block_ids)
    ordering = jnp.argsort(jnp.argsort(second)).astype(jnp.int32)
    return jnp.where(chosen, ordering, -1).astype(jnp.int32)


def shard_levels(key, shape, pieces, smallest, high):
    loudness, own = 1.0, jax.random.fold_in(key, 6)
    for position, blocks in pieces:
        steps = jnp.exp(jax.random.uniform(jax.random.fold_in(own, position), (blocks,), jnp.float32, smallest / len(pieces), high / len(pieces)))
        loudness = loudness * jnp.repeat(steps, shape[position] // blocks).reshape([-1 if axis == position else 1 for axis in range(len(shape))])
    return loudness


def normal_values(key, shape, width, most, cuts=(), kind=jnp.bfloat16):
    drawn = width * jax.random.normal(key, shape, jnp.float32)
    if cuts:
        drawn = drawn * shard_levels(key, shape, cuts, -0.22, 0.18)
    return jnp.clip(drawn, -most, most).astype(kind)


def setup_inputs(seed: int = 0, part: int = 0) -> dict:
    splits = jax.random.split(jax.random.key(seed), 10)
    own_keys = jax.random.split(jax.random.fold_in(splits[9], part), 10)
    latents = normal_values(own_keys[0], (TOKENS, D), 1.0, 6.0, ((0, 4),))
    modulation = normal_values(own_keys[1], (3, D), 0.5, 3.0, (), jnp.float32)
    key_cache = draw_key_cache(jax.random.fold_in(jax.random.fold_in(splits[9], part), 71), part)
    value_cache = normal_values(own_keys[3], (TOKENS, HEADS * HD), 1.0, 5.0, ((0, 4), (1, 4)))
    block_worker = draw_block_worker(jax.random.fold_in(jax.random.fold_in(splits[9], part), 71), part)
    query_weight = normal_values(splits[5], (D, HEADS * HD), (D // 4) ** -0.5, 0.3125, ((1, 4),))
    key_weight = normal_values(splits[6], (D, HEADS * HD), D ** -0.5, 0.15625, ((1, 4),))
    value_weight = normal_values(splits[7], (D, HEADS * HD), D ** -0.5, 0.15625, ((1, 4),))
    out_weight = normal_values(splits[8], (HEADS * HD, D), (HEADS * HD // 16) ** -0.5, 0.75, ((0, 4),))
    return {"latents": latents, "modulation": modulation, "key_cache": key_cache, "value_cache": value_cache, "block_worker": block_worker, "query_weight": query_weight, "key_weight": key_weight, "value_weight": value_weight, "out_weight": out_weight}


def normalize(latents, modulation):
    floats = latents.astype(jnp.float32)
    center = floats - lax.optimization_barrier(jnp.mean(floats, axis=-1, keepdims=True))
    spread = lax.optimization_barrier(jnp.mean(center * center, axis=-1, keepdims=True))
    return (center * lax.rsqrt(spread + 1e-06) * (1.0 + modulation[1]) + modulation[0]).astype(jnp.bfloat16)

def reference(latents, modulation, key_cache, value_cache, block_worker, query_weight, key_weight, value_weight, out_weight):
    normed = normalize(latents, modulation)
    row_flags = jnp.repeat(block_worker >= 0, ROWS)[:, None]
    fresh_keys = jnp.dot(normed, key_weight, preferred_element_type=jnp.float32).astype(jnp.bfloat16)
    fresh_values = jnp.dot(normed, value_weight, preferred_element_type=jnp.float32).astype(jnp.bfloat16)
    key_rows = jnp.where(row_flags, fresh_keys, key_cache)
    value_rows = jnp.where(row_flags, fresh_values, value_cache)
    blocks = jnp.nonzero(block_worker >= 0, size=N_FRAME)[0].astype(jnp.int32)
    active_rows = (blocks[:, None] * ROWS + jnp.arange(ROWS, dtype=jnp.int32)[None, :]).reshape(-1).astype(jnp.int32)
    selected = normed[active_rows]
    queries = (jnp.dot(selected, query_weight, preferred_element_type=jnp.float32) * HD ** (-0.5)).astype(jnp.bfloat16)
    query_heads = jnp.transpose(queries.reshape(-1, HEADS, HD), (1, 0, 2))
    key_heads = jnp.transpose(key_rows.reshape(-1, HEADS, HD), (1, 0, 2))
    value_heads = jnp.transpose(value_rows.reshape(-1, HEADS, HD), (1, 0, 2))

    def attend_head(operands):
        query_part, key_part, value_part = operands
        scores = jnp.dot(query_part, key_part.T, preferred_element_type=jnp.float32)
        highest = lax.optimization_barrier(jnp.max(scores, axis=-1, keepdims=True))
        weights = jnp.exp(scores - highest)
        summed = jnp.dot(weights.astype(jnp.bfloat16), value_part, preferred_element_type=jnp.float32)
        return (summed / lax.optimization_barrier(jnp.sum(weights, axis=-1, keepdims=True))).astype(jnp.bfloat16)
    attended = lax.map(attend_head, (query_heads, key_heads, value_heads))
    attended = jnp.transpose(attended, (1, 0, 2)).reshape(-1, HEADS * HD)
    branch = jnp.dot(attended, out_weight, preferred_element_type=jnp.float32) * modulation[2]
    return jnp.zeros((TOKENS, D), jnp.float32).at[active_rows].set(branch)
```

```python
import functools

import jax
import jax.numpy as jnp
from jax import lax
from jax.experimental import pallas as pl
from jax.experimental.pallas import tpu as pltpu
from jax.sharding import PartitionSpec as P

HD = 128
EPS = 1e-06
CHUNK = 32
TAIL = 16
MIB = 1 << 20

VMEM = pl.BlockSpec(memory_space=pltpu.VMEM)
SMEM = pl.BlockSpec(memory_space=pltpu.SMEM)


def normalize_active(worker_ref, latents_ref, modulation_ref, normed_ref, block_rows):
    gain = 1.0 + modulation_ref[1:2, :]
    shift = modulation_ref[0:1, :]

    def one_block(j, carry):
        @pl.when(worker_ref[j] >= 0)
        def _():
            def one_chunk(c, inner):
                start = pl.multiple_of(j * block_rows + c * CHUNK, CHUNK)
                floats = latents_ref[pl.ds(start, CHUNK), :].astype(jnp.float32)
                center = floats - jnp.mean(floats, axis=-1, keepdims=True)
                spread = jnp.mean(center * center, axis=-1, keepdims=True)
                normed_ref[pl.ds(start, CHUNK), :] = (
                    center * lax.rsqrt(spread + EPS) * gain + shift
                ).astype(jnp.bfloat16)
                return inner

            lax.fori_loop(0, block_rows // CHUNK, one_chunk, 0)

        return carry

    lax.fori_loop(0, worker_ref.shape[0], one_block, 0)


def query_kernel(n_frame, worker_ref, latents_ref, modulation_ref, weight_ref, *rest):
    outs, (normed_ref, queries_ref) = rest[:n_frame], rest[n_frame:]
    n_local = worker_ref.shape[0]
    block_rows = latents_ref.shape[0] // n_local
    frame = lax.axis_index("frame")
    normalize_active(worker_ref, latents_ref, modulation_ref, normed_ref, block_rows)
    queries_ref[...] = (
        jnp.dot(normed_ref[...], weight_ref[...], preferred_element_type=jnp.float32) * HD ** (-0.5)
    ).astype(jnp.bfloat16)
    for s in range(n_frame):
        outs[s][...] = jnp.zeros_like(outs[s])
    for j in range(n_local):
        worker = worker_ref[j]
        away = lax.rem(worker - frame + n_frame, n_frame)
        for s in range(n_frame):

            @pl.when((worker >= 0) & (away == s))
            def _():
                outs[s][...] = queries_ref[j * block_rows : (j + 1) * block_rows, :]


def key_value_kernel(
    worker_ref,
    latents_ref,
    modulation_ref,
    key_weight_ref,
    value_weight_ref,
    key_cache_ref,
    value_cache_ref,
    keys_ref,
    values_t_ref,
    normed_ref,
):
    n_local = worker_ref.shape[0]
    block_rows = latents_ref.shape[0] // n_local
    normalize_active(worker_ref, latents_ref, modulation_ref, normed_ref, block_rows)
    for j in range(n_local):
        rows = slice(j * block_rows, (j + 1) * block_rows)

        @pl.when(worker_ref[j] >= 0)
        def _():
            normed = normed_ref[rows, :]
            keys_ref[rows, :] = jnp.dot(
                normed, key_weight_ref[...], preferred_element_type=jnp.float32
            ).astype(jnp.bfloat16)
            values_t_ref[:, rows] = (
                jnp.dot(normed, value_weight_ref[...], preferred_element_type=jnp.float32)
                .astype(jnp.bfloat16)
                .T
            )

        @pl.when(worker_ref[j] < 0)
        def _():
            keys_ref[rows, :] = key_cache_ref[rows, :]
            values_t_ref[:, rows] = value_cache_ref[rows, :].T


def three_terms(x):
    first = x.astype(jnp.bfloat16).astype(jnp.float32)
    rest = x - first
    second = rest.astype(jnp.bfloat16).astype(jnp.float32)
    return [first, second, rest - second]


def attend_kernel(queries_ref, keys_ref, values_t_ref, out_ref):
    width = keys_ref.shape[1]
    stats = []
    for h in range(width // HD):
        cols = slice(h * HD, (h + 1) * HD)
        scores = lax.dot_general(
            keys_ref[:, cols],
            queries_ref[:, cols],
            (((1,), (1,)), ((), ())),
            preferred_element_type=jnp.float32,
        )
        highest = jnp.max(scores, axis=0, keepdims=True)
        weights = jnp.exp(scores - highest)
        total = jnp.sum(weights, axis=0, keepdims=True)
        out_ref[cols, :] = jnp.dot(
            values_t_ref[cols, :], weights.astype(jnp.bfloat16), preferred_element_type=jnp.float32
        ).astype(jnp.bfloat16)
        stats += three_terms(highest) + three_terms(total)
    shape = (out_ref.shape[0] - width, out_ref.shape[1])
    row = lax.broadcasted_iota(jnp.int32, shape, 0)
    tail = jnp.zeros(shape, jnp.float32)
    for i, stat in enumerate(stats):
        tail = jnp.where(row == i, stat, tail)
    out_ref[width:, :] = tail.astype(jnp.bfloat16)


def combine_kernel(*refs):
    parts, out_ref = refs[:-1], refs[-1]
    width = out_ref.shape[1]
    tails = [part[width:, :].astype(jnp.float32) for part in parts]
    for h in range(width // HD):
        cols = slice(h * HD, (h + 1) * HD)

        def stat(tail, at):
            at += 6 * h
            return tail[at : at + 1, :] + tail[at + 1 : at + 2, :] + tail[at + 2 : at + 3, :]

        maxima = [stat(tail, 0) for tail in tails]
        highest = functools.reduce(jnp.maximum, maxima)
        factors = [jnp.exp(m - highest) for m in maxima]
        total = sum(stat(tail, 3) * factor for tail, factor in zip(tails, factors))
        summed = sum(
            part[cols, :].astype(jnp.float32) * factor for part, factor in zip(parts, factors)
        )
        out_ref[:, cols] = (summed / total).T.astype(jnp.bfloat16)


def select_kernel(n_frame, n_head, n_rep, worker_ref, *refs):
    slots, outs = refs[:n_frame], refs[n_frame:]
    block_rows = slots[0].shape[0]
    rows = outs[0].shape[0]
    frame = lax.axis_index("frame")
    head = lax.axis_index("head")
    rep = lax.axis_index("rep")
    for d in range(n_head * n_rep):
        target_head = lax.rem(head + d // n_rep, n_head)
        target = target_head * n_rep + lax.rem(rep + d % n_rep, n_rep)
        start = target * rows
        worker = worker_ref[start // block_rows]
        offset = pl.multiple_of(lax.rem(start, block_rows), rows)
        away = lax.rem(frame - worker + n_frame, n_frame)

        @pl.when(worker < 0)
        def _():
            outs[d][...] = jnp.zeros_like(outs[d])

        for s in range(n_frame):

            @pl.when((worker >= 0) & (away == s))
            def _():
                outs[d][...] = slots[s][pl.ds(offset, rows), :]


def project_kernel(n_rep, worker_ref, modulation_ref, *refs):
    refs, out_ref = refs[:-1], refs[-1]
    parts, weights = refs[: len(refs) // 2], refs[len(refs) // 2 :]
    rows, width = out_ref.shape
    n_devices = len(parts)
    block_rows = rows * n_devices // worker_ref.shape[0]
    place = lax.axis_index("head") * n_rep + lax.axis_index("rep")
    worker = worker_ref[place * rows // block_rows]

    @pl.when(worker >= 0)
    def _():
        step = 512
        for start in range(0, width, step):
            cols = slice(start, start + step)
            total = sum(
                jnp.dot(part[...], weight[:, cols], preferred_element_type=jnp.float32)
                for part, weight in zip(parts, weights)
            )
            out_ref[:, cols] = total * modulation_ref[2:3, cols]

    @pl.when(worker < 0)
    def _():
        out_ref[...] = jnp.zeros_like(out_ref)


def params(mib):
    return pltpu.CompilerParams(vmem_limit_bytes=mib * MIB)


def cost(flops, moved, exps=0):
    return pl.CostEstimate(flops=flops, bytes_accessed=moved, transcendentals=exps)


def per_device(
    n_frame,
    n_head,
    n_rep,
    latents,
    modulation,
    key_cache,
    value_cache,
    block_worker,
    query_weight,
    key_weight,
    value_weight,
    out_weight,
):
    tokens, model = latents.shape
    n_local = block_worker.shape[0]
    block_rows = tokens // n_local
    width = query_weight.shape[1]
    n_place = n_head * n_rep
    own_rows = tokens // n_place
    tail = TAIL * -(-6 * (width // HD) // TAIL)
    half = jnp.bfloat16

    def along_frame(x, shift):
        return lax.ppermute(x, "frame", [(i, (i + shift) % n_frame) for i in range(n_frame)])

    def along_head(x, shift):
        return lax.ppermute(x, "head", [(i, (i + shift) % n_head) for i in range(n_head)])

    def along_rep(x, shift):
        return lax.ppermute(x, "rep", [(i, (i + shift) % n_rep) for i in range(n_rep)])

    def in_frame(x, d):
        pairs = []
        for h in range(n_head):
            for r in range(n_rep):
                to = ((h + d // n_rep) % n_head) * n_rep + (r + d % n_rep) % n_rep
                pairs.append((h * n_rep + r, to))
        return lax.ppermute(x, ("head", "rep"), pairs)

    slots = pl.pallas_call(
        functools.partial(query_kernel, n_frame),
        out_shape=[jax.ShapeDtypeStruct((block_rows, width), half)] * n_frame,
        in_specs=[SMEM, VMEM, VMEM, VMEM],
        out_specs=[VMEM] * n_frame,
        scratch_shapes=[pltpu.VMEM((tokens, model), half), pltpu.VMEM((tokens, width), half)],
        compiler_params=params(20),
        cost_estimate=cost(2 * tokens * model * width, 2 * tokens * model + 2 * model * width),
        name="queries",
    )(block_worker, latents, modulation, query_weight)
    mine = slots[0]
    for s in range(1, n_frame):
        mine = mine + along_frame(slots[s], s)

    keys, values_t = pl.pallas_call(
        key_value_kernel,
        out_shape=[
            jax.ShapeDtypeStruct((tokens, width), half),
            jax.ShapeDtypeStruct((width, tokens), half),
        ],
        in_specs=[SMEM] + [VMEM] * 6,
        out_specs=[VMEM, VMEM],
        scratch_shapes=[pltpu.VMEM((tokens, model), half)],
        compiler_params=params(20),
        cost_estimate=cost(4 * tokens * model * width, 2 * tokens * model + 4 * model * width),
        name="keys_values",
    )(block_worker, latents, modulation, key_weight, value_weight, key_cache, value_cache)

    attend = pl.pallas_call(
        attend_kernel,
        out_shape=jax.ShapeDtypeStruct((width + tail, block_rows), half),
        in_specs=[VMEM] * 3,
        out_specs=VMEM,
        compiler_params=params(20),
        cost_estimate=cost(
            4 * tokens * block_rows * width, 4 * tokens * width, tokens * block_rows * width // HD
        ),
        name="attend",
    )
    shared = [mine] + [along_frame(mine, s) for s in range(1, n_frame)]
    partial = [attend(queries, keys, values_t) for queries in shared]
    gathered = partial[:1] + [along_frame(partial[s], n_frame - s) for s in range(1, n_frame)]
    attended = pl.pallas_call(
        combine_kernel,
        out_shape=jax.ShapeDtypeStruct((block_rows, width), half),
        in_specs=[VMEM] * n_frame,
        out_specs=VMEM,
        compiler_params=params(20),
        cost_estimate=cost(4 * n_frame * block_rows * width, 2 * n_frame * block_rows * width),
        name="combine",
    )(*gathered)
    copies = [attended] + [along_frame(attended, s) for s in range(1, n_frame)]
    pieces = pl.pallas_call(
        functools.partial(select_kernel, n_frame, n_head, n_rep),
        out_shape=[jax.ShapeDtypeStruct((own_rows, width), half)] * n_place,
        in_specs=[SMEM] + [VMEM] * n_frame,
        out_specs=[VMEM] * n_place,
        compiler_params=params(20),
        cost_estimate=cost(0, 4 * n_frame * block_rows * width),
        name="select",
    )(block_worker, *copies)
    pieces = [pieces[0]] + [in_frame(pieces[d], d) for d in range(1, n_place)]

    weights = []
    for dh in range(n_head):
        across = along_head(out_weight, dh) if dh else out_weight
        for dr in range(n_rep):
            weights.append(along_rep(across, dr) if dr else across)
    return pl.pallas_call(
        functools.partial(project_kernel, n_rep),
        out_shape=jax.ShapeDtypeStruct((own_rows, model), jnp.float32),
        in_specs=[SMEM] + [VMEM] * (1 + 2 * n_place),
        out_specs=VMEM,
        compiler_params=params(20),
        cost_estimate=cost(2 * own_rows * model * width * n_place, 2 * model * width * n_place),
        name="project",
    )(block_worker, modulation, *pieces, *weights)


def solution(mesh):
    in_specs = (
        P(("groups", "frame"), None),
        P("groups", None),
        P(("groups", "frame"), ("head", "rep")),
        P(("groups", "frame"), ("head", "rep")),
        P(("groups", "frame")),
        P(None, ("head", "rep")),
        P(None, ("head", "rep")),
        P(None, ("head", "rep")),
        P(("head", "rep"), None),
    )
    out_specs = P(("groups", "frame", "head", "rep"), None)
    body = functools.partial(
        per_device, mesh.shape["frame"], mesh.shape["head"], mesh.shape["rep"]
    )
    return jax.shard_map(body, mesh=mesh, in_specs=in_specs, out_specs=out_specs, check_vma=False)
```

```python
import functools

import jax
import jax.numpy as jnp
from jax import lax
from jax.experimental import pallas as pl
from jax.experimental.pallas import tpu as pltpu
from jax.sharding import PartitionSpec as P

HD = 128
EPS = 1e-06
CHUNK = 16
COLUMNS = 512
SLOTS = 3
TAIL = 16
MIB = 1 << 20

VMEM = pl.BlockSpec(memory_space=pltpu.VMEM)
HBM = pl.BlockSpec(memory_space=pltpu.HBM)
ANY = pl.BlockSpec(memory_space=pl.ANY)


def normalize_block(latents_ref, modulation_ref, normed_ref, start, block_rows):
    def one_chunk(c, carry):
        at = pl.multiple_of(start + c * CHUNK, CHUNK)
        floats = latents_ref[pl.ds(at, CHUNK), :].astype(jnp.float32)
        center = floats - jnp.mean(floats, axis=-1, keepdims=True)
        spread = jnp.mean(center * center, axis=-1, keepdims=True)
        normed_ref[pl.ds(at, CHUNK), :] = (
            center * lax.rsqrt(spread + EPS) * (1.0 + modulation_ref[1:2, :])
            + modulation_ref[0:1, :]
        ).astype(jnp.bfloat16)
        return carry

    lax.fori_loop(0, block_rows // CHUNK, one_chunk, 0, unroll=4)


def query_kernel(n_frame, worker_in, latents_in, modulation_in, weight_in, *rest):
    outs = rest[:n_frame]
    worker_ref, latents_ref, modulation_ref, weight_ref, normed_ref, queries_ref, sems = rest[
        n_frame:
    ]
    n_local = worker_ref.shape[0]
    block_rows = latents_ref.shape[0] // n_local
    frame = lax.axis_index("frame")
    blocks = [slice(j * block_rows, (j + 1) * block_rows) for j in range(n_local)]
    first = [
        pltpu.make_async_copy(worker_in, worker_ref, sems.at[0]),
        pltpu.make_async_copy(modulation_in, modulation_ref, sems.at[1]),
    ]
    each = [
        pltpu.make_async_copy(latents_in.at[rows, :], latents_ref.at[rows, :], sems.at[3 + j])
        for j, rows in enumerate(blocks)
    ]
    weight = pltpu.make_async_copy(weight_in, weight_ref, sems.at[2])
    for copy in first + each + [weight]:
        copy.start()
    for s in range(n_frame):
        outs[s][...] = jnp.zeros_like(outs[s])
    for copy in first:
        copy.wait()
    for j in range(n_local):
        each[j].wait()

        @pl.when(worker_ref[j] >= 0)
        def _():
            normalize_block(latents_ref, modulation_ref, normed_ref, j * block_rows, block_rows)

    weight.wait()
    queries_ref[...] = (
        jnp.dot(normed_ref[...], weight_ref[...], preferred_element_type=jnp.float32) * HD ** (-0.5)
    ).astype(jnp.bfloat16)
    for j in range(n_local):
        worker = worker_ref[j]
        away = lax.rem(worker - frame + n_frame, n_frame)
        for s in range(n_frame):

            @pl.when((worker >= 0) & (away == s))
            def _():
                outs[s][...] = queries_ref[blocks[j], :]


def key_value_kernel(
    n_frame,
    n_head,
    n_rep,
    worker_in,
    latents_in,
    modulation_in,
    key_weight_in,
    value_weight_in,
    key_cache_in,
    value_cache_in,
    keys_ref,
    values_t_ref,
    masks_ref,
    worker_ref,
    latents_ref,
    modulation_ref,
    key_weight_ref,
    value_weight_ref,
    value_cache_ref,
    normed_ref,
    fresh_ref,
    sems,
):
    n_local = worker_ref.shape[0]
    tokens = latents_ref.shape[0]
    block_rows = tokens // n_local
    blocks = [slice(j * block_rows, (j + 1) * block_rows) for j in range(n_local)]
    first = [
        pltpu.make_async_copy(worker_in, worker_ref, sems.at[0]),
        pltpu.make_async_copy(modulation_in, modulation_ref, sems.at[1]),
        pltpu.make_async_copy(latents_in, latents_ref, sems.at[2]),
    ]
    second = [
        pltpu.make_async_copy(key_weight_in, key_weight_ref, sems.at[3]),
        pltpu.make_async_copy(value_weight_in, value_weight_ref, sems.at[4]),
        pltpu.make_async_copy(key_cache_in, keys_ref, sems.at[5]),
        pltpu.make_async_copy(value_cache_in, value_cache_ref, sems.at[6]),
    ]
    for copy in first + second:
        copy.start()
    for copy in first:
        copy.wait()
    frame, head, rep = lax.axis_index("frame"), lax.axis_index("head"), lax.axis_index("rep")
    n_place = n_head * n_rep
    for d in range(n_place):
        target = lax.rem(head + d // n_rep, n_head) * n_rep + lax.rem(rep + d % n_rep, n_rep)
        worker = worker_ref[target * (tokens // n_place) // block_rows]
        away = jnp.where(worker < 0, -1, lax.rem(frame - worker + n_frame, n_frame))
        for s in range(n_frame):
            masks_ref[d * n_frame + s : d * n_frame + s + 1, :] = jnp.full(
                (1, masks_ref.shape[1]), jnp.where(away == s, 1.0, 0.0), jnp.float32
            )
    for j in range(n_local):

        @pl.when(worker_ref[j] >= 0)
        def _():
            normalize_block(latents_ref, modulation_ref, normed_ref, j * block_rows, block_rows)

    for copy in second:
        copy.wait()
    fresh_ref[...] = jnp.dot(
        normed_ref[...], key_weight_ref[...], preferred_element_type=jnp.float32
    ).astype(jnp.bfloat16)
    for j in range(n_local):

        @pl.when(worker_ref[j] >= 0)
        def _():
            keys_ref[blocks[j], :] = fresh_ref[blocks[j], :]

    fresh_ref[...] = jnp.dot(
        normed_ref[...], value_weight_ref[...], preferred_element_type=jnp.float32
    ).astype(jnp.bfloat16)
    for j in range(n_local):

        @pl.when(worker_ref[j] >= 0)
        def _():
            value_cache_ref[blocks[j], :] = fresh_ref[blocks[j], :]

    for h in range(keys_ref.shape[1] // HD):
        cols = slice(h * HD, (h + 1) * HD)
        values_t_ref[cols, :] = value_cache_ref[:, cols].T


def three_terms(x):
    first = x.astype(jnp.bfloat16).astype(jnp.float32)
    rest = x - first
    second = rest.astype(jnp.bfloat16).astype(jnp.float32)
    return [first, second, rest - second]


def collect_kernel(*refs):
    *parts, _, out_ref = refs
    out_ref[...] = sum(part[...].astype(jnp.float32) for part in parts).astype(jnp.bfloat16)


def attend_kernel(count, *refs):
    keys_ref, values_t_ref = refs[count : count + 2]
    for queries_ref, out_ref in zip(refs[:count], refs[-count:]):
        attend_slot(queries_ref, keys_ref, values_t_ref, out_ref)


def attend_slot(queries_ref, keys_ref, values_t_ref, out_ref):
    width = keys_ref.shape[1]
    stats = []
    for h in range(width // HD):
        cols = slice(h * HD, (h + 1) * HD)
        scores = lax.dot_general(
            keys_ref[:, cols],
            queries_ref[:, cols],
            (((1,), (1,)), ((), ())),
            preferred_element_type=jnp.float32,
        )
        highest = jnp.max(scores, axis=0, keepdims=True)
        weights = jnp.exp(scores - highest)
        total = jnp.sum(weights, axis=0, keepdims=True)
        out_ref[cols, :] = jnp.dot(
            values_t_ref[cols, :], weights.astype(jnp.bfloat16), preferred_element_type=jnp.float32
        ).astype(jnp.bfloat16)
        stats += three_terms(highest) + three_terms(total)
    shape = (out_ref.shape[0] - width, out_ref.shape[1])
    row = lax.broadcasted_iota(jnp.int32, shape, 0)
    tail = jnp.zeros(shape, jnp.float32)
    for i, stat in enumerate(stats):
        tail = jnp.where(row == i, stat, tail)
    out_ref[width:, :] = tail.astype(jnp.bfloat16)


def combine_kernel(n_frame, *refs):
    parts, out_ref = refs[:n_frame], refs[n_frame + (len(refs) - n_frame - 1) // 2]
    width = out_ref.shape[1]
    tails = [part[width:, :].astype(jnp.float32) for part in parts]
    for h in range(width // HD):
        cols = slice(h * HD, (h + 1) * HD)

        def stat(tail, at):
            at += 6 * h
            return tail[at : at + 1, :] + tail[at + 1 : at + 2, :] + tail[at + 2 : at + 3, :]

        maxima = [stat(tail, 0) for tail in tails]
        highest = functools.reduce(jnp.maximum, maxima)
        factors = [jnp.exp(m - highest) for m in maxima]
        total = sum(stat(tail, 3) * factor for tail, factor in zip(tails, factors))
        summed = sum(
            part[cols, :].astype(jnp.float32) * factor for part, factor in zip(parts, factors)
        )
        out_ref[:, cols] = (summed / total).T.astype(jnp.bfloat16)


def select_kernel(n_frame, n_head, n_rep, *refs):
    slots, masks_ref, outs = refs[:n_frame], refs[n_frame], refs[n_frame + 1 :]
    block_rows, width = slots[0].shape
    rows = outs[0].shape[0]
    head, rep = lax.axis_index("head"), lax.axis_index("rep")
    for d in range(n_head * n_rep):
        if rows == block_rows:
            some = slice(None)
        else:
            target = lax.rem(head + d // n_rep, n_head) * n_rep + lax.rem(rep + d % n_rep, n_rep)
            some = pl.ds(pl.multiple_of(lax.rem(target * rows, block_rows), rows), rows)
        for h in range(width // HD):
            cols = slice(h * HD, (h + 1) * HD)
            chosen = jnp.zeros((rows, HD), jnp.float32)
            for s in range(n_frame):
                mask = masks_ref[d * n_frame + s : d * n_frame + s + 1, :]
                chosen = jnp.where(mask > 0.5, slots[s][some, cols].astype(jnp.float32), chosen)
            outs[d][:, cols] = chosen.astype(jnp.bfloat16)


def project_kernel(modulation_ref, *refs):
    refs, out_ref = refs[:-1], refs[-1]
    parts, weights = refs[: len(refs) // 2], refs[len(refs) // 2 :]
    width = out_ref.shape[1]
    for start in range(0, width, COLUMNS):
        cols = slice(start, start + COLUMNS)
        total = sum(
            jnp.dot(part[...], weight[:, cols], preferred_element_type=jnp.float32)
            for part, weight in zip(parts, weights)
        )
        out_ref[:, cols] = total * modulation_ref[2:3, cols]


def params(mib):
    return pltpu.CompilerParams(vmem_limit_bytes=mib * MIB)


def cost(flops, moved, exps=0):
    return pl.CostEstimate(flops=flops, bytes_accessed=moved, transcendentals=exps)


def per_device(
    n_frame,
    n_head,
    n_rep,
    latents,
    modulation,
    key_cache,
    value_cache,
    block_worker,
    query_weight,
    key_weight,
    value_weight,
    out_weight,
):
    tokens, model = latents.shape
    n_local = block_worker.shape[0]
    block_rows = tokens // n_local
    width = query_weight.shape[1]
    n_place = n_head * n_rep
    own_rows = tokens // n_place
    tail = TAIL * -(-6 * (width // HD) // TAIL)
    half = jnp.bfloat16

    def along_frame(x, shift):
        return lax.ppermute(x, "frame", [(i, (i + shift) % n_frame) for i in range(n_frame)])

    def along_head(x, shift):
        return lax.ppermute(x, "head", [(i, (i + shift) % n_head) for i in range(n_head)])

    def along_rep(x, shift):
        return lax.ppermute(x, "rep", [(i, (i + shift) % n_rep) for i in range(n_rep)])

    def in_frame(x, d):
        pairs = []
        for h in range(n_head):
            for r in range(n_rep):
                to = ((h + d // n_rep) % n_head) * n_rep + (r + d % n_rep) % n_rep
                pairs.append((h * n_rep + r, to))
        return lax.ppermute(x, ("head", "rep"), pairs)

    across = [along_head(out_weight, dh) for dh in range(1, n_head)]

    slots = pl.pallas_call(
        functools.partial(query_kernel, n_frame),
        out_shape=[jax.ShapeDtypeStruct((block_rows, width), half)] * n_frame,
        in_specs=[HBM] * 4,
        out_specs=[VMEM] * n_frame,
        scratch_shapes=[
            pltpu.SMEM(block_worker.shape, jnp.int32),
            pltpu.VMEM(latents.shape, half),
            pltpu.VMEM(modulation.shape, jnp.float32),
            pltpu.VMEM(query_weight.shape, half),
            pltpu.VMEM(latents.shape, half),
            pltpu.VMEM((tokens, width), half),
            pltpu.SemaphoreType.DMA((3 + n_local,)),
        ],
        compiler_params=params(60),
        cost_estimate=cost(2 * tokens * model * width, 2 * tokens * model + 2 * model * width),
        name="queries",
    )(block_worker, latents, modulation, query_weight)
    arrived = [along_frame(slots[s], s) for s in range(1, n_frame)]

    keys, values_t, masks = pl.pallas_call(
        functools.partial(key_value_kernel, n_frame, n_head, n_rep),
        out_shape=[
            jax.ShapeDtypeStruct((tokens, width), half),
            jax.ShapeDtypeStruct((width, tokens), half),
            jax.ShapeDtypeStruct((n_place * n_frame, HD), jnp.float32),
        ],
        in_specs=[HBM] * 7,
        out_specs=[VMEM] * 3,
        scratch_shapes=[
            pltpu.SMEM(block_worker.shape, jnp.int32),
            pltpu.VMEM(latents.shape, half),
            pltpu.VMEM(modulation.shape, jnp.float32),
            pltpu.VMEM(key_weight.shape, half),
            pltpu.VMEM(value_weight.shape, half),
            pltpu.VMEM(value_cache.shape, half),
            pltpu.VMEM(latents.shape, half),
            pltpu.VMEM((tokens, width), half),
            pltpu.SemaphoreType.DMA((7,)),
        ],
        compiler_params=params(53),
        cost_estimate=cost(4 * tokens * model * width, 2 * tokens * model + 4 * model * width),
        name="keys_values",
    )(block_worker, latents, modulation, key_weight, value_weight, key_cache, value_cache)

    mine = pl.pallas_call(
        collect_kernel,
        out_shape=jax.ShapeDtypeStruct((block_rows, width), half),
        in_specs=[VMEM] * n_frame + [ANY],
        out_specs=VMEM,
        compiler_params=params(16),
        cost_estimate=cost(n_frame * block_rows * width, 2 * n_frame * block_rows * width),
        name="collect",
    )(slots[0], *arrived, masks)

    def attend(queries, after=()):
        count = len(queries)
        return pl.pallas_call(
            functools.partial(attend_kernel, count),
            out_shape=[jax.ShapeDtypeStruct((width + tail, block_rows), half)] * count,
            in_specs=[VMEM] * (count + 2) + [ANY] * len(after),
            out_specs=[VMEM] * count,
            compiler_params=params(16),
            cost_estimate=cost(
                4 * tokens * block_rows * width * count,
                4 * tokens * width,
                tokens * block_rows * width // HD * count,
            ),
            name="attend",
        )(*queries, keys, values_t, *after)

    partial = list(attend([mine]))
    shared = [along_frame(mine, s) for s in range(1, n_frame)]
    for start in range(0, n_frame - 1, SLOTS):
        partial += attend(shared[start : start + SLOTS], partial[:1])
    gathered = partial[:1] + [along_frame(partial[s], n_frame - s) for s in range(1, n_frame)]
    attended, *across = pl.pallas_call(
        functools.partial(combine_kernel, n_frame),
        out_shape=[jax.ShapeDtypeStruct((block_rows, width), half)]
        + [jax.ShapeDtypeStruct(w.shape, w.dtype) for w in across],
        in_specs=[VMEM] * n_frame + [ANY] * len(across),
        out_specs=[VMEM] + [ANY] * len(across),
        input_output_aliases={n_frame + h: 1 + h for h in range(len(across))},
        compiler_params=params(16),
        cost_estimate=cost(4 * n_frame * block_rows * width, 2 * n_frame * block_rows * width),
        name="combine",
    )(*gathered, *across)
    copies = [attended] + [along_frame(attended, s) for s in range(1, n_frame)]
    pieces = pl.pallas_call(
        functools.partial(select_kernel, n_frame, n_head, n_rep),
        out_shape=[jax.ShapeDtypeStruct((own_rows, width), half)] * n_place,
        in_specs=[VMEM] * (n_frame + 1),
        out_specs=[VMEM] * n_place,
        compiler_params=params(16),
        cost_estimate=cost(0, 4 * n_frame * block_rows * width),
        name="select",
    )(*copies, masks)
    pieces = [pieces[0]] + [in_frame(pieces[d], d) for d in range(1, n_place)]

    weights = []
    for held in [out_weight] + across:
        weights += [held] + [along_rep(held, dr) for dr in range(1, n_rep)]
    return pl.pallas_call(
        project_kernel,
        out_shape=jax.ShapeDtypeStruct((own_rows, model), jnp.float32),
        in_specs=[VMEM] * (1 + 2 * n_place),
        out_specs=VMEM,
        compiler_params=params(16),
        cost_estimate=cost(2 * own_rows * model * width * n_place, 2 * model * width * n_place),
        name="project",
    )(modulation, *pieces, *weights)


def solution(mesh):
    in_specs = (
        P(("groups", "frame"), None),
        P("groups", None),
        P(("groups", "frame"), ("head", "rep")),
        P(("groups", "frame"), ("head", "rep")),
        P(("groups", "frame")),
        P(None, ("head", "rep")),
        P(None, ("head", "rep")),
        P(None, ("head", "rep")),
        P(("head", "rep"), None),
    )
    out_specs = P(("groups", "frame", "head", "rep"), None)
    body = functools.partial(
        per_device, mesh.shape["frame"], mesh.shape["head"], mesh.shape["rep"]
    )
    return jax.shard_map(body, mesh=mesh, in_specs=in_specs, out_specs=out_specs, check_vma=False)
```

```python
import functools

import jax
import jax.numpy as jnp
from jax import lax
from jax.experimental import pallas as pl
from jax.experimental.pallas import tpu as pltpu
from jax.sharding import PartitionSpec as P

HD = 128
EPS = 1e-06
CHUNK = 16
COLUMNS = 512
SLOTS = 4
TAIL = 16
MIB = 1 << 20

VMEM = pl.BlockSpec(memory_space=pltpu.VMEM)
HBM = pl.BlockSpec(memory_space=pltpu.HBM)
ANY = pl.BlockSpec(memory_space=pl.ANY)


def normalize_block(latents_ref, modulation_ref, normed_ref, start, block_rows):
    def one_chunk(c, carry):
        at = pl.multiple_of(start + c * CHUNK, CHUNK)
        floats = latents_ref[pl.ds(at, CHUNK), :].astype(jnp.float32)
        center = floats - jnp.mean(floats, axis=-1, keepdims=True)
        spread = jnp.mean(center * center, axis=-1, keepdims=True)
        normed_ref[pl.ds(at, CHUNK), :] = (
            center * lax.rsqrt(spread + EPS) * (1.0 + modulation_ref[1:2, :])
            + modulation_ref[0:1, :]
        ).astype(jnp.bfloat16)
        return carry

    lax.fori_loop(0, block_rows // CHUNK, one_chunk, 0, unroll=4)


def query_kernel(n_frame, worker_in, latents_in, modulation_in, weight_in, *rest):
    outs = rest[:n_frame]
    worker_ref, latents_ref, modulation_ref, weight_ref, normed_ref, queries_ref, sems = rest[
        n_frame:
    ]
    n_local = worker_ref.shape[0]
    block_rows = latents_ref.shape[0] // n_local
    frame = lax.axis_index("frame")
    blocks = [slice(j * block_rows, (j + 1) * block_rows) for j in range(n_local)]
    first = [
        pltpu.make_async_copy(worker_in, worker_ref, sems.at[0]),
        pltpu.make_async_copy(modulation_in, modulation_ref, sems.at[1]),
    ]
    each = [
        pltpu.make_async_copy(latents_in.at[rows, :], latents_ref.at[rows, :], sems.at[3 + j])
        for j, rows in enumerate(blocks)
    ]
    weight = pltpu.make_async_copy(weight_in, weight_ref, sems.at[2])
    for copy in first + each + [weight]:
        copy.start()
    for s in range(n_frame):
        outs[s][...] = jnp.zeros_like(outs[s])
    for copy in first:
        copy.wait()
    for j in range(n_local):
        each[j].wait()

        @pl.when(worker_ref[j] >= 0)
        def _():
            normalize_block(latents_ref, modulation_ref, normed_ref, j * block_rows, block_rows)

    weight.wait()
    queries_ref[...] = (
        jnp.dot(normed_ref[...], weight_ref[...], preferred_element_type=jnp.float32) * HD ** (-0.5)
    ).astype(jnp.bfloat16)
    for j in range(n_local):
        worker = worker_ref[j]
        away = lax.rem(worker - frame + n_frame, n_frame)
        for s in range(n_frame):

            @pl.when((worker >= 0) & (away == s))
            def _():
                outs[s][...] = queries_ref[blocks[j], :]


def key_value_kernel(
    n_frame,
    n_place,
    worker_in,
    latents_in,
    modulation_in,
    key_weight_in,
    value_weight_in,
    key_cache_in,
    value_cache_in,
    keys_ref,
    values_t_ref,
    masks_ref,
    worker_ref,
    latents_ref,
    modulation_ref,
    key_weight_ref,
    value_weight_ref,
    value_cache_ref,
    normed_ref,
    fresh_ref,
    sems,
):
    n_local = worker_ref.shape[0]
    tokens = latents_ref.shape[0]
    block_rows = tokens // n_local
    blocks = [slice(j * block_rows, (j + 1) * block_rows) for j in range(n_local)]
    first = [
        pltpu.make_async_copy(worker_in, worker_ref, sems.at[0]),
        pltpu.make_async_copy(modulation_in, modulation_ref, sems.at[1]),
        pltpu.make_async_copy(latents_in, latents_ref, sems.at[2]),
    ]
    second = [
        pltpu.make_async_copy(key_weight_in, key_weight_ref, sems.at[3]),
        pltpu.make_async_copy(value_weight_in, value_weight_ref, sems.at[4]),
        pltpu.make_async_copy(key_cache_in, keys_ref, sems.at[5]),
        pltpu.make_async_copy(value_cache_in, value_cache_ref, sems.at[6]),
    ]
    for copy in first + second:
        copy.start()
    for copy in first:
        copy.wait()
    for p in range(n_place):
        worker = worker_ref[p * (tokens // n_place) // block_rows]
        for s in range(n_frame):
            masks_ref[p * n_frame + s : p * n_frame + s + 1, :] = jnp.full(
                (1, masks_ref.shape[1]), jnp.where(worker == s, 1.0, 0.0), jnp.float32
            )
    for j in range(n_local):

        @pl.when(worker_ref[j] >= 0)
        def _():
            normalize_block(latents_ref, modulation_ref, normed_ref, j * block_rows, block_rows)

    for copy in second:
        copy.wait()
    fresh_ref[...] = jnp.dot(
        normed_ref[...], key_weight_ref[...], preferred_element_type=jnp.float32
    ).astype(jnp.bfloat16)
    for j in range(n_local):

        @pl.when(worker_ref[j] >= 0)
        def _():
            keys_ref[blocks[j], :] = fresh_ref[blocks[j], :]

    fresh_ref[...] = jnp.dot(
        normed_ref[...], value_weight_ref[...], preferred_element_type=jnp.float32
    ).astype(jnp.bfloat16)
    for j in range(n_local):

        @pl.when(worker_ref[j] >= 0)
        def _():
            value_cache_ref[blocks[j], :] = fresh_ref[blocks[j], :]

    for h in range(keys_ref.shape[1] // HD):
        cols = slice(h * HD, (h + 1) * HD)
        values_t_ref[cols, :] = value_cache_ref[:, cols].T


def three_terms(x):
    first = x.astype(jnp.bfloat16).astype(jnp.float32)
    rest = x - first
    second = rest.astype(jnp.bfloat16).astype(jnp.float32)
    return [first, second, rest - second]


def collect_kernel(*refs):
    *parts, _, out_ref = refs
    mine = sum(part[...].astype(jnp.float32) for part in parts).astype(jnp.bfloat16)
    for s in range(out_ref.shape[0]):
        out_ref[s] = mine


def attend_kernel(queries_ref, keys_ref, values_t_ref, out_ref):
    count = queries_ref.shape[0]

    def one_slot(s, carry):
        attend_slot(queries_ref.at[s], keys_ref, values_t_ref, out_ref.at[s])
        return carry

    lax.fori_loop(0, count, one_slot, 0, unroll=min(count, SLOTS))


def attend_slot(queries_ref, keys_ref, values_t_ref, out_ref):
    width = keys_ref.shape[1]
    stats = []
    for h in range(width // HD):
        cols = slice(h * HD, (h + 1) * HD)
        scores = lax.dot_general(
            keys_ref[:, cols],
            queries_ref[:, cols],
            (((1,), (1,)), ((), ())),
            preferred_element_type=jnp.float32,
        )
        highest = jnp.max(scores, axis=0, keepdims=True)
        weights = jnp.exp(scores - highest)
        total = jnp.sum(weights, axis=0, keepdims=True)
        out_ref[cols, :] = jnp.dot(
            values_t_ref[cols, :], weights.astype(jnp.bfloat16), preferred_element_type=jnp.float32
        ).astype(jnp.bfloat16)
        stats += three_terms(highest) + three_terms(total)
    shape = (out_ref.shape[0] - width, out_ref.shape[1])
    row = lax.broadcasted_iota(jnp.int32, shape, 0)
    tail = jnp.zeros(shape, jnp.float32)
    for i, stat in enumerate(stats):
        tail = jnp.where(row == i, stat, tail)
    out_ref[width:, :] = tail.astype(jnp.bfloat16)


def combine_kernel(parts_ref, *refs):
    out_ref = refs[len(refs) // 2]
    count, _, width = out_ref.shape
    parts = [parts_ref.at[s] for s in range(count)]
    tails = [part[width:, :].astype(jnp.float32) for part in parts]
    for h in range(width // HD):
        cols = slice(h * HD, (h + 1) * HD)

        def stat(tail, at):
            at += 6 * h
            return tail[at : at + 1, :] + tail[at + 1 : at + 2, :] + tail[at + 2 : at + 3, :]

        maxima = [stat(tail, 0) for tail in tails]
        highest = functools.reduce(jnp.maximum, maxima)
        factors = [jnp.exp(m - highest) for m in maxima]
        total = sum(stat(tail, 3) * factor for tail, factor in zip(tails, factors))
        summed = sum(
            part[cols, :].astype(jnp.float32) * factor for part, factor in zip(parts, factors)
        )
        attended = (summed / total).T.astype(jnp.bfloat16)
        for s in range(count):
            out_ref[s, :, cols] = attended


def select_kernel(n_place, slots_ref, masks_ref, out_ref):
    n_frame, block_rows, width = slots_ref.shape
    rows = out_ref.shape[1]
    for p in range(n_place):
        start = p * rows % block_rows
        for h in range(width // HD):
            cols = slice(h * HD, (h + 1) * HD)
            chosen = jnp.zeros((rows, HD), jnp.float32)
            for s in range(n_frame):
                mask = masks_ref[p * n_frame + s : p * n_frame + s + 1, :]
                slot = slots_ref[s, start : start + rows, cols].astype(jnp.float32)
                chosen = jnp.where(mask > 0.5, slot, chosen)
            out_ref[p, :, cols] = chosen.astype(jnp.bfloat16)


def project_kernel(n_head, n_rep, modulation_ref, parts_ref, *refs):
    weights, out_ref = refs[:-1], refs[-1]
    head, rep = lax.axis_index("head"), lax.axis_index("rep")
    width = out_ref.shape[1]
    parts = []
    for d in range(n_head * n_rep):
        source_head = lax.rem(head + n_head - d // n_rep, n_head)
        parts.append(parts_ref[source_head * n_rep + lax.rem(rep + n_rep - d % n_rep, n_rep)])
    for start in range(0, width, COLUMNS):
        cols = slice(start, start + COLUMNS)
        total = sum(
            jnp.dot(part, weight[:, cols], preferred_element_type=jnp.float32)
            for part, weight in zip(parts, weights)
        )
        out_ref[:, cols] = total * modulation_ref[2:3, cols]


def params(mib):
    return pltpu.CompilerParams(vmem_limit_bytes=mib * MIB)


def cost(flops, moved, exps=0):
    return pl.CostEstimate(flops=flops, bytes_accessed=moved, transcendentals=exps)


def per_device(
    n_frame,
    n_head,
    n_rep,
    latents,
    modulation,
    key_cache,
    value_cache,
    block_worker,
    query_weight,
    key_weight,
    value_weight,
    out_weight,
):
    tokens, model = latents.shape
    n_local = block_worker.shape[0]
    block_rows = tokens // n_local
    width = query_weight.shape[1]
    n_place = n_head * n_rep
    own_rows = tokens // n_place
    tail = TAIL * -(-6 * (width // HD) // TAIL)
    half = jnp.bfloat16

    def along_frame(x, shift):
        return lax.ppermute(x, "frame", [(i, (i + shift) % n_frame) for i in range(n_frame)])

    def along_head(x, shift):
        return lax.ppermute(x, "head", [(i, (i + shift) % n_head) for i in range(n_head)])

    def along_rep(x, shift):
        return lax.ppermute(x, "rep", [(i, (i + shift) % n_rep) for i in range(n_rep)])

    def exchange(x, axes):
        return lax.all_to_all(x, axes, 0, 0, tiled=True)

    across = [along_head(out_weight, dh) for dh in range(1, n_head)]

    slots = pl.pallas_call(
        functools.partial(query_kernel, n_frame),
        out_shape=[jax.ShapeDtypeStruct((block_rows, width), half)] * n_frame,
        in_specs=[HBM] * 4,
        out_specs=[VMEM] * n_frame,
        scratch_shapes=[
            pltpu.SMEM(block_worker.shape, jnp.int32),
            pltpu.VMEM(latents.shape, half),
            pltpu.VMEM(modulation.shape, jnp.float32),
            pltpu.VMEM(query_weight.shape, half),
            pltpu.VMEM(latents.shape, half),
            pltpu.VMEM((tokens, width), half),
            pltpu.SemaphoreType.DMA((3 + n_local,)),
        ],
        compiler_params=params(60),
        cost_estimate=cost(2 * tokens * model * width, 2 * tokens * model + 2 * model * width),
        name="queries",
    )(block_worker, latents, modulation, query_weight)
    arrived = [along_frame(slots[s], s) for s in range(1, n_frame)]

    keys, values_t, masks = pl.pallas_call(
        functools.partial(key_value_kernel, n_frame, n_place),
        out_shape=[
            jax.ShapeDtypeStruct((tokens, width), half),
            jax.ShapeDtypeStruct((width, tokens), half),
            jax.ShapeDtypeStruct((n_place * n_frame, HD), jnp.float32),
        ],
        in_specs=[HBM] * 7,
        out_specs=[VMEM] * 3,
        scratch_shapes=[
            pltpu.SMEM(block_worker.shape, jnp.int32),
            pltpu.VMEM(latents.shape, half),
            pltpu.VMEM(modulation.shape, jnp.float32),
            pltpu.VMEM(key_weight.shape, half),
            pltpu.VMEM(value_weight.shape, half),
            pltpu.VMEM(value_cache.shape, half),
            pltpu.VMEM(latents.shape, half),
            pltpu.VMEM((tokens, width), half),
            pltpu.SemaphoreType.DMA((7,)),
        ],
        compiler_params=params(53),
        cost_estimate=cost(4 * tokens * model * width, 2 * tokens * model + 4 * model * width),
        name="keys_values",
    )(block_worker, latents, modulation, key_weight, value_weight, key_cache, value_cache)

    copies = pl.pallas_call(
        collect_kernel,
        out_shape=jax.ShapeDtypeStruct((n_frame, block_rows, width), half),
        in_specs=[VMEM] * n_frame + [ANY],
        out_specs=VMEM,
        compiler_params=params(16),
        cost_estimate=cost(n_frame * block_rows * width, 4 * n_frame * block_rows * width),
        name="collect",
    )(slots[0], *arrived, masks)
    queries = exchange(copies, "frame")
    partial = pl.pallas_call(
        attend_kernel,
        out_shape=jax.ShapeDtypeStruct((n_frame, width + tail, block_rows), half),
        in_specs=[VMEM] * 3,
        out_specs=VMEM,
        compiler_params=params(16),
        cost_estimate=cost(
            4 * tokens * block_rows * width * n_frame,
            4 * tokens * width,
            tokens * block_rows * width // HD * n_frame,
        ),
        name="attend",
    )(queries, keys, values_t)
    gathered = exchange(partial, "frame")
    copies, *across = pl.pallas_call(
        combine_kernel,
        out_shape=[jax.ShapeDtypeStruct((n_frame, block_rows, width), half)]
        + [jax.ShapeDtypeStruct(w.shape, w.dtype) for w in across],
        in_specs=[VMEM] + [ANY] * len(across),
        out_specs=[VMEM] + [ANY] * len(across),
        input_output_aliases={1 + h: 1 + h for h in range(len(across))},
        compiler_params=params(16),
        cost_estimate=cost(4 * n_frame * block_rows * width, 2 * n_frame * block_rows * width),
        name="combine",
    )(gathered, *across)
    attended = exchange(copies, "frame")
    pieces = pl.pallas_call(
        functools.partial(select_kernel, n_place),
        out_shape=jax.ShapeDtypeStruct((n_place, own_rows, width), half),
        in_specs=[VMEM] * 2,
        out_specs=VMEM,
        compiler_params=params(16),
        cost_estimate=cost(0, 4 * n_frame * block_rows * width),
        name="select",
    )(attended, masks)
    pieces = exchange(pieces, ("head", "rep"))

    weights = []
    for held in [out_weight] + across:
        weights += [held] + [along_rep(held, dr) for dr in range(1, n_rep)]
    return pl.pallas_call(
        functools.partial(project_kernel, n_head, n_rep),
        out_shape=jax.ShapeDtypeStruct((own_rows, model), jnp.float32),
        in_specs=[VMEM] * (2 + n_place),
        out_specs=VMEM,
        compiler_params=params(16),
        cost_estimate=cost(2 * own_rows * model * width * n_place, 2 * model * width * n_place),
        name="project",
    )(modulation, pieces, *weights)


def solution(mesh):
    in_specs = (
        P(("groups", "frame"), None),
        P("groups", None),
        P(("groups", "frame"), ("head", "rep")),
        P(("groups", "frame"), ("head", "rep")),
        P(("groups", "frame")),
        P(None, ("head", "rep")),
        P(None, ("head", "rep")),
        P(None, ("head", "rep")),
        P(("head", "rep"), None),
    )
    out_specs = P(("groups", "frame", "head", "rep"), None)
    body = functools.partial(
        per_device, mesh.shape["frame"], mesh.shape["head"], mesh.shape["rep"]
    )
    return jax.shard_map(body, mesh=mesh, in_specs=in_specs, out_specs=out_specs, check_vma=False)
```

```python
import functools

import jax
import jax.numpy as jnp
from jax import lax
from jax.experimental import pallas as pl
from jax.experimental.pallas import tpu as pltpu
from jax.sharding import PartitionSpec as P

HD = 128
EPS = 1e-06
CHUNK = 16
COLUMNS = 512
TAIL = 16
MIB = 1 << 20

VMEM = pl.BlockSpec(memory_space=pltpu.VMEM)
HBM = pl.BlockSpec(memory_space=pltpu.HBM)
ANY = pl.BlockSpec(memory_space=pl.ANY)


def normalize_block(latents_ref, modulation_ref, normed_ref, start, block_rows):
    def one_chunk(c, carry):
        at = pl.multiple_of(start + c * CHUNK, CHUNK)
        floats = latents_ref[pl.ds(at, CHUNK), :].astype(jnp.float32)
        center = floats - jnp.mean(floats, axis=-1, keepdims=True)
        spread = jnp.mean(center * center, axis=-1, keepdims=True)
        normed_ref[pl.ds(at, CHUNK), :] = (
            center * lax.rsqrt(spread + EPS) * (1.0 + modulation_ref[1:2, :])
            + modulation_ref[0:1, :]
        ).astype(jnp.bfloat16)
        return carry

    lax.fori_loop(0, block_rows // CHUNK, one_chunk, 0, unroll=4)


def query_kernel(n_frame, worker_in, latents_in, modulation_in, weight_in, *rest):
    outs = rest[:n_frame]
    worker_ref, latents_ref, modulation_ref, weight_ref, normed_ref, queries_ref, sems = rest[
        n_frame:
    ]
    n_local = worker_ref.shape[0]
    block_rows = latents_ref.shape[0] // n_local
    frame = lax.axis_index("frame")
    blocks = [slice(j * block_rows, (j + 1) * block_rows) for j in range(n_local)]
    first = [
        pltpu.make_async_copy(worker_in, worker_ref, sems.at[0]),
        pltpu.make_async_copy(modulation_in, modulation_ref, sems.at[1]),
    ]
    each = [
        pltpu.make_async_copy(latents_in.at[rows, :], latents_ref.at[rows, :], sems.at[3 + j])
        for j, rows in enumerate(blocks)
    ]
    weight = pltpu.make_async_copy(weight_in, weight_ref, sems.at[2])
    for copy in first + each + [weight]:
        copy.start()
    for s in range(n_frame):
        outs[s][...] = jnp.zeros_like(outs[s])
    for copy in first:
        copy.wait()
    for j in range(n_local):
        each[j].wait()

        @pl.when(worker_ref[j] >= 0)
        def _():
            normalize_block(latents_ref, modulation_ref, normed_ref, j * block_rows, block_rows)

    weight.wait()
    queries_ref[...] = (
        jnp.dot(normed_ref[...], weight_ref[...], preferred_element_type=jnp.float32) * HD ** (-0.5)
    ).astype(jnp.bfloat16)
    for j in range(n_local):
        worker = worker_ref[j]
        for s in range(n_frame):

            @pl.when((worker >= 0) & (jnp.bitwise_xor(frame, s) == worker))
            def _():
                outs[s][...] = queries_ref[blocks[j], :]


def key_value_kernel(
    n_frame,
    n_head,
    n_rep,
    worker_in,
    latents_in,
    modulation_in,
    key_weight_in,
    value_weight_in,
    key_cache_in,
    value_cache_in,
    keys_ref,
    values_t_ref,
    masks_ref,
    worker_ref,
    latents_ref,
    modulation_ref,
    key_weight_ref,
    value_weight_ref,
    value_cache_ref,
    normed_ref,
    fresh_ref,
    sems,
):
    n_local = worker_ref.shape[0]
    tokens = latents_ref.shape[0]
    block_rows = tokens // n_local
    blocks = [slice(j * block_rows, (j + 1) * block_rows) for j in range(n_local)]
    first = [
        pltpu.make_async_copy(worker_in, worker_ref, sems.at[0]),
        pltpu.make_async_copy(modulation_in, modulation_ref, sems.at[1]),
        pltpu.make_async_copy(latents_in, latents_ref, sems.at[2]),
    ]
    second = [
        pltpu.make_async_copy(key_weight_in, key_weight_ref, sems.at[3]),
        pltpu.make_async_copy(value_weight_in, value_weight_ref, sems.at[4]),
        pltpu.make_async_copy(key_cache_in, keys_ref, sems.at[5]),
        pltpu.make_async_copy(value_cache_in, value_cache_ref, sems.at[6]),
    ]
    for copy in first + second:
        copy.start()
    for copy in first:
        copy.wait()
    frame, head, rep = lax.axis_index("frame"), lax.axis_index("head"), lax.axis_index("rep")
    n_place = n_head * n_rep
    for d in range(n_place):
        target = lax.rem(head + d // n_rep, n_head) * n_rep + lax.rem(rep + d % n_rep, n_rep)
        worker = worker_ref[target * (tokens // n_place) // block_rows]
        for s in range(n_frame):
            held = (worker >= 0) & (jnp.bitwise_xor(frame, s) == worker)
            masks_ref[d * n_frame + s : d * n_frame + s + 1, :] = jnp.full(
                (1, masks_ref.shape[1]), jnp.where(held, 1.0, 0.0), jnp.float32
            )
    for j in range(n_local):

        @pl.when(worker_ref[j] >= 0)
        def _():
            normalize_block(latents_ref, modulation_ref, normed_ref, j * block_rows, block_rows)

    for copy in second:
        copy.wait()
    fresh_ref[...] = jnp.dot(
        normed_ref[...], key_weight_ref[...], preferred_element_type=jnp.float32
    ).astype(jnp.bfloat16)
    for j in range(n_local):

        @pl.when(worker_ref[j] >= 0)
        def _():
            keys_ref[blocks[j], :] = fresh_ref[blocks[j], :]

    fresh_ref[...] = jnp.dot(
        normed_ref[...], value_weight_ref[...], preferred_element_type=jnp.float32
    ).astype(jnp.bfloat16)
    for j in range(n_local):

        @pl.when(worker_ref[j] >= 0)
        def _():
            value_cache_ref[blocks[j], :] = fresh_ref[blocks[j], :]

    for h in range(keys_ref.shape[1] // HD):
        cols = slice(h * HD, (h + 1) * HD)
        values_t_ref[cols, :] = value_cache_ref[:, cols].T


def three_terms(x):
    first = x.astype(jnp.bfloat16).astype(jnp.float32)
    rest = x - first
    second = rest.astype(jnp.bfloat16).astype(jnp.float32)
    return [first, second, rest - second]


def collect_kernel(*refs):
    *parts, _, out_ref = refs
    out_ref[...] = sum(part[...].astype(jnp.float32) for part in parts).astype(jnp.bfloat16)


def attend_kernel(queries_ref, keys_ref, values_t_ref, *refs):
    out_ref = refs[len(refs) // 2]
    width = keys_ref.shape[1]
    stats = []
    for h in range(width // HD):
        cols = slice(h * HD, (h + 1) * HD)
        scores = lax.dot_general(
            keys_ref[:, cols],
            queries_ref[:, cols],
            (((1,), (1,)), ((), ())),
            preferred_element_type=jnp.float32,
        )
        highest = jnp.max(scores, axis=0, keepdims=True)
        weights = jnp.exp(scores - highest)
        total = jnp.sum(weights, axis=0, keepdims=True)
        out_ref[cols, :] = jnp.dot(
            values_t_ref[cols, :], weights.astype(jnp.bfloat16), preferred_element_type=jnp.float32
        ).astype(jnp.bfloat16)
        stats += three_terms(highest) + three_terms(total)
    shape = (out_ref.shape[0] - width, out_ref.shape[1])
    row = lax.broadcasted_iota(jnp.int32, shape, 0)
    tail = jnp.zeros(shape, jnp.float32)
    for i, stat in enumerate(stats):
        tail = jnp.where(row == i, stat, tail)
    out_ref[width:, :] = tail.astype(jnp.bfloat16)


def combine_kernel(*refs):
    parts, out_ref = refs[:-1], refs[-1]
    width = out_ref.shape[1]
    tails = [part[width:, :].astype(jnp.float32) for part in parts]
    for h in range(width // HD):
        cols = slice(h * HD, (h + 1) * HD)

        def stat(tail, at):
            at += 6 * h
            return tail[at : at + 1, :] + tail[at + 1 : at + 2, :] + tail[at + 2 : at + 3, :]

        maxima = [stat(tail, 0) for tail in tails]
        highest = functools.reduce(jnp.maximum, maxima)
        factors = [jnp.exp(m - highest) for m in maxima]
        total = sum(stat(tail, 3) * factor for tail, factor in zip(tails, factors))
        summed = sum(
            part[cols, :].astype(jnp.float32) * factor for part, factor in zip(parts, factors)
        )
        out_ref[:, cols] = (summed / total).T.astype(jnp.bfloat16)


def select_kernel(n_frame, n_head, n_rep, *refs):
    slots, masks_ref = refs[:n_frame], refs[n_frame]
    first = len(refs) - (len(refs) - n_frame - 1 - n_head * n_rep) // 2 - n_head * n_rep
    outs = refs[first : first + n_head * n_rep]
    block_rows, width = slots[0].shape
    rows = outs[0].shape[0]
    head, rep = lax.axis_index("head"), lax.axis_index("rep")
    for d in range(n_head * n_rep):
        if rows == block_rows:
            some = slice(None)
        else:
            target = lax.rem(head + d // n_rep, n_head) * n_rep + lax.rem(rep + d % n_rep, n_rep)
            some = pl.ds(pl.multiple_of(lax.rem(target * rows, block_rows), rows), rows)
        for h in range(width // HD):
            cols = slice(h * HD, (h + 1) * HD)
            chosen = jnp.zeros((rows, HD), jnp.float32)
            for s in range(n_frame):
                mask = masks_ref[d * n_frame + s : d * n_frame + s + 1, :]
                chosen = jnp.where(mask > 0.5, slots[s][some, cols].astype(jnp.float32), chosen)
            outs[d][:, cols] = chosen.astype(jnp.bfloat16)


def project_kernel(modulation_ref, *refs):
    refs, out_ref = refs[:-1], refs[-1]
    parts, weights = refs[: len(refs) // 2], refs[len(refs) // 2 :]
    width = out_ref.shape[1]
    for start in range(0, width, COLUMNS):
        cols = slice(start, start + COLUMNS)
        total = sum(
            jnp.dot(part[...], weight[:, cols], preferred_element_type=jnp.float32)
            for part, weight in zip(parts, weights)
        )
        out_ref[:, cols] = total * modulation_ref[2:3, cols]


def params(mib):
    return pltpu.CompilerParams(vmem_limit_bytes=mib * MIB)


def cost(flops, moved, exps=0):
    return pl.CostEstimate(flops=flops, bytes_accessed=moved, transcendentals=exps)


def per_device(
    n_frame,
    n_head,
    n_rep,
    latents,
    modulation,
    key_cache,
    value_cache,
    block_worker,
    query_weight,
    key_weight,
    value_weight,
    out_weight,
):
    tokens, model = latents.shape
    n_local = block_worker.shape[0]
    block_rows = tokens // n_local
    width = query_weight.shape[1]
    n_place = n_head * n_rep
    own_rows = tokens // n_place
    tail = TAIL * -(-6 * (width // HD) // TAIL)
    half = jnp.bfloat16

    def along_frame(x, s):
        return lax.ppermute(x, "frame", [(i, i ^ s) for i in range(n_frame)])

    def along_head(x, shift):
        return lax.ppermute(x, "head", [(i, (i + shift) % n_head) for i in range(n_head)])

    def along_rep(x, shift):
        return lax.ppermute(x, "rep", [(i, (i + shift) % n_rep) for i in range(n_rep)])

    def in_frame(x, d):
        pairs = []
        for h in range(n_head):
            for r in range(n_rep):
                to = ((h + d // n_rep) % n_head) * n_rep + (r + d % n_rep) % n_rep
                pairs.append((h * n_rep + r, to))
        return lax.ppermute(x, ("head", "rep"), pairs)

    across = [along_head(out_weight, dh) for dh in range(1, n_head)]

    slots = pl.pallas_call(
        functools.partial(query_kernel, n_frame),
        out_shape=[jax.ShapeDtypeStruct((block_rows, width), half)] * n_frame,
        in_specs=[HBM] * 4,
        out_specs=[VMEM] * n_frame,
        scratch_shapes=[
            pltpu.SMEM(block_worker.shape, jnp.int32),
            pltpu.VMEM(latents.shape, half),
            pltpu.VMEM(modulation.shape, jnp.float32),
            pltpu.VMEM(query_weight.shape, half),
            pltpu.VMEM(latents.shape, half),
            pltpu.VMEM((tokens, width), half),
            pltpu.SemaphoreType.DMA((3 + n_local,)),
        ],
        compiler_params=params(60),
        cost_estimate=cost(2 * tokens * model * width, 2 * tokens * model + 2 * model * width),
        name="queries",
    )(block_worker, latents, modulation, query_weight)
    arrived = [along_frame(slots[s], s) for s in range(1, n_frame)]

    keys, values_t, masks = pl.pallas_call(
        functools.partial(key_value_kernel, n_frame, n_head, n_rep),
        out_shape=[
            jax.ShapeDtypeStruct((tokens, width), half),
            jax.ShapeDtypeStruct((width, tokens), half),
            jax.ShapeDtypeStruct((n_place * n_frame, HD), jnp.float32),
        ],
        in_specs=[HBM] * 7,
        out_specs=[VMEM] * 3,
        scratch_shapes=[
            pltpu.SMEM(block_worker.shape, jnp.int32),
            pltpu.VMEM(latents.shape, half),
            pltpu.VMEM(modulation.shape, jnp.float32),
            pltpu.VMEM(key_weight.shape, half),
            pltpu.VMEM(value_weight.shape, half),
            pltpu.VMEM(value_cache.shape, half),
            pltpu.VMEM(latents.shape, half),
            pltpu.VMEM((tokens, width), half),
            pltpu.SemaphoreType.DMA((7,)),
        ],
        compiler_params=params(53),
        cost_estimate=cost(4 * tokens * model * width, 2 * tokens * model + 4 * model * width),
        name="keys_values",
    )(block_worker, latents, modulation, key_weight, value_weight, key_cache, value_cache)

    mine = pl.pallas_call(
        collect_kernel,
        out_shape=jax.ShapeDtypeStruct((block_rows, width), half),
        in_specs=[VMEM] * n_frame + [ANY],
        out_specs=VMEM,
        compiler_params=params(16),
        cost_estimate=cost(n_frame * block_rows * width, 2 * n_frame * block_rows * width),
        name="collect",
    )(slots[0], *arrived, masks)

    def attend(queries, through=()):
        return pl.pallas_call(
            attend_kernel,
            out_shape=[jax.ShapeDtypeStruct((width + tail, block_rows), half)]
            + [jax.ShapeDtypeStruct(w.shape, w.dtype) for w in through],
            in_specs=[VMEM] * 3 + [ANY] * len(through),
            out_specs=[VMEM] + [ANY] * len(through),
            input_output_aliases={3 + i: 1 + i for i in range(len(through))},
            compiler_params=params(16),
            cost_estimate=cost(
                4 * tokens * block_rows * width,
                20 * tokens * width,
                tokens * block_rows * width // HD,
            ),
            name="attend",
        )(queries, keys, values_t, *through)

    shared = [along_frame(mine, s) for s in range(1, n_frame)]
    sent = [along_frame(attend(queries)[0], s) for s, queries in enumerate(shared, 1)]
    (own,) = attend(mine)
    attended = pl.pallas_call(
        combine_kernel,
        out_shape=jax.ShapeDtypeStruct((block_rows, width), half),
        in_specs=[VMEM] * n_frame,
        out_specs=VMEM,
        compiler_params=params(16),
        cost_estimate=cost(4 * n_frame * block_rows * width, 2 * n_frame * block_rows * width),
        name="combine",
    )(own, *sent)
    copies = [attended] + [along_frame(attended, s) for s in range(1, n_frame)]
    pieces = pl.pallas_call(
        functools.partial(select_kernel, n_frame, n_head, n_rep),
        out_shape=[jax.ShapeDtypeStruct((own_rows, width), half)] * n_place
        + [jax.ShapeDtypeStruct(w.shape, w.dtype) for w in across],
        in_specs=[VMEM] * (n_frame + 1) + [ANY] * len(across),
        out_specs=[VMEM] * n_place + [ANY] * len(across),
        input_output_aliases={n_frame + 1 + i: n_place + i for i in range(len(across))},
        compiler_params=params(16),
        cost_estimate=cost(0, 4 * n_frame * block_rows * width),
        name="select",
    )(*copies, masks, *across)
    pieces, across = pieces[:n_place], list(pieces[n_place:])
    pieces = [pieces[0]] + [in_frame(pieces[d], d) for d in range(1, n_place)]

    weights = []
    for held in [out_weight] + across:
        weights += [held] + [along_rep(held, dr) for dr in range(1, n_rep)]
    return pl.pallas_call(
        project_kernel,
        out_shape=jax.ShapeDtypeStruct((own_rows, model), jnp.float32),
        in_specs=[VMEM] * (1 + 2 * n_place),
        out_specs=VMEM,
        compiler_params=params(16),
        cost_estimate=cost(2 * own_rows * model * width * n_place, 2 * model * width * n_place),
        name="project",
    )(modulation, *pieces, *weights)


def solution(mesh):
    in_specs = (
        P(("groups", "frame"), None),
        P("groups", None),
        P(("groups", "frame"), ("head", "rep")),
        P(("groups", "frame"), ("head", "rep")),
        P(("groups", "frame")),
        P(None, ("head", "rep")),
        P(None, ("head", "rep")),
        P(None, ("head", "rep")),
        P(("head", "rep"), None),
    )
    out_specs = P(("groups", "frame", "head", "rep"), None)
    body = functools.partial(
        per_device, mesh.shape["frame"], mesh.shape["head"], mesh.shape["rep"]
    )
    return jax.shard_map(body, mesh=mesh, in_specs=in_specs, out_specs=out_specs, check_vma=False)
```

```python
import functools

import jax
import jax.numpy as jnp
from jax import lax
from jax.experimental import pallas as pl
from jax.experimental.pallas import tpu as pltpu
from jax.sharding import PartitionSpec as P

HD = 128
EPS = 1e-06
CHUNK = 16
COLUMNS = 512
TAIL = 16
MIB = 1 << 20

VMEM = pl.BlockSpec(memory_space=pltpu.VMEM)
HBM = pl.BlockSpec(memory_space=pltpu.HBM)
ANY = pl.BlockSpec(memory_space=pl.ANY)


def normalize_block(latents_ref, modulation_ref, normed_ref, start, block_rows):
    def one_chunk(c, carry):
        at = pl.multiple_of(start + c * CHUNK, CHUNK)
        floats = latents_ref[pl.ds(at, CHUNK), :].astype(jnp.float32)
        center = floats - jnp.mean(floats, axis=-1, keepdims=True)
        spread = jnp.mean(center * center, axis=-1, keepdims=True)
        normed_ref[pl.ds(at, CHUNK), :] = (
            center * lax.rsqrt(spread + EPS) * (1.0 + modulation_ref[1:2, :])
            + modulation_ref[0:1, :]
        ).astype(jnp.bfloat16)
        return carry

    lax.fori_loop(0, block_rows // CHUNK, one_chunk, 0, unroll=4)


def query_kernel(n_frame, worker_in, latents_in, modulation_in, weight_in, *rest):
    outs, normed_out = rest[:n_frame], rest[n_frame]
    worker_ref, latents_ref, modulation_ref, weight_ref, normed_ref, queries_ref, sems = rest[
        n_frame + 1 :
    ]
    n_local = worker_ref.shape[0]
    block_rows = latents_ref.shape[0] // n_local
    frame = lax.axis_index("frame")
    blocks = [slice(j * block_rows, (j + 1) * block_rows) for j in range(n_local)]
    first = [
        pltpu.make_async_copy(worker_in, worker_ref, sems.at[0]),
        pltpu.make_async_copy(modulation_in, modulation_ref, sems.at[1]),
    ]
    each = [
        pltpu.make_async_copy(latents_in.at[rows, :], latents_ref.at[rows, :], sems.at[3 + j])
        for j, rows in enumerate(blocks)
    ]
    back = [
        pltpu.make_async_copy(
            normed_ref.at[rows, :], normed_out.at[rows, :], sems.at[3 + n_local + j]
        )
        for j, rows in enumerate(blocks)
    ]
    weight = pltpu.make_async_copy(weight_in, weight_ref, sems.at[2])
    for copy in first + each + [weight]:
        copy.start()
    for s in range(n_frame):
        outs[s][...] = jnp.zeros_like(outs[s])
    for copy in first:
        copy.wait()
    for j in range(n_local):
        each[j].wait()

        @pl.when(worker_ref[j] >= 0)
        def _():
            normalize_block(latents_ref, modulation_ref, normed_ref, j * block_rows, block_rows)
            back[j].start()

    weight.wait()
    queries_ref[...] = (
        jnp.dot(normed_ref[...], weight_ref[...], preferred_element_type=jnp.float32) * HD ** (-0.5)
    ).astype(jnp.bfloat16)
    for j in range(n_local):
        worker = worker_ref[j]
        for s in range(n_frame):

            @pl.when((worker >= 0) & (jnp.bitwise_xor(frame, s) == worker))
            def _():
                outs[s][...] = queries_ref[blocks[j], :]

        @pl.when(worker >= 0)
        def _():
            back[j].wait()


def key_kernel(
    worker_in, normed_in, weight_in, cache_in, keys_ref, worker_ref, normed_ref, weight_ref, sems
):
    n_local = worker_ref.shape[0]
    block_rows = normed_ref.shape[0] // n_local
    copies = [
        pltpu.make_async_copy(source, target, sems.at[i])
        for i, (source, target) in enumerate(
            [
                (worker_in, worker_ref),
                (normed_in, normed_ref),
                (weight_in, weight_ref),
                (cache_in, keys_ref),
            ]
        )
    ]
    for copy in copies:
        copy.start()
    for copy in copies:
        copy.wait()
    fresh = jnp.dot(
        normed_ref[...], weight_ref[...], preferred_element_type=jnp.float32
    ).astype(jnp.bfloat16)
    for j in range(n_local):
        rows = slice(j * block_rows, (j + 1) * block_rows)

        @pl.when(worker_ref[j] >= 0)
        def _():
            keys_ref[rows, :] = fresh[rows, :]


def value_kernel(
    n_frame,
    n_head,
    n_rep,
    worker_in,
    normed_in,
    weight_in,
    cache_in,
    _,
    values_t_ref,
    masks_ref,
    worker_ref,
    normed_ref,
    weight_ref,
    values_ref,
    sems,
):
    n_local = worker_ref.shape[0]
    tokens = normed_ref.shape[0]
    block_rows = tokens // n_local
    copies = [
        pltpu.make_async_copy(source, target, sems.at[i])
        for i, (source, target) in enumerate(
            [
                (worker_in, worker_ref),
                (normed_in, normed_ref),
                (weight_in, weight_ref),
                (cache_in, values_ref),
            ]
        )
    ]
    for copy in copies:
        copy.start()
    copies[0].wait()
    frame, head, rep = lax.axis_index("frame"), lax.axis_index("head"), lax.axis_index("rep")
    n_place = n_head * n_rep
    for d in range(n_place):
        target = lax.rem(head + d // n_rep, n_head) * n_rep + lax.rem(rep + d % n_rep, n_rep)
        worker = worker_ref[target * (tokens // n_place) // block_rows]
        for s in range(n_frame):
            held = (worker >= 0) & (jnp.bitwise_xor(frame, s) == worker)
            masks_ref[d * n_frame + s : d * n_frame + s + 1, :] = jnp.full(
                (1, masks_ref.shape[1]), jnp.where(held, 1.0, 0.0), jnp.float32
            )
    for copy in copies[1:]:
        copy.wait()
    fresh = jnp.dot(
        normed_ref[...], weight_ref[...], preferred_element_type=jnp.float32
    ).astype(jnp.bfloat16)
    for j in range(n_local):
        rows = slice(j * block_rows, (j + 1) * block_rows)

        @pl.when(worker_ref[j] >= 0)
        def _():
            values_ref[rows, :] = fresh[rows, :]

    for h in range(values_ref.shape[1] // HD):
        cols = slice(h * HD, (h + 1) * HD)
        values_t_ref[cols, :] = values_ref[:, cols].T


def three_terms(x):
    first = x.astype(jnp.bfloat16).astype(jnp.float32)
    rest = x - first
    second = rest.astype(jnp.bfloat16).astype(jnp.float32)
    return [first, second, rest - second]


def collect_kernel(*refs):
    *parts, _, out_ref = refs
    out_ref[...] = sum(part[...].astype(jnp.float32) for part in parts).astype(jnp.bfloat16)


def attend_kernel(queries_ref, keys_ref, values_t_ref, *refs):
    out_ref = refs[len(refs) // 2]
    width = keys_ref.shape[1]
    stats = []
    for h in range(width // HD):
        cols = slice(h * HD, (h + 1) * HD)
        scores = lax.dot_general(
            keys_ref[:, cols],
            queries_ref[:, cols],
            (((1,), (1,)), ((), ())),
            preferred_element_type=jnp.float32,
        )
        highest = jnp.max(scores, axis=0, keepdims=True)
        weights = jnp.exp(scores - highest)
        total = jnp.sum(weights, axis=0, keepdims=True)
        out_ref[cols, :] = jnp.dot(
            values_t_ref[cols, :], weights.astype(jnp.bfloat16), preferred_element_type=jnp.float32
        ).astype(jnp.bfloat16)
        stats += three_terms(highest) + three_terms(total)
    shape = (out_ref.shape[0] - width, out_ref.shape[1])
    row = lax.broadcasted_iota(jnp.int32, shape, 0)
    tail = jnp.zeros(shape, jnp.float32)
    for i, stat in enumerate(stats):
        tail = jnp.where(row == i, stat, tail)
    out_ref[width:, :] = tail.astype(jnp.bfloat16)


def combine_kernel(*refs):
    parts, out_ref = refs[:-1], refs[-1]
    width = out_ref.shape[1]
    tails = [part[width:, :].astype(jnp.float32) for part in parts]
    for h in range(width // HD):
        cols = slice(h * HD, (h + 1) * HD)

        def stat(tail, at):
            at += 6 * h
            return tail[at : at + 1, :] + tail[at + 1 : at + 2, :] + tail[at + 2 : at + 3, :]

        maxima = [stat(tail, 0) for tail in tails]
        highest = functools.reduce(jnp.maximum, maxima)
        factors = [jnp.exp(m - highest) for m in maxima]
        total = sum(stat(tail, 3) * factor for tail, factor in zip(tails, factors))
        summed = sum(
            part[cols, :].astype(jnp.float32) * factor for part, factor in zip(parts, factors)
        )
        out_ref[:, cols] = (summed / total).T.astype(jnp.bfloat16)


def select_kernel(n_frame, n_head, n_rep, *refs):
    slots, masks_ref = refs[:n_frame], refs[n_frame]
    first = len(refs) - (len(refs) - n_frame - 1 - n_head * n_rep) // 2 - n_head * n_rep
    outs = refs[first : first + n_head * n_rep]
    block_rows, width = slots[0].shape
    rows = outs[0].shape[0]
    head, rep = lax.axis_index("head"), lax.axis_index("rep")
    for d in range(n_head * n_rep):
        if rows == block_rows:
            some = slice(None)
        else:
            target = lax.rem(head + d // n_rep, n_head) * n_rep + lax.rem(rep + d % n_rep, n_rep)
            some = pl.ds(pl.multiple_of(lax.rem(target * rows, block_rows), rows), rows)
        for h in range(width // HD):
            cols = slice(h * HD, (h + 1) * HD)
            chosen = jnp.zeros((rows, HD), jnp.float32)
            for s in range(n_frame):
                mask = masks_ref[d * n_frame + s : d * n_frame + s + 1, :]
                chosen = jnp.where(mask > 0.5, slots[s][some, cols].astype(jnp.float32), chosen)
            outs[d][:, cols] = chosen.astype(jnp.bfloat16)


def project_near_kernel(*refs):
    refs, out_ref = refs[:-1], refs[-1]
    parts, weights = refs[: len(refs) // 2], refs[len(refs) // 2 :]
    for start in range(0, out_ref.shape[1], COLUMNS):
        cols = slice(start, start + COLUMNS)
        out_ref[:, cols] = sum(
            jnp.dot(part[...], weight[:, cols], preferred_element_type=jnp.float32)
            for part, weight in zip(parts, weights)
        )


def project_kernel(modulation_ref, near_ref, *refs):
    refs, out_ref = refs[:-1], refs[-1]
    parts, weights = refs[: len(refs) // 2], refs[len(refs) // 2 :]
    for start in range(0, out_ref.shape[1], COLUMNS):
        cols = slice(start, start + COLUMNS)
        total = near_ref[:, cols] + sum(
            jnp.dot(part[...], weight[:, cols], preferred_element_type=jnp.float32)
            for part, weight in zip(parts, weights)
        )
        out_ref[:, cols] = total * modulation_ref[2:3, cols]


def params(mib):
    return pltpu.CompilerParams(vmem_limit_bytes=mib * MIB)


def cost(flops, moved, exps=0):
    return pl.CostEstimate(flops=flops, bytes_accessed=moved, transcendentals=exps)


def per_device(
    n_frame,
    n_head,
    n_rep,
    latents,
    modulation,
    key_cache,
    value_cache,
    block_worker,
    query_weight,
    key_weight,
    value_weight,
    out_weight,
):
    tokens, model = latents.shape
    n_local = block_worker.shape[0]
    block_rows = tokens // n_local
    width = query_weight.shape[1]
    n_place = n_head * n_rep
    own_rows = tokens // n_place
    tail = TAIL * -(-6 * (width // HD) // TAIL)
    half = jnp.bfloat16

    def along_frame(x, s):
        return lax.ppermute(x, "frame", [(i, i ^ s) for i in range(n_frame)])

    def along_head(x, shift):
        return lax.ppermute(x, "head", [(i, (i + shift) % n_head) for i in range(n_head)])

    def along_rep(x, shift):
        return lax.ppermute(x, "rep", [(i, (i + shift) % n_rep) for i in range(n_rep)])

    def in_frame(x, d):
        pairs = []
        for h in range(n_head):
            for r in range(n_rep):
                to = ((h + d // n_rep) % n_head) * n_rep + (r + d % n_rep) % n_rep
                pairs.append((h * n_rep + r, to))
        return lax.ppermute(x, ("head", "rep"), pairs)

    across = [along_head(out_weight, dh) for dh in range(1, n_head)]

    *slots, normed = pl.pallas_call(
        functools.partial(query_kernel, n_frame),
        out_shape=[jax.ShapeDtypeStruct((block_rows, width), half)] * n_frame
        + [jax.ShapeDtypeStruct(latents.shape, half)],
        in_specs=[HBM] * 4,
        out_specs=[VMEM] * n_frame + [HBM],
        scratch_shapes=[
            pltpu.SMEM(block_worker.shape, jnp.int32),
            pltpu.VMEM(latents.shape, half),
            pltpu.VMEM(modulation.shape, jnp.float32),
            pltpu.VMEM(query_weight.shape, half),
            pltpu.VMEM(latents.shape, half),
            pltpu.VMEM((tokens, width), half),
            pltpu.SemaphoreType.DMA((3 + 2 * n_local,)),
        ],
        compiler_params=params(60),
        cost_estimate=cost(2 * tokens * model * width, 2 * tokens * model + 2 * model * width),
        name="queries",
    )(block_worker, latents, modulation, query_weight)
    arrived = [along_frame(slots[s], s) for s in range(n_frame - 1, 0, -1)]

    keys = pl.pallas_call(
        key_kernel,
        out_shape=jax.ShapeDtypeStruct((tokens, width), half),
        in_specs=[HBM] * 4,
        out_specs=VMEM,
        scratch_shapes=[
            pltpu.SMEM(block_worker.shape, jnp.int32),
            pltpu.VMEM(latents.shape, half),
            pltpu.VMEM(key_weight.shape, half),
            pltpu.SemaphoreType.DMA((4,)),
        ],
        compiler_params=params(53),
        cost_estimate=cost(2 * tokens * model * width, 6 * tokens * model),
        name="keys",
    )(block_worker, normed, key_weight, key_cache)

    mine = pl.pallas_call(
        collect_kernel,
        out_shape=jax.ShapeDtypeStruct((block_rows, width), half),
        in_specs=[VMEM] * n_frame + [ANY],
        out_specs=VMEM,
        compiler_params=params(16),
        cost_estimate=cost(n_frame * block_rows * width, 2 * n_frame * block_rows * width),
        name="collect",
    )(slots[0], *arrived, keys)

    values_t, masks = pl.pallas_call(
        functools.partial(value_kernel, n_frame, n_head, n_rep),
        out_shape=[
            jax.ShapeDtypeStruct((width, tokens), half),
            jax.ShapeDtypeStruct((n_place * n_frame, HD), jnp.float32),
        ],
        in_specs=[HBM] * 4 + [ANY],
        out_specs=[VMEM] * 2,
        scratch_shapes=[
            pltpu.SMEM(block_worker.shape, jnp.int32),
            pltpu.VMEM(latents.shape, half),
            pltpu.VMEM(value_weight.shape, half),
            pltpu.VMEM(value_cache.shape, half),
            pltpu.SemaphoreType.DMA((4,)),
        ],
        compiler_params=params(53),
        cost_estimate=cost(2 * tokens * model * width, 6 * tokens * model),
        name="values",
    )(block_worker, normed, value_weight, value_cache, mine)

    def attend(queries, through=()):
        return pl.pallas_call(
            attend_kernel,
            out_shape=[jax.ShapeDtypeStruct((width + tail, block_rows), half)]
            + [jax.ShapeDtypeStruct(w.shape, w.dtype) for w in through],
            in_specs=[VMEM] * 3 + [ANY] * len(through),
            out_specs=[VMEM] + [ANY] * len(through),
            input_output_aliases={3 + i: 1 + i for i in range(len(through))},
            compiler_params=params(16),
            cost_estimate=cost(
                4 * tokens * block_rows * width,
                20 * tokens * width,
                tokens * block_rows * width // HD,
            ),
            name="attend",
        )(queries, keys, values_t, *through)

    far_first = range(n_frame - 1, 0, -1)
    shared = {s: along_frame(mine, s) for s in far_first}
    sent = [along_frame(attend(shared[s])[0], s) for s in far_first]
    (own,) = attend(mine)
    attended = pl.pallas_call(
        combine_kernel,
        out_shape=jax.ShapeDtypeStruct((block_rows, width), half),
        in_specs=[VMEM] * n_frame,
        out_specs=VMEM,
        compiler_params=params(16),
        cost_estimate=cost(4 * n_frame * block_rows * width, 2 * n_frame * block_rows * width),
        name="combine",
    )(own, *sent)
    copies = {s: along_frame(attended, s) for s in far_first}
    copies = [attended] + [copies[s] for s in range(1, n_frame)]
    pieces = pl.pallas_call(
        functools.partial(select_kernel, n_frame, n_head, n_rep),
        out_shape=[jax.ShapeDtypeStruct((own_rows, width), half)] * n_place
        + [jax.ShapeDtypeStruct(w.shape, w.dtype) for w in across],
        in_specs=[VMEM] * (n_frame + 1) + [ANY] * len(across),
        out_specs=[VMEM] * n_place + [ANY] * len(across),
        input_output_aliases={n_frame + 1 + i: n_place + i for i in range(len(across))},
        compiler_params=params(16),
        cost_estimate=cost(0, 4 * n_frame * block_rows * width),
        name="select",
    )(*copies, masks, *across)
    pieces, across = pieces[:n_place], list(pieces[n_place:])
    pieces = [pieces[0]] + [in_frame(pieces[d], d) for d in range(1, n_place)]

    weights = []
    for held in [out_weight] + across:
        weights += [held] + [along_rep(held, dr) for dr in range(1, n_rep)]
    near = pl.pallas_call(
        project_near_kernel,
        out_shape=jax.ShapeDtypeStruct((own_rows, model), jnp.float32),
        in_specs=[VMEM] * (2 * n_rep),
        out_specs=VMEM,
        compiler_params=params(16),
        cost_estimate=cost(2 * own_rows * model * width * n_rep, 4 * model * width * n_rep),
        name="project_near",
    )(*pieces[:n_rep], *weights[:n_rep])
    return pl.pallas_call(
        project_kernel,
        out_shape=jax.ShapeDtypeStruct((own_rows, model), jnp.float32),
        in_specs=[VMEM] * (2 + 2 * (n_place - n_rep)),
        out_specs=VMEM,
        compiler_params=params(16),
        cost_estimate=cost(2 * own_rows * model * width * n_rep, 2 * model * width * n_place),
        name="project",
    )(modulation, near, *pieces[n_rep:], *weights[n_rep:])


def solution(mesh):
    in_specs = (
        P(("groups", "frame"), None),
        P("groups", None),
        P(("groups", "frame"), ("head", "rep")),
        P(("groups", "frame"), ("head", "rep")),
        P(("groups", "frame")),
        P(None, ("head", "rep")),
        P(None, ("head", "rep")),
        P(None, ("head", "rep")),
        P(("head", "rep"), None),
    )
    out_specs = P(("groups", "frame", "head", "rep"), None)
    body = functools.partial(
        per_device, mesh.shape["frame"], mesh.shape["head"], mesh.shape["rep"]
    )
    return jax.shard_map(body, mesh=mesh, in_specs=in_specs, out_specs=out_specs, check_vma=False)
```

```python
import functools

import jax
import jax.numpy as jnp
from jax import lax
from jax.experimental import pallas as pl
from jax.experimental.pallas import tpu as pltpu
from jax.sharding import PartitionSpec as P

HD = 128
EPS = 1e-06
CHUNK = 16
COLUMNS = 512
SLOTS = 3
TAIL = 16
MIB = 1 << 20

VMEM = pl.BlockSpec(memory_space=pltpu.VMEM)
HBM = pl.BlockSpec(memory_space=pltpu.HBM)
ANY = pl.BlockSpec(memory_space=pl.ANY)


def normalize_block(latents_ref, modulation_ref, normed_ref, start, block_rows):
    def one_chunk(c, carry):
        at = pl.multiple_of(start + c * CHUNK, CHUNK)
        floats = latents_ref[pl.ds(at, CHUNK), :].astype(jnp.float32)
        center = floats - jnp.mean(floats, axis=-1, keepdims=True)
        spread = jnp.mean(center * center, axis=-1, keepdims=True)
        normed_ref[pl.ds(at, CHUNK), :] = (
            center * lax.rsqrt(spread + EPS) * (1.0 + modulation_ref[1:2, :])
            + modulation_ref[0:1, :]
        ).astype(jnp.bfloat16)
        return carry

    lax.fori_loop(0, block_rows // CHUNK, one_chunk, 0, unroll=4)


def query_kernel(n_frame, worker_in, latents_in, modulation_in, weight_in, *rest):
    outs, normed_out = rest[:n_frame], rest[n_frame]
    worker_ref, latents_ref, modulation_ref, weight_ref, normed_ref, queries_ref, sems = rest[
        n_frame + 1 :
    ]
    n_local = worker_ref.shape[0]
    block_rows = latents_ref.shape[0] // n_local
    frame = lax.axis_index("frame")
    blocks = [slice(j * block_rows, (j + 1) * block_rows) for j in range(n_local)]
    first = [
        pltpu.make_async_copy(worker_in, worker_ref, sems.at[0]),
        pltpu.make_async_copy(modulation_in, modulation_ref, sems.at[1]),
    ]
    each = [
        pltpu.make_async_copy(latents_in.at[rows, :], latents_ref.at[rows, :], sems.at[3 + j])
        for j, rows in enumerate(blocks)
    ]
    back = [
        pltpu.make_async_copy(
            normed_ref.at[rows, :], normed_out.at[rows, :], sems.at[3 + n_local + j]
        )
        for j, rows in enumerate(blocks)
    ]
    weight = pltpu.make_async_copy(weight_in, weight_ref, sems.at[2])
    for copy in first + each + [weight]:
        copy.start()
    for s in range(n_frame):
        outs[s][...] = jnp.zeros_like(outs[s])
    for copy in first:
        copy.wait()
    for j in range(n_local):
        each[j].wait()

        @pl.when(worker_ref[j] >= 0)
        def _():
            normalize_block(latents_ref, modulation_ref, normed_ref, j * block_rows, block_rows)
            back[j].start()

    weight.wait()
    queries_ref[...] = (
        jnp.dot(normed_ref[...], weight_ref[...], preferred_element_type=jnp.float32) * HD ** (-0.5)
    ).astype(jnp.bfloat16)
    for j in range(n_local):
        worker = worker_ref[j]
        for s in range(n_frame):

            @pl.when((worker >= 0) & (jnp.bitwise_xor(frame, s) == worker))
            def _():
                outs[s][...] = queries_ref[blocks[j], :]

        @pl.when(worker >= 0)
        def _():
            back[j].wait()


def key_kernel(
    worker_in, normed_in, weight_in, cache_in, keys_ref, worker_ref, normed_ref, weight_ref, sems
):
    n_local = worker_ref.shape[0]
    block_rows = normed_ref.shape[0] // n_local
    copies = [
        pltpu.make_async_copy(source, target, sems.at[i])
        for i, (source, target) in enumerate(
            [
                (worker_in, worker_ref),
                (normed_in, normed_ref),
                (weight_in, weight_ref),
                (cache_in, keys_ref),
            ]
        )
    ]
    for copy in copies:
        copy.start()
    for copy in copies:
        copy.wait()
    fresh = jnp.dot(
        normed_ref[...], weight_ref[...], preferred_element_type=jnp.float32
    ).astype(jnp.bfloat16)
    for j in range(n_local):
        rows = slice(j * block_rows, (j + 1) * block_rows)

        @pl.when(worker_ref[j] >= 0)
        def _():
            keys_ref[rows, :] = fresh[rows, :]


def value_kernel(
    n_frame,
    n_head,
    n_rep,
    worker_in,
    normed_in,
    weight_in,
    cache_in,
    _,
    values_t_ref,
    masks_ref,
    worker_ref,
    normed_ref,
    weight_ref,
    values_ref,
    sems,
):
    n_local = worker_ref.shape[0]
    tokens = normed_ref.shape[0]
    block_rows = tokens // n_local
    copies = [
        pltpu.make_async_copy(source, target, sems.at[i])
        for i, (source, target) in enumerate(
            [
                (worker_in, worker_ref),
                (normed_in, normed_ref),
                (weight_in, weight_ref),
                (cache_in, values_ref),
            ]
        )
    ]
    for copy in copies:
        copy.start()
    copies[0].wait()
    frame, head, rep = lax.axis_index("frame"), lax.axis_index("head"), lax.axis_index("rep")
    n_place = n_head * n_rep
    for d in range(n_place):
        target = lax.rem(head + d // n_rep, n_head) * n_rep + lax.rem(rep + d % n_rep, n_rep)
        worker = worker_ref[target * (tokens // n_place) // block_rows]
        for s in range(n_frame):
            held = (worker >= 0) & (jnp.bitwise_xor(frame, s) == worker)
            masks_ref[d * n_frame + s : d * n_frame + s + 1, :] = jnp.full(
                (1, masks_ref.shape[1]), jnp.where(held, 1.0, 0.0), jnp.float32
            )
    for copy in copies[1:]:
        copy.wait()
    fresh = jnp.dot(
        normed_ref[...], weight_ref[...], preferred_element_type=jnp.float32
    ).astype(jnp.bfloat16)
    for j in range(n_local):
        rows = slice(j * block_rows, (j + 1) * block_rows)

        @pl.when(worker_ref[j] >= 0)
        def _():
            values_ref[rows, :] = fresh[rows, :]

    for h in range(values_ref.shape[1] // HD):
        cols = slice(h * HD, (h + 1) * HD)
        values_t_ref[cols, :] = values_ref[:, cols].T


def three_terms(x):
    first = x.astype(jnp.bfloat16).astype(jnp.float32)
    rest = x - first
    second = rest.astype(jnp.bfloat16).astype(jnp.float32)
    return [first, second, rest - second]


def collect_kernel(*refs):
    *parts, _, out_ref = refs
    out_ref[...] = sum(part[...].astype(jnp.float32) for part in parts).astype(jnp.bfloat16)


def attend_kernel(count, *refs):
    keys_ref, values_t_ref = refs[count : count + 2]
    for queries_ref, out_ref in zip(refs[:count], refs[-count:]):
        attend_slot(queries_ref, keys_ref, values_t_ref, out_ref)


def attend_slot(queries_ref, keys_ref, values_t_ref, out_ref):
    width = keys_ref.shape[1]
    stats = []
    for h in range(width // HD):
        cols = slice(h * HD, (h + 1) * HD)
        scores = lax.dot_general(
            keys_ref[:, cols],
            queries_ref[:, cols],
            (((1,), (1,)), ((), ())),
            preferred_element_type=jnp.float32,
        )
        highest = jnp.max(scores, axis=0, keepdims=True)
        weights = jnp.exp(scores - highest)
        total = jnp.sum(weights, axis=0, keepdims=True)
        out_ref[cols, :] = jnp.dot(
            values_t_ref[cols, :], weights.astype(jnp.bfloat16), preferred_element_type=jnp.float32
        ).astype(jnp.bfloat16)
        stats += three_terms(highest) + three_terms(total)
    shape = (out_ref.shape[0] - width, out_ref.shape[1])
    row = lax.broadcasted_iota(jnp.int32, shape, 0)
    tail = jnp.zeros(shape, jnp.float32)
    for i, stat in enumerate(stats):
        tail = jnp.where(row == i, stat, tail)
    out_ref[width:, :] = tail.astype(jnp.bfloat16)


def combine_kernel(*refs):
    parts, out_ref = refs[:-1], refs[-1]
    width = out_ref.shape[1]
    tails = [part[width:, :].astype(jnp.float32) for part in parts]
    for h in range(width // HD):
        cols = slice(h * HD, (h + 1) * HD)

        def stat(tail, at):
            at += 6 * h
            return tail[at : at + 1, :] + tail[at + 1 : at + 2, :] + tail[at + 2 : at + 3, :]

        maxima = [stat(tail, 0) for tail in tails]
        highest = functools.reduce(jnp.maximum, maxima)
        factors = [jnp.exp(m - highest) for m in maxima]
        total = sum(stat(tail, 3) * factor for tail, factor in zip(tails, factors))
        summed = sum(
            part[cols, :].astype(jnp.float32) * factor for part, factor in zip(parts, factors)
        )
        out_ref[:, cols] = (summed / total).T.astype(jnp.bfloat16)


def select_kernel(n_frame, n_head, n_rep, *refs):
    slots, masks_ref = refs[:n_frame], refs[n_frame]
    first = len(refs) - (len(refs) - n_frame - 1 - n_head * n_rep) // 2 - n_head * n_rep
    outs = refs[first : first + n_head * n_rep]
    block_rows, width = slots[0].shape
    rows = outs[0].shape[0]
    head, rep = lax.axis_index("head"), lax.axis_index("rep")
    for d in range(n_head * n_rep):
        if rows == block_rows:
            some = slice(None)
        else:
            target = lax.rem(head + d // n_rep, n_head) * n_rep + lax.rem(rep + d % n_rep, n_rep)
            some = pl.ds(pl.multiple_of(lax.rem(target * rows, block_rows), rows), rows)
        for h in range(width // HD):
            cols = slice(h * HD, (h + 1) * HD)
            chosen = jnp.zeros((rows, HD), jnp.float32)
            for s in range(n_frame):
                mask = masks_ref[d * n_frame + s : d * n_frame + s + 1, :]
                chosen = jnp.where(mask > 0.5, slots[s][some, cols].astype(jnp.float32), chosen)
            outs[d][:, cols] = chosen.astype(jnp.bfloat16)


def project_near_kernel(*refs):
    refs, out_ref = refs[:-1], refs[-1]
    parts, weights = refs[: len(refs) // 2], refs[len(refs) // 2 :]
    for start in range(0, out_ref.shape[1], COLUMNS):
        cols = slice(start, start + COLUMNS)
        out_ref[:, cols] = sum(
            jnp.dot(part[...], weight[:, cols], preferred_element_type=jnp.float32)
            for part, weight in zip(parts, weights)
        )


def project_kernel(modulation_ref, near_ref, *refs):
    refs, (out, total_ref, sems) = refs[:-3], refs[-3:]
    parts, weights = refs[: len(refs) // 2], refs[len(refs) // 2 :]
    copies = []
    for i, start in enumerate(range(0, total_ref.shape[1], COLUMNS)):
        cols = slice(start, start + COLUMNS)
        total = near_ref[:, cols] + sum(
            jnp.dot(part[...], weight[:, cols], preferred_element_type=jnp.float32)
            for part, weight in zip(parts, weights)
        )
        total_ref[:, cols] = total * modulation_ref[2:3, cols]
        copies.append(pltpu.make_async_copy(total_ref.at[:, cols], out.at[:, cols], sems.at[i]))
        copies[-1].start()
    for copy in copies:
        copy.wait()


def params(mib):
    return pltpu.CompilerParams(vmem_limit_bytes=mib * MIB)


def cost(flops, moved, exps=0):
    return pl.CostEstimate(flops=flops, bytes_accessed=moved, transcendentals=exps)


def per_device(
    n_frame,
    n_head,
    n_rep,
    latents,
    modulation,
    key_cache,
    value_cache,
    block_worker,
    query_weight,
    key_weight,
    value_weight,
    out_weight,
):
    tokens, model = latents.shape
    n_local = block_worker.shape[0]
    block_rows = tokens // n_local
    width = query_weight.shape[1]
    n_place = n_head * n_rep
    own_rows = tokens // n_place
    tail = TAIL * -(-6 * (width // HD) // TAIL)
    half = jnp.bfloat16

    def along_frame(x, s):
        return lax.ppermute(x, "frame", [(i, i ^ s) for i in range(n_frame)])

    def along_head(x, shift):
        return lax.ppermute(x, "head", [(i, (i + shift) % n_head) for i in range(n_head)])

    def along_rep(x, shift):
        return lax.ppermute(x, "rep", [(i, (i + shift) % n_rep) for i in range(n_rep)])

    def in_frame(x, d):
        pairs = []
        for h in range(n_head):
            for r in range(n_rep):
                to = ((h + d // n_rep) % n_head) * n_rep + (r + d % n_rep) % n_rep
                pairs.append((h * n_rep + r, to))
        return lax.ppermute(x, ("head", "rep"), pairs)

    across = [along_head(out_weight, dh) for dh in range(1, n_head)]

    *slots, normed = pl.pallas_call(
        functools.partial(query_kernel, n_frame),
        out_shape=[jax.ShapeDtypeStruct((block_rows, width), half)] * n_frame
        + [jax.ShapeDtypeStruct(latents.shape, half)],
        in_specs=[HBM] * 4,
        out_specs=[VMEM] * n_frame + [HBM],
        scratch_shapes=[
            pltpu.SMEM(block_worker.shape, jnp.int32),
            pltpu.VMEM(latents.shape, half),
            pltpu.VMEM(modulation.shape, jnp.float32),
            pltpu.VMEM(query_weight.shape, half),
            pltpu.VMEM(latents.shape, half),
            pltpu.VMEM((tokens, width), half),
            pltpu.SemaphoreType.DMA((3 + 2 * n_local,)),
        ],
        compiler_params=params(60),
        cost_estimate=cost(2 * tokens * model * width, 2 * tokens * model + 2 * model * width),
        name="queries",
    )(block_worker, latents, modulation, query_weight)
    arrived = [along_frame(slots[s], s) for s in range(n_frame - 1, 0, -1)]

    keys = pl.pallas_call(
        key_kernel,
        out_shape=jax.ShapeDtypeStruct((tokens, width), half),
        in_specs=[HBM] * 4,
        out_specs=VMEM,
        scratch_shapes=[
            pltpu.SMEM(block_worker.shape, jnp.int32),
            pltpu.VMEM(latents.shape, half),
            pltpu.VMEM(key_weight.shape, half),
            pltpu.SemaphoreType.DMA((4,)),
        ],
        compiler_params=params(53),
        cost_estimate=cost(2 * tokens * model * width, 6 * tokens * model),
        name="keys",
    )(block_worker, normed, key_weight, key_cache)

    mine = pl.pallas_call(
        collect_kernel,
        out_shape=jax.ShapeDtypeStruct((block_rows, width), half),
        in_specs=[VMEM] * n_frame + [ANY],
        out_specs=VMEM,
        compiler_params=params(16),
        cost_estimate=cost(n_frame * block_rows * width, 2 * n_frame * block_rows * width),
        name="collect",
    )(slots[0], *arrived, keys)

    values_t, masks = pl.pallas_call(
        functools.partial(value_kernel, n_frame, n_head, n_rep),
        out_shape=[
            jax.ShapeDtypeStruct((width, tokens), half),
            jax.ShapeDtypeStruct((n_place * n_frame, HD), jnp.float32),
        ],
        in_specs=[HBM] * 4 + [ANY],
        out_specs=[VMEM] * 2,
        scratch_shapes=[
            pltpu.SMEM(block_worker.shape, jnp.int32),
            pltpu.VMEM(latents.shape, half),
            pltpu.VMEM(value_weight.shape, half),
            pltpu.VMEM(value_cache.shape, half),
            pltpu.SemaphoreType.DMA((4,)),
        ],
        compiler_params=params(53),
        cost_estimate=cost(2 * tokens * model * width, 6 * tokens * model),
        name="values",
    )(block_worker, normed, value_weight, value_cache, mine)

    def attend(queries, after=()):
        count = len(queries)
        return pl.pallas_call(
            functools.partial(attend_kernel, count),
            out_shape=[jax.ShapeDtypeStruct((width + tail, block_rows), half)] * count,
            in_specs=[VMEM] * (count + 2) + [ANY] * len(after),
            out_specs=[VMEM] * count,
            compiler_params=params(16),
            cost_estimate=cost(
                4 * tokens * block_rows * width * count,
                20 * tokens * width,
                tokens * block_rows * width // HD * count,
            ),
            name="attend",
        )(*queries, keys, values_t, *after)

    far_first = list(range(n_frame - 1, 0, -1))
    shared = [along_frame(mine, s) for s in far_first]
    own = list(attend([mine]))
    partial = []
    for start in range(0, n_frame - 1, SLOTS):
        partial += attend(shared[start : start + SLOTS], own)
    sent = [along_frame(x, s) for s, x in zip(far_first, partial)]
    attended = pl.pallas_call(
        combine_kernel,
        out_shape=jax.ShapeDtypeStruct((block_rows, width), half),
        in_specs=[VMEM] * n_frame,
        out_specs=VMEM,
        compiler_params=params(16),
        cost_estimate=cost(4 * n_frame * block_rows * width, 2 * n_frame * block_rows * width),
        name="combine",
    )(*own, *sent)
    copies = {s: along_frame(attended, s) for s in far_first}
    copies = [attended] + [copies[s] for s in range(1, n_frame)]
    pieces = pl.pallas_call(
        functools.partial(select_kernel, n_frame, n_head, n_rep),
        out_shape=[jax.ShapeDtypeStruct((own_rows, width), half)] * n_place
        + [jax.ShapeDtypeStruct(w.shape, w.dtype) for w in across],
        in_specs=[VMEM] * (n_frame + 1) + [ANY] * len(across),
        out_specs=[VMEM] * n_place + [ANY] * len(across),
        input_output_aliases={n_frame + 1 + i: n_place + i for i in range(len(across))},
        compiler_params=params(16),
        cost_estimate=cost(0, 4 * n_frame * block_rows * width),
        name="select",
    )(*copies, masks, *across)
    pieces, across = pieces[:n_place], list(pieces[n_place:])
    moved = {d: in_frame(pieces[d], d) for d in range(n_place - 1, 0, -1)}
    pieces = [pieces[0]] + [moved[d] for d in range(1, n_place)]

    weights = []
    for held in [out_weight] + across:
        weights += [held] + [along_rep(held, dr) for dr in range(1, n_rep)]
    near = pl.pallas_call(
        project_near_kernel,
        out_shape=jax.ShapeDtypeStruct((own_rows, model), jnp.float32),
        in_specs=[VMEM] * (2 * n_rep),
        out_specs=VMEM,
        compiler_params=params(16),
        cost_estimate=cost(2 * own_rows * model * width * n_rep, 4 * model * width * n_rep),
        name="project_near",
    )(*pieces[:n_rep], *weights[:n_rep])
    return pl.pallas_call(
        project_kernel,
        out_shape=jax.ShapeDtypeStruct((own_rows, model), jnp.float32),
        in_specs=[VMEM] * (2 + 2 * (n_place - n_rep)),
        out_specs=ANY,
        scratch_shapes=[
            pltpu.VMEM((own_rows, model), jnp.float32),
            pltpu.SemaphoreType.DMA((-(-model // COLUMNS),)),
        ],
        compiler_params=params(16),
        cost_estimate=cost(2 * own_rows * model * width * n_rep, 2 * model * width * n_place),
        name="project",
    )(modulation, near, *pieces[n_rep:], *weights[n_rep:])


def solution(mesh):
    in_specs = (
        P(("groups", "frame"), None),
        P("groups", None),
        P(("groups", "frame"), ("head", "rep")),
        P(("groups", "frame"), ("head", "rep")),
        P(("groups", "frame")),
        P(None, ("head", "rep")),
        P(None, ("head", "rep")),
        P(None, ("head", "rep")),
        P(("head", "rep"), None),
    )
    out_specs = P(("groups", "frame", "head", "rep"), None)
    body = functools.partial(
        per_device, mesh.shape["frame"], mesh.shape["head"], mesh.shape["rep"]
    )
    return jax.shard_map(body, mesh=mesh, in_specs=in_specs, out_specs=out_specs, check_vma=False)
```

```python
import functools

import jax
import jax.numpy as jnp
from jax import lax
from jax.experimental import pallas as pl
from jax.experimental.pallas import tpu as pltpu
from jax.sharding import PartitionSpec as P

HD = 128
EPS = 1e-06
CHUNK = 16
COLUMNS = 512
SLOTS = 3
TAIL = 16
MIB = 1 << 20

VMEM = pl.BlockSpec(memory_space=pltpu.VMEM)
HBM = pl.BlockSpec(memory_space=pltpu.HBM)
ANY = pl.BlockSpec(memory_space=pl.ANY)


def normalize_block(latents_ref, modulation_ref, normed_ref, start, block_rows):
    def one_chunk(c, carry):
        at = pl.multiple_of(start + c * CHUNK, CHUNK)
        floats = latents_ref[pl.ds(at, CHUNK), :].astype(jnp.float32)
        center = floats - jnp.mean(floats, axis=-1, keepdims=True)
        spread = jnp.mean(center * center, axis=-1, keepdims=True)
        normed_ref[pl.ds(at, CHUNK), :] = (
            center * lax.rsqrt(spread + EPS) * (1.0 + modulation_ref[1:2, :])
            + modulation_ref[0:1, :]
        ).astype(jnp.bfloat16)
        return carry

    lax.fori_loop(0, block_rows // CHUNK, one_chunk, 0, unroll=4)


def query_kernel(n_frame, worker_in, latents_in, modulation_in, weight_in, *rest):
    outs, normed_out = rest[:n_frame], rest[n_frame]
    worker_ref, latents_ref, modulation_ref, weight_ref, normed_ref, queries_ref, sems = rest[
        n_frame + 1 :
    ]
    n_local = worker_ref.shape[0]
    block_rows = latents_ref.shape[0] // n_local
    frame = lax.axis_index("frame")
    blocks = [slice(j * block_rows, (j + 1) * block_rows) for j in range(n_local)]
    first = [
        pltpu.make_async_copy(worker_in, worker_ref, sems.at[0]),
        pltpu.make_async_copy(modulation_in, modulation_ref, sems.at[1]),
    ]
    each = [
        pltpu.make_async_copy(latents_in.at[rows, :], latents_ref.at[rows, :], sems.at[3 + j])
        for j, rows in enumerate(blocks)
    ]
    back = [
        pltpu.make_async_copy(
            normed_ref.at[rows, :], normed_out.at[rows, :], sems.at[3 + n_local + j]
        )
        for j, rows in enumerate(blocks)
    ]
    weight = pltpu.make_async_copy(weight_in, weight_ref, sems.at[2])
    for copy in first + each + [weight]:
        copy.start()
    for s in range(n_frame):
        outs[s][...] = jnp.zeros_like(outs[s])
    for copy in first:
        copy.wait()
    for j in range(n_local):
        each[j].wait()

        @pl.when(worker_ref[j] >= 0)
        def _():
            normalize_block(latents_ref, modulation_ref, normed_ref, j * block_rows, block_rows)
            back[j].start()

    weight.wait()
    queries_ref[...] = (
        jnp.dot(normed_ref[...], weight_ref[...], preferred_element_type=jnp.float32) * HD ** (-0.5)
    ).astype(jnp.bfloat16)
    for j in range(n_local):
        worker = worker_ref[j]
        for s in range(n_frame):

            @pl.when((worker >= 0) & (jnp.bitwise_xor(frame, s) == worker))
            def _():
                outs[s][...] = queries_ref[blocks[j], :]

        @pl.when(worker >= 0)
        def _():
            back[j].wait()


def key_kernel(
    worker_in, normed_in, weight_in, cache_in, _, keys_ref, worker_ref, normed_ref, weight_ref, sems
):
    n_local = worker_ref.shape[0]
    block_rows = normed_ref.shape[0] // n_local
    copies = [
        pltpu.make_async_copy(source, target, sems.at[i])
        for i, (source, target) in enumerate(
            [
                (worker_in, worker_ref),
                (normed_in, normed_ref),
                (weight_in, weight_ref),
                (cache_in, keys_ref),
            ]
        )
    ]
    for copy in copies:
        copy.start()
    for copy in copies:
        copy.wait()
    fresh = jnp.dot(
        normed_ref[...], weight_ref[...], preferred_element_type=jnp.float32
    ).astype(jnp.bfloat16)
    for j in range(n_local):
        rows = slice(j * block_rows, (j + 1) * block_rows)

        @pl.when(worker_ref[j] >= 0)
        def _():
            keys_ref[rows, :] = fresh[rows, :]


def value_kernel(
    n_frame,
    n_head,
    n_rep,
    worker_in,
    normed_in,
    weight_in,
    cache_in,
    _,
    values_t_ref,
    masks_ref,
    worker_ref,
    normed_ref,
    weight_ref,
    values_ref,
    sems,
):
    n_local = worker_ref.shape[0]
    tokens = normed_ref.shape[0]
    block_rows = tokens // n_local
    copies = [
        pltpu.make_async_copy(source, target, sems.at[i])
        for i, (source, target) in enumerate(
            [
                (worker_in, worker_ref),
                (normed_in, normed_ref),
                (weight_in, weight_ref),
                (cache_in, values_ref),
            ]
        )
    ]
    for copy in copies:
        copy.start()
    copies[0].wait()
    frame, head, rep = lax.axis_index("frame"), lax.axis_index("head"), lax.axis_index("rep")
    n_place = n_head * n_rep
    for d in range(n_place):
        target = lax.rem(head + d // n_rep, n_head) * n_rep + lax.rem(rep + d % n_rep, n_rep)
        worker = worker_ref[target * (tokens // n_place) // block_rows]
        for s in range(n_frame):
            held = (worker >= 0) & (jnp.bitwise_xor(frame, s) == worker)
            masks_ref[d * n_frame + s : d * n_frame + s + 1, :] = jnp.full(
                (1, masks_ref.shape[1]), jnp.where(held, 1.0, 0.0), jnp.float32
            )
    for copy in copies[1:]:
        copy.wait()
    fresh = jnp.dot(
        normed_ref[...], weight_ref[...], preferred_element_type=jnp.float32
    ).astype(jnp.bfloat16)
    for j in range(n_local):
        rows = slice(j * block_rows, (j + 1) * block_rows)

        @pl.when(worker_ref[j] >= 0)
        def _():
            values_ref[rows, :] = fresh[rows, :]

    for h in range(values_ref.shape[1] // HD):
        cols = slice(h * HD, (h + 1) * HD)
        values_t_ref[cols, :] = values_ref[:, cols].T


def three_terms(x):
    first = x.astype(jnp.bfloat16).astype(jnp.float32)
    rest = x - first
    second = rest.astype(jnp.bfloat16).astype(jnp.float32)
    return [first, second, rest - second]


def collect_kernel(*refs):
    *parts, _, out_ref = refs
    out_ref[...] = sum(part[...].astype(jnp.float32) for part in parts).astype(jnp.bfloat16)


def attend_kernel(count, *refs):
    keys_ref, values_t_ref = refs[count : count + 2]
    for queries_ref, out_ref in zip(refs[:count], refs[-count:]):
        attend_slot(queries_ref, keys_ref, values_t_ref, out_ref)


def attend_slot(queries_ref, keys_ref, values_t_ref, out_ref):
    width = keys_ref.shape[1]
    stats = []
    for h in range(width // HD):
        cols = slice(h * HD, (h + 1) * HD)
        scores = lax.dot_general(
            keys_ref[:, cols],
            queries_ref[:, cols],
            (((1,), (1,)), ((), ())),
            preferred_element_type=jnp.float32,
        )
        highest = jnp.max(scores, axis=0, keepdims=True)
        weights = jnp.exp(scores - highest)
        total = jnp.sum(weights, axis=0, keepdims=True)
        out_ref[cols, :] = jnp.dot(
            values_t_ref[cols, :], weights.astype(jnp.bfloat16), preferred_element_type=jnp.float32
        ).astype(jnp.bfloat16)
        stats += three_terms(highest) + three_terms(total)
    write_stats(out_ref, width, stats)


def write_stats(out_ref, width, stats):
    shape = (out_ref.shape[0] - width, out_ref.shape[1])
    row = lax.broadcasted_iota(jnp.int32, shape, 0)
    tail = jnp.zeros(shape, jnp.float32)
    for i, stat in enumerate(stats):
        tail = jnp.where(row == i, stat, tail)
    out_ref[width:, :] = tail.astype(jnp.bfloat16)


def add_up(parts, width, h):
    tails = [part[width:, :].astype(jnp.float32) for part in parts]

    def stat(tail, at):
        at += 6 * h
        return tail[at : at + 1, :] + tail[at + 1 : at + 2, :] + tail[at + 2 : at + 3, :]

    maxima = [stat(tail, 0) for tail in tails]
    highest = functools.reduce(jnp.maximum, maxima)
    factors = [jnp.exp(m - highest) for m in maxima]
    total = sum(stat(tail, 3) * factor for tail, factor in zip(tails, factors))
    summed = sum(
        part[h * HD : (h + 1) * HD, :].astype(jnp.float32) * factor
        for part, factor in zip(parts, factors)
    )
    return highest, total, summed


def merge_kernel(width, *refs):
    parts, out_ref = refs[:-1], refs[-1]
    stats = []
    for h in range(width // HD):
        highest, total, summed = add_up(parts, width, h)
        out_ref[h * HD : (h + 1) * HD, :] = summed.astype(jnp.bfloat16)
        stats += three_terms(highest) + three_terms(total)
    write_stats(out_ref, width, stats)


def combine_kernel(*refs):
    parts, out_ref = refs[:-1], refs[-1]
    width = out_ref.shape[1]
    for h in range(width // HD):
        _, total, summed = add_up(parts, width, h)
        out_ref[:, h * HD : (h + 1) * HD] = (summed / total).T.astype(jnp.bfloat16)


def select_kernel(n_frame, n_head, n_rep, *refs):
    slots, masks_ref = refs[:n_frame], refs[n_frame]
    first = len(refs) - (len(refs) - n_frame - 1 - n_head * n_rep) // 2 - n_head * n_rep
    outs = refs[first : first + n_head * n_rep]
    block_rows, width = slots[0].shape
    rows = outs[0].shape[0]
    head, rep = lax.axis_index("head"), lax.axis_index("rep")
    for d in range(n_head * n_rep):
        if rows == block_rows:
            some = slice(None)
        else:
            target = lax.rem(head + d // n_rep, n_head) * n_rep + lax.rem(rep + d % n_rep, n_rep)
            some = pl.ds(pl.multiple_of(lax.rem(target * rows, block_rows), rows), rows)
        for h in range(width // HD):
            cols = slice(h * HD, (h + 1) * HD)
            chosen = jnp.zeros((rows, HD), jnp.float32)
            for s in range(n_frame):
                mask = masks_ref[d * n_frame + s : d * n_frame + s + 1, :]
                chosen = jnp.where(mask > 0.5, slots[s][some, cols].astype(jnp.float32), chosen)
            outs[d][:, cols] = chosen.astype(jnp.bfloat16)


def project_near_kernel(*refs):
    refs, out_ref = refs[:-1], refs[-1]
    parts, weights = refs[: len(refs) // 2], refs[len(refs) // 2 :]
    for start in range(0, out_ref.shape[1], COLUMNS):
        cols = slice(start, start + COLUMNS)
        out_ref[:, cols] = sum(
            jnp.dot(part[...], weight[:, cols], preferred_element_type=jnp.float32)
            for part, weight in zip(parts, weights)
        )


def project_kernel(modulation_ref, near_ref, *refs):
    refs, (out, total_ref, sems) = refs[:-3], refs[-3:]
    parts, weights = refs[: len(refs) // 2], refs[len(refs) // 2 :]
    copies = []
    for i, start in enumerate(range(0, total_ref.shape[1], COLUMNS)):
        cols = slice(start, start + COLUMNS)
        total = near_ref[:, cols] + sum(
            jnp.dot(part[...], weight[:, cols], preferred_element_type=jnp.float32)
            for part, weight in zip(parts, weights)
        )
        total_ref[:, cols] = total * modulation_ref[2:3, cols]
        copies.append(pltpu.make_async_copy(total_ref.at[:, cols], out.at[:, cols], sems.at[i]))
        copies[-1].start()
    for copy in copies:
        copy.wait()


def params(mib):
    return pltpu.CompilerParams(vmem_limit_bytes=mib * MIB)


def cost(flops, moved, exps=0):
    return pl.CostEstimate(flops=flops, bytes_accessed=moved, transcendentals=exps)


def per_device(
    n_frame,
    n_head,
    n_rep,
    latents,
    modulation,
    key_cache,
    value_cache,
    block_worker,
    query_weight,
    key_weight,
    value_weight,
    out_weight,
):
    tokens, model = latents.shape
    n_local = block_worker.shape[0]
    block_rows = tokens // n_local
    width = query_weight.shape[1]
    n_place = n_head * n_rep
    own_rows = tokens // n_place
    tail = TAIL * -(-6 * (width // HD) // TAIL)
    half = jnp.bfloat16

    def along_frame(x, s):
        return lax.ppermute(x, "frame", [(i, i ^ s) for i in range(n_frame)])

    def spread(x, after=None):
        held = {0: x}
        bit = n_frame // 2
        while bit:
            held.update({s ^ bit: along_frame(held[s], bit) for s in list(held)})
            if after is not None and len(held) == 2:
                held[bit], _ = lax.optimization_barrier((held[bit], after))
            bit //= 2
        return held

    def gather(parts, merge):
        arrived = {s: [parts[s]] for s in range(n_frame)}
        bit = 1
        while bit < n_frame:
            for s in range(n_frame - bit, 0, -2 * bit):
                piece = merge(arrived[s]) if len(arrived[s]) > 1 else arrived[s][0]
                arrived[s ^ bit].append(along_frame(piece, bit))
            bit *= 2
        return arrived[0]

    def along_head(x, shift):
        return lax.ppermute(x, "head", [(i, (i + shift) % n_head) for i in range(n_head)])

    def along_rep(x, shift):
        return lax.ppermute(x, "rep", [(i, (i + shift) % n_rep) for i in range(n_rep)])

    def in_frame(x, d):
        pairs = []
        for h in range(n_head):
            for r in range(n_rep):
                to = ((h + d // n_rep) % n_head) * n_rep + (r + d % n_rep) % n_rep
                pairs.append((h * n_rep + r, to))
        return lax.ppermute(x, ("head", "rep"), pairs)

    across = [along_head(out_weight, dh) for dh in range(1, n_head)]

    *slots, normed = pl.pallas_call(
        functools.partial(query_kernel, n_frame),
        out_shape=[jax.ShapeDtypeStruct((block_rows, width), half)] * n_frame
        + [jax.ShapeDtypeStruct(latents.shape, half)],
        in_specs=[HBM] * 4,
        out_specs=[VMEM] * n_frame + [HBM],
        scratch_shapes=[
            pltpu.SMEM(block_worker.shape, jnp.int32),
            pltpu.VMEM(latents.shape, half),
            pltpu.VMEM(modulation.shape, jnp.float32),
            pltpu.VMEM(query_weight.shape, half),
            pltpu.VMEM(latents.shape, half),
            pltpu.VMEM((tokens, width), half),
            pltpu.SemaphoreType.DMA((3 + 2 * n_local,)),
        ],
        compiler_params=params(60),
        cost_estimate=cost(2 * tokens * model * width, 2 * tokens * model + 2 * model * width),
        name="queries",
    )(block_worker, latents, modulation, query_weight)
    sums = [slots[0]]

    def add(blocks):
        sums.append(sum(blocks[1:], blocks[0]))
        return sums[-1]

    arrived = gather(slots, add)

    keys = pl.pallas_call(
        key_kernel,
        out_shape=jax.ShapeDtypeStruct((tokens, width), half),
        in_specs=[HBM] * 4 + [ANY],
        out_specs=VMEM,
        scratch_shapes=[
            pltpu.SMEM(block_worker.shape, jnp.int32),
            pltpu.VMEM(latents.shape, half),
            pltpu.VMEM(key_weight.shape, half),
            pltpu.SemaphoreType.DMA((4,)),
        ],
        compiler_params=params(53),
        cost_estimate=cost(2 * tokens * model * width, 6 * tokens * model),
        name="keys",
    )(block_worker, normed, key_weight, key_cache, sums[-1])

    mine = pl.pallas_call(
        collect_kernel,
        out_shape=jax.ShapeDtypeStruct((block_rows, width), half),
        in_specs=[VMEM] * len(arrived) + [ANY],
        out_specs=VMEM,
        compiler_params=params(16),
        cost_estimate=cost(n_frame * block_rows * width, 2 * n_frame * block_rows * width),
        name="collect",
    )(*arrived, keys)

    values_t, masks = pl.pallas_call(
        functools.partial(value_kernel, n_frame, n_head, n_rep),
        out_shape=[
            jax.ShapeDtypeStruct((width, tokens), half),
            jax.ShapeDtypeStruct((n_place * n_frame, HD), jnp.float32),
        ],
        in_specs=[HBM] * 4 + [ANY],
        out_specs=[VMEM] * 2,
        scratch_shapes=[
            pltpu.SMEM(block_worker.shape, jnp.int32),
            pltpu.VMEM(latents.shape, half),
            pltpu.VMEM(value_weight.shape, half),
            pltpu.VMEM(value_cache.shape, half),
            pltpu.SemaphoreType.DMA((4,)),
        ],
        compiler_params=params(53),
        cost_estimate=cost(2 * tokens * model * width, 6 * tokens * model),
        name="values",
    )(block_worker, normed, value_weight, value_cache, mine)

    def attend(queries, after=()):
        count = len(queries)
        return pl.pallas_call(
            functools.partial(attend_kernel, count),
            out_shape=[jax.ShapeDtypeStruct((width + tail, block_rows), half)] * count,
            in_specs=[VMEM] * (count + 2) + [ANY] * len(after),
            out_specs=[VMEM] * count,
            compiler_params=params(16),
            cost_estimate=cost(
                4 * tokens * block_rows * width * count,
                20 * tokens * width,
                tokens * block_rows * width // HD * count,
            ),
            name="attend",
        )(*queries, keys, values_t, *after)

    shared = spread(mine, masks)
    own = attend([mine], [shared[n_frame // 2]])
    others = list(range(n_frame - 1, 0, -1))
    partial = []
    for start in range(0, n_frame - 1, SLOTS):
        partial += attend([shared[s] for s in others[start : start + SLOTS]], own)

    def merge(parts):
        return pl.pallas_call(
            functools.partial(merge_kernel, width),
            out_shape=jax.ShapeDtypeStruct((width + tail, block_rows), half),
            in_specs=[VMEM] * len(parts),
            out_specs=VMEM,
            compiler_params=params(16),
            cost_estimate=cost(4 * n_frame * block_rows * width, 4 * n_frame * block_rows * width),
            name="merge",
        )(*parts)

    gathered = gather({0: own[0], **dict(zip(others, partial))}, merge)
    attended = pl.pallas_call(
        combine_kernel,
        out_shape=jax.ShapeDtypeStruct((block_rows, width), half),
        in_specs=[VMEM] * len(gathered),
        out_specs=VMEM,
        compiler_params=params(16),
        cost_estimate=cost(4 * n_frame * block_rows * width, 2 * n_frame * block_rows * width),
        name="combine",
    )(*gathered)
    copies = spread(attended)
    copies = [copies[s] for s in range(n_frame)]
    pieces = pl.pallas_call(
        functools.partial(select_kernel, n_frame, n_head, n_rep),
        out_shape=[jax.ShapeDtypeStruct((own_rows, width), half)] * n_place
        + [jax.ShapeDtypeStruct(w.shape, w.dtype) for w in across],
        in_specs=[VMEM] * (n_frame + 1) + [ANY] * len(across),
        out_specs=[VMEM] * n_place + [ANY] * len(across),
        input_output_aliases={n_frame + 1 + i: n_place + i for i in range(len(across))},
        compiler_params=params(16),
        cost_estimate=cost(0, 4 * n_frame * block_rows * width),
        name="select",
    )(*copies, masks, *across)
    pieces, across = pieces[:n_place], list(pieces[n_place:])
    moved = {d: in_frame(pieces[d], d) for d in range(n_place - 1, 0, -1)}
    pieces = [pieces[0]] + [moved[d] for d in range(1, n_place)]

    weights = []
    for held in [out_weight] + across:
        weights += [held] + [along_rep(held, dr) for dr in range(1, n_rep)]
    near = pl.pallas_call(
        project_near_kernel,
        out_shape=jax.ShapeDtypeStruct((own_rows, model), jnp.float32),
        in_specs=[VMEM] * (2 * n_rep),
        out_specs=VMEM,
        compiler_params=params(16),
        cost_estimate=cost(2 * own_rows * model * width * n_rep, 4 * model * width * n_rep),
        name="project_near",
    )(*pieces[:n_rep], *weights[:n_rep])
    return pl.pallas_call(
        project_kernel,
        out_shape=jax.ShapeDtypeStruct((own_rows, model), jnp.float32),
        in_specs=[VMEM] * (2 + 2 * (n_place - n_rep)),
        out_specs=ANY,
        scratch_shapes=[
            pltpu.VMEM((own_rows, model), jnp.float32),
            pltpu.SemaphoreType.DMA((-(-model // COLUMNS),)),
        ],
        compiler_params=params(16),
        cost_estimate=cost(2 * own_rows * model * width * n_rep, 2 * model * width * n_place),
        name="project",
    )(modulation, near, *pieces[n_rep:], *weights[n_rep:])


def solution(mesh):
    in_specs = (
        P(("groups", "frame"), None),
        P("groups", None),
        P(("groups", "frame"), ("head", "rep")),
        P(("groups", "frame"), ("head", "rep")),
        P(("groups", "frame")),
        P(None, ("head", "rep")),
        P(None, ("head", "rep")),
        P(None, ("head", "rep")),
        P(("head", "rep"), None),
    )
    out_specs = P(("groups", "frame", "head", "rep"), None)
    body = functools.partial(
        per_device, mesh.shape["frame"], mesh.shape["head"], mesh.shape["rep"]
    )
    return jax.shard_map(body, mesh=mesh, in_specs=in_specs, out_specs=out_specs, check_vma=False)
```

```python
import functools

import jax
import jax.numpy as jnp
from jax import lax
from jax.experimental import pallas as pl
from jax.experimental.pallas import tpu as pltpu
from jax.sharding import PartitionSpec as P

HD = 128
EPS = 1e-06
CHUNK = 16
COLUMNS = 512
SLOTS = 3
TAIL = 16
MIB = 1 << 20

VMEM = pl.BlockSpec(memory_space=pltpu.VMEM)
HBM = pl.BlockSpec(memory_space=pltpu.HBM)
ANY = pl.BlockSpec(memory_space=pl.ANY)


def normalize_block(latents_ref, modulation_ref, normed_ref, start, block_rows):
    def one_chunk(c, carry):
        at = pl.multiple_of(start + c * CHUNK, CHUNK)
        floats = latents_ref[pl.ds(at, CHUNK), :].astype(jnp.float32)
        center = floats - jnp.mean(floats, axis=-1, keepdims=True)
        spread = jnp.mean(center * center, axis=-1, keepdims=True)
        normed_ref[pl.ds(at, CHUNK), :] = (
            center * lax.rsqrt(spread + EPS) * (1.0 + modulation_ref[1:2, :])
            + modulation_ref[0:1, :]
        ).astype(jnp.bfloat16)
        return carry

    lax.fori_loop(0, block_rows // CHUNK, one_chunk, 0, unroll=4)


def query_kernel(n_frame, worker_in, latents_in, modulation_in, weight_in, *rest):
    outs, normed_out = rest[:n_frame], rest[n_frame]
    worker_ref, latents_ref, modulation_ref, weight_ref, normed_ref, queries_ref, sems = rest[
        n_frame + 1 :
    ]
    n_local = worker_ref.shape[0]
    block_rows = latents_ref.shape[0] // n_local
    frame = lax.axis_index("frame")
    blocks = [slice(j * block_rows, (j + 1) * block_rows) for j in range(n_local)]
    first = [
        pltpu.make_async_copy(worker_in, worker_ref, sems.at[0]),
        pltpu.make_async_copy(modulation_in, modulation_ref, sems.at[1]),
    ]
    each = [
        pltpu.make_async_copy(latents_in.at[rows, :], latents_ref.at[rows, :], sems.at[3 + j])
        for j, rows in enumerate(blocks)
    ]
    back = [
        pltpu.make_async_copy(
            normed_ref.at[rows, :], normed_out.at[rows, :], sems.at[3 + n_local + j]
        )
        for j, rows in enumerate(blocks)
    ]
    weight = pltpu.make_async_copy(weight_in, weight_ref, sems.at[2])
    for copy in first + each + [weight]:
        copy.start()
    for s in range(n_frame):
        outs[s][...] = jnp.zeros_like(outs[s])
    for copy in first:
        copy.wait()
    for j in range(n_local):
        each[j].wait()

        @pl.when(worker_ref[j] >= 0)
        def _():
            normalize_block(latents_ref, modulation_ref, normed_ref, j * block_rows, block_rows)
            back[j].start()

    weight.wait()
    queries_ref[...] = (
        jnp.dot(normed_ref[...], weight_ref[...], preferred_element_type=jnp.float32) * HD ** (-0.5)
    ).astype(jnp.bfloat16)
    for j in range(n_local):
        worker = worker_ref[j]
        for s in range(n_frame):

            @pl.when((worker >= 0) & (jnp.bitwise_xor(frame, s) == worker))
            def _():
                outs[s][...] = queries_ref[blocks[j], :]

        @pl.when(worker >= 0)
        def _():
            back[j].wait()


def key_kernel(
    worker_in, normed_in, weight_in, cache_in, keys_ref, worker_ref, normed_ref, weight_ref, sems
):
    n_local = worker_ref.shape[0]
    block_rows = normed_ref.shape[0] // n_local
    copies = [
        pltpu.make_async_copy(source, target, sems.at[i])
        for i, (source, target) in enumerate(
            [
                (worker_in, worker_ref),
                (normed_in, normed_ref),
                (weight_in, weight_ref),
                (cache_in, keys_ref),
            ]
        )
    ]
    for copy in copies:
        copy.start()
    for copy in copies:
        copy.wait()
    fresh = jnp.dot(
        normed_ref[...], weight_ref[...], preferred_element_type=jnp.float32
    ).astype(jnp.bfloat16)
    for j in range(n_local):
        rows = slice(j * block_rows, (j + 1) * block_rows)

        @pl.when(worker_ref[j] >= 0)
        def _():
            keys_ref[rows, :] = fresh[rows, :]


def value_kernel(
    n_frame,
    n_head,
    n_rep,
    worker_in,
    normed_in,
    weight_in,
    cache_in,
    _,
    values_t_ref,
    masks_ref,
    worker_ref,
    normed_ref,
    weight_ref,
    values_ref,
    sems,
):
    n_local = worker_ref.shape[0]
    tokens = normed_ref.shape[0]
    block_rows = tokens // n_local
    copies = [
        pltpu.make_async_copy(source, target, sems.at[i])
        for i, (source, target) in enumerate(
            [
                (worker_in, worker_ref),
                (normed_in, normed_ref),
                (weight_in, weight_ref),
                (cache_in, values_ref),
            ]
        )
    ]
    for copy in copies:
        copy.start()
    copies[0].wait()
    frame, head, rep = lax.axis_index("frame"), lax.axis_index("head"), lax.axis_index("rep")
    n_place = n_head * n_rep
    for d in range(n_place):
        target = lax.rem(head + d // n_rep, n_head) * n_rep + lax.rem(rep + d % n_rep, n_rep)
        worker = worker_ref[target * (tokens // n_place) // block_rows]
        for s in range(n_frame):
            held = (worker >= 0) & (jnp.bitwise_xor(frame, s) == worker)
            masks_ref[d * n_frame + s : d * n_frame + s + 1, :] = jnp.full(
                (1, masks_ref.shape[1]), jnp.where(held, 1.0, 0.0), jnp.float32
            )
    for copy in copies[1:]:
        copy.wait()
    fresh = jnp.dot(
        normed_ref[...], weight_ref[...], preferred_element_type=jnp.float32
    ).astype(jnp.bfloat16)
    for j in range(n_local):
        rows = slice(j * block_rows, (j + 1) * block_rows)

        @pl.when(worker_ref[j] >= 0)
        def _():
            values_ref[rows, :] = fresh[rows, :]

    for h in range(values_ref.shape[1] // HD):
        cols = slice(h * HD, (h + 1) * HD)
        values_t_ref[cols, :] = values_ref[:, cols].T


def three_terms(x):
    first = x.astype(jnp.bfloat16).astype(jnp.float32)
    rest = x - first
    second = rest.astype(jnp.bfloat16).astype(jnp.float32)
    return [first, second, rest - second]


def collect_kernel(*refs):
    *parts, _, out_ref = refs
    out_ref[...] = sum(part[...].astype(jnp.float32) for part in parts).astype(jnp.bfloat16)


def attend_kernel(count, *refs):
    keys_ref, values_t_ref = refs[count : count + 2]
    for queries_ref, out_ref in zip(refs[:count], refs[-count:]):
        attend_slot(queries_ref, keys_ref, values_t_ref, out_ref)


def attend_slot(queries_ref, keys_ref, values_t_ref, out_ref):
    width = keys_ref.shape[1]
    stats = []
    for h in range(width // HD):
        cols = slice(h * HD, (h + 1) * HD)
        scores = lax.dot_general(
            keys_ref[:, cols],
            queries_ref[:, cols],
            (((1,), (1,)), ((), ())),
            preferred_element_type=jnp.float32,
        )
        highest = jnp.max(scores, axis=0, keepdims=True)
        weights = jnp.exp(scores - highest)
        total = jnp.sum(weights, axis=0, keepdims=True)
        out_ref[cols, :] = jnp.dot(
            values_t_ref[cols, :], weights.astype(jnp.bfloat16), preferred_element_type=jnp.float32
        ).astype(jnp.bfloat16)
        stats += three_terms(highest) + three_terms(total)
    shape = (out_ref.shape[0] - width, out_ref.shape[1])
    row = lax.broadcasted_iota(jnp.int32, shape, 0)
    tail = jnp.zeros(shape, jnp.float32)
    for i, stat in enumerate(stats):
        tail = jnp.where(row == i, stat, tail)
    out_ref[width:, :] = tail.astype(jnp.bfloat16)


def combine_kernel(*refs):
    parts, out_ref = refs[:-1], refs[-1]
    width = out_ref.shape[1]
    tails = [part[width:, :].astype(jnp.float32) for part in parts]
    for h in range(width // HD):
        cols = slice(h * HD, (h + 1) * HD)

        def stat(tail, at):
            at += 6 * h
            return tail[at : at + 1, :] + tail[at + 1 : at + 2, :] + tail[at + 2 : at + 3, :]

        maxima = [stat(tail, 0) for tail in tails]
        highest = functools.reduce(jnp.maximum, maxima)
        factors = [jnp.exp(m - highest) for m in maxima]
        total = sum(stat(tail, 3) * factor for tail, factor in zip(tails, factors))
        summed = sum(
            part[cols, :].astype(jnp.float32) * factor for part, factor in zip(parts, factors)
        )
        out_ref[:, cols] = (summed / total).T.astype(jnp.bfloat16)


def select_kernel(n_frame, n_head, n_rep, *refs):
    slots, masks_ref = refs[:n_frame], refs[n_frame]
    first = len(refs) - (len(refs) - n_frame - 1 - n_head * n_rep) // 2 - n_head * n_rep
    outs = refs[first : first + n_head * n_rep]
    block_rows, width = slots[0].shape
    rows = outs[0].shape[0]
    head, rep = lax.axis_index("head"), lax.axis_index("rep")
    for d in range(n_head * n_rep):
        if rows == block_rows:
            some = slice(None)
        else:
            target = lax.rem(head + d // n_rep, n_head) * n_rep + lax.rem(rep + d % n_rep, n_rep)
            some = pl.ds(pl.multiple_of(lax.rem(target * rows, block_rows), rows), rows)
        for h in range(width // HD):
            cols = slice(h * HD, (h + 1) * HD)
            chosen = jnp.zeros((rows, HD), jnp.float32)
            for s in range(n_frame):
                mask = masks_ref[d * n_frame + s : d * n_frame + s + 1, :]
                chosen = jnp.where(mask > 0.5, slots[s][some, cols].astype(jnp.float32), chosen)
            outs[d][:, cols] = chosen.astype(jnp.bfloat16)


def project_near_kernel(*refs):
    refs, out_ref = refs[:-1], refs[-1]
    parts, weights = refs[: len(refs) // 2], refs[len(refs) // 2 :]
    for start in range(0, out_ref.shape[1], COLUMNS):
        cols = slice(start, start + COLUMNS)
        out_ref[:, cols] = sum(
            jnp.dot(part[...], weight[:, cols], preferred_element_type=jnp.float32)
            for part, weight in zip(parts, weights)
        )


def project_kernel(modulation_ref, near_ref, *refs):
    refs, (out, total_ref, sems) = refs[:-3], refs[-3:]
    parts, weights = refs[: len(refs) // 2], refs[len(refs) // 2 :]
    copies = []
    for i, start in enumerate(range(0, total_ref.shape[1], COLUMNS)):
        cols = slice(start, start + COLUMNS)
        total = near_ref[:, cols] + sum(
            jnp.dot(part[...], weight[:, cols], preferred_element_type=jnp.float32)
            for part, weight in zip(parts, weights)
        )
        total_ref[:, cols] = total * modulation_ref[2:3, cols]
        copies.append(pltpu.make_async_copy(total_ref.at[:, cols], out.at[:, cols], sems.at[i]))
        copies[-1].start()
    for copy in copies:
        copy.wait()


def params(mib):
    return pltpu.CompilerParams(vmem_limit_bytes=mib * MIB)


def cost(flops, moved, exps=0):
    return pl.CostEstimate(flops=flops, bytes_accessed=moved, transcendentals=exps)


def per_device(
    n_frame,
    n_head,
    n_rep,
    latents,
    modulation,
    key_cache,
    value_cache,
    block_worker,
    query_weight,
    key_weight,
    value_weight,
    out_weight,
):
    tokens, model = latents.shape
    n_local = block_worker.shape[0]
    block_rows = tokens // n_local
    width = query_weight.shape[1]
    n_place = n_head * n_rep
    own_rows = tokens // n_place
    tail = TAIL * -(-6 * (width // HD) // TAIL)
    half = jnp.bfloat16

    def along_frame(x, s):
        return lax.ppermute(x, "frame", [(i, i ^ s) for i in range(n_frame)])

    def along_head(x, shift):
        return lax.ppermute(x, "head", [(i, (i + shift) % n_head) for i in range(n_head)])

    def along_rep(x, shift):
        return lax.ppermute(x, "rep", [(i, (i + shift) % n_rep) for i in range(n_rep)])

    def in_frame(x, d):
        pairs = []
        for h in range(n_head):
            for r in range(n_rep):
                to = ((h + d // n_rep) % n_head) * n_rep + (r + d % n_rep) % n_rep
                pairs.append((h * n_rep + r, to))
        return lax.ppermute(x, ("head", "rep"), pairs)

    across = [along_head(out_weight, dh) for dh in range(1, n_head)]

    *slots, normed = pl.pallas_call(
        functools.partial(query_kernel, n_frame),
        out_shape=[jax.ShapeDtypeStruct((block_rows, width), half)] * n_frame
        + [jax.ShapeDtypeStruct(latents.shape, half)],
        in_specs=[HBM] * 4,
        out_specs=[VMEM] * n_frame + [HBM],
        scratch_shapes=[
            pltpu.SMEM(block_worker.shape, jnp.int32),
            pltpu.VMEM(latents.shape, half),
            pltpu.VMEM(modulation.shape, jnp.float32),
            pltpu.VMEM(query_weight.shape, half),
            pltpu.VMEM(latents.shape, half),
            pltpu.VMEM((tokens, width), half),
            pltpu.SemaphoreType.DMA((3 + 2 * n_local,)),
        ],
        compiler_params=params(60),
        cost_estimate=cost(2 * tokens * model * width, 2 * tokens * model + 2 * model * width),
        name="queries",
    )(block_worker, latents, modulation, query_weight)
    arrived = [along_frame(slots[s], s) for s in range(1, n_frame)]

    keys = pl.pallas_call(
        key_kernel,
        out_shape=jax.ShapeDtypeStruct((tokens, width), half),
        in_specs=[HBM] * 4,
        out_specs=VMEM,
        scratch_shapes=[
            pltpu.SMEM(block_worker.shape, jnp.int32),
            pltpu.VMEM(latents.shape, half),
            pltpu.VMEM(key_weight.shape, half),
            pltpu.SemaphoreType.DMA((4,)),
        ],
        compiler_params=params(53),
        cost_estimate=cost(2 * tokens * model * width, 6 * tokens * model),
        name="keys",
    )(block_worker, normed, key_weight, key_cache)

    mine = pl.pallas_call(
        collect_kernel,
        out_shape=jax.ShapeDtypeStruct((block_rows, width), half),
        in_specs=[VMEM] * n_frame + [ANY],
        out_specs=VMEM,
        compiler_params=params(16),
        cost_estimate=cost(n_frame * block_rows * width, 2 * n_frame * block_rows * width),
        name="collect",
    )(slots[0], *arrived, keys)

    values_t, masks = pl.pallas_call(
        functools.partial(value_kernel, n_frame, n_head, n_rep),
        out_shape=[
            jax.ShapeDtypeStruct((width, tokens), half),
            jax.ShapeDtypeStruct((n_place * n_frame, HD), jnp.float32),
        ],
        in_specs=[HBM] * 4 + [ANY],
        out_specs=[VMEM] * 2,
        scratch_shapes=[
            pltpu.SMEM(block_worker.shape, jnp.int32),
            pltpu.VMEM(latents.shape, half),
            pltpu.VMEM(value_weight.shape, half),
            pltpu.VMEM(value_cache.shape, half),
            pltpu.SemaphoreType.DMA((4,)),
        ],
        compiler_params=params(53),
        cost_estimate=cost(2 * tokens * model * width, 6 * tokens * model),
        name="values",
    )(block_worker, normed, value_weight, value_cache, mine)

    def attend(queries, after=()):
        count = len(queries)
        return pl.pallas_call(
            functools.partial(attend_kernel, count),
            out_shape=[jax.ShapeDtypeStruct((width + tail, block_rows), half)] * count,
            in_specs=[VMEM] * (count + 2) + [ANY] * len(after),
            out_specs=[VMEM] * count,
            compiler_params=params(16),
            cost_estimate=cost(
                4 * tokens * block_rows * width * count,
                20 * tokens * width,
                tokens * block_rows * width // HD * count,
            ),
            name="attend",
        )(*queries, keys, values_t, *after)

    near_first = list(range(1, n_frame))
    shared = [along_frame(mine, s) for s in near_first]
    own = list(attend([mine]))
    partial = []
    for start in range(0, n_frame - 1, SLOTS):
        partial += attend(shared[start : start + SLOTS], own)
    sent = [along_frame(x, s) for s, x in zip(near_first, partial)]
    attended = pl.pallas_call(
        combine_kernel,
        out_shape=jax.ShapeDtypeStruct((block_rows, width), half),
        in_specs=[VMEM] * n_frame,
        out_specs=VMEM,
        compiler_params=params(16),
        cost_estimate=cost(4 * n_frame * block_rows * width, 2 * n_frame * block_rows * width),
        name="combine",
    )(*own, *sent)
    copies = {s: along_frame(attended, s) for s in near_first}
    copies = [attended] + [copies[s] for s in range(1, n_frame)]
    pieces = pl.pallas_call(
        functools.partial(select_kernel, n_frame, n_head, n_rep),
        out_shape=[jax.ShapeDtypeStruct((own_rows, width), half)] * n_place
        + [jax.ShapeDtypeStruct(w.shape, w.dtype) for w in across],
        in_specs=[VMEM] * (n_frame + 1) + [ANY] * len(across),
        out_specs=[VMEM] * n_place + [ANY] * len(across),
        input_output_aliases={n_frame + 1 + i: n_place + i for i in range(len(across))},
        compiler_params=params(16),
        cost_estimate=cost(0, 4 * n_frame * block_rows * width),
        name="select",
    )(*copies, masks, *across)
    pieces, across = pieces[:n_place], list(pieces[n_place:])
    moved = {d: in_frame(pieces[d], d) for d in range(n_place - 1, 0, -1)}
    pieces = [pieces[0]] + [moved[d] for d in range(1, n_place)]

    weights = []
    for held in [out_weight] + across:
        weights += [held] + [along_rep(held, dr) for dr in range(1, n_rep)]
    near = pl.pallas_call(
        project_near_kernel,
        out_shape=jax.ShapeDtypeStruct((own_rows, model), jnp.float32),
        in_specs=[VMEM] * (2 * n_rep),
        out_specs=VMEM,
        compiler_params=params(16),
        cost_estimate=cost(2 * own_rows * model * width * n_rep, 4 * model * width * n_rep),
        name="project_near",
    )(*pieces[:n_rep], *weights[:n_rep])
    return pl.pallas_call(
        project_kernel,
        out_shape=jax.ShapeDtypeStruct((own_rows, model), jnp.float32),
        in_specs=[VMEM] * (2 + 2 * (n_place - n_rep)),
        out_specs=ANY,
        scratch_shapes=[
            pltpu.VMEM((own_rows, model), jnp.float32),
            pltpu.SemaphoreType.DMA((-(-model // COLUMNS),)),
        ],
        compiler_params=params(16),
        cost_estimate=cost(2 * own_rows * model * width * n_rep, 2 * model * width * n_place),
        name="project",
    )(modulation, near, *pieces[n_rep:], *weights[n_rep:])


def solution(mesh):
    in_specs = (
        P(("groups", "frame"), None),
        P("groups", None),
        P(("groups", "frame"), ("head", "rep")),
        P(("groups", "frame"), ("head", "rep")),
        P(("groups", "frame")),
        P(None, ("head", "rep")),
        P(None, ("head", "rep")),
        P(None, ("head", "rep")),
        P(("head", "rep"), None),
    )
    out_specs = P(("groups", "frame", "head", "rep"), None)
    body = functools.partial(
        per_device, mesh.shape["frame"], mesh.shape["head"], mesh.shape["rep"]
    )
    return jax.shard_map(body, mesh=mesh, in_specs=in_specs, out_specs=out_specs, check_vma=False)
```

```python
import functools

import jax
import jax.numpy as jnp
from jax import lax
from jax.experimental import pallas as pl
from jax.experimental.pallas import tpu as pltpu
from jax.sharding import PartitionSpec as P

HD = 128
EPS = 1e-06
CHUNK = 16
UNROLL = 4
COLUMNS = 512
SLOTS = 3
TAIL = 16
MIB = 1 << 20

VMEM = pl.BlockSpec(memory_space=pltpu.VMEM)
HBM = pl.BlockSpec(memory_space=pltpu.HBM)
ANY = pl.BlockSpec(memory_space=pl.ANY)


def normalize_block(latents_ref, gain_ref, shift_ref, normed_ref, start, block_rows):
    def one_chunk(c, carry):
        at = pl.multiple_of(start + c * CHUNK, CHUNK)
        floats = latents_ref[pl.ds(at, CHUNK), :].astype(jnp.float32)
        center = floats - jnp.mean(floats, axis=-1, keepdims=True)
        spread = jnp.mean(center * center, axis=-1, keepdims=True)
        normed_ref[pl.ds(at, CHUNK), :] = (
            center * lax.rsqrt(spread + EPS) * gain_ref[...] + shift_ref[...]
        ).astype(jnp.bfloat16)
        return carry

    lax.fori_loop(0, block_rows // CHUNK, one_chunk, 0, unroll=UNROLL)


def query_kernel(n_frame, worker_in, latents_in, modulation_in, weight_in, *rest):
    outs, normed_out = rest[:n_frame], rest[n_frame]
    (
        worker_ref,
        latents_ref,
        modulation_ref,
        weight_ref,
        normed_ref,
        queries_ref,
        gain_ref,
        shift_ref,
        sems,
    ) = rest[n_frame + 1 :]
    n_local = worker_ref.shape[0]
    block_rows = latents_ref.shape[0] // n_local
    frame = lax.axis_index("frame")
    blocks = [slice(j * block_rows, (j + 1) * block_rows) for j in range(n_local)]
    first = [
        pltpu.make_async_copy(worker_in, worker_ref, sems.at[0]),
        pltpu.make_async_copy(modulation_in, modulation_ref, sems.at[1]),
    ]
    each = [
        pltpu.make_async_copy(latents_in.at[rows, :], latents_ref.at[rows, :], sems.at[3 + j])
        for j, rows in enumerate(blocks)
    ]
    back = [
        pltpu.make_async_copy(
            normed_ref.at[rows, :], normed_out.at[rows, :], sems.at[3 + n_local + j]
        )
        for j, rows in enumerate(blocks)
    ]
    weight = pltpu.make_async_copy(weight_in, weight_ref, sems.at[2])
    for copy in first + each + [weight]:
        copy.start()
    for s in range(n_frame):
        outs[s][...] = jnp.zeros_like(outs[s])
    for copy in first:
        copy.wait()
    gain_ref[...] = jnp.broadcast_to(1.0 + modulation_ref[1:2, :], gain_ref.shape)
    shift_ref[...] = jnp.broadcast_to(modulation_ref[0:1, :], shift_ref.shape)
    for j in range(n_local):
        each[j].wait()

        @pl.when(worker_ref[j] >= 0)
        def _():
            normalize_block(
                latents_ref, gain_ref, shift_ref, normed_ref, j * block_rows, block_rows
            )
            back[j].start()

    weight.wait()
    queries_ref[...] = (
        jnp.dot(normed_ref[...], weight_ref[...], preferred_element_type=jnp.float32) * HD ** (-0.5)
    ).astype(jnp.bfloat16)
    for j in range(n_local):
        worker = worker_ref[j]
        for s in range(n_frame):

            @pl.when((worker >= 0) & (jnp.bitwise_xor(frame, s) == worker))
            def _():
                outs[s][...] = queries_ref[blocks[j], :]

        @pl.when(worker >= 0)
        def _():
            back[j].wait()


def key_kernel(
    worker_in, normed_in, weight_in, cache_in, keys_ref, worker_ref, normed_ref, weight_ref, sems
):
    n_local = worker_ref.shape[0]
    block_rows = normed_ref.shape[0] // n_local
    copies = [
        pltpu.make_async_copy(source, target, sems.at[i])
        for i, (source, target) in enumerate(
            [
                (worker_in, worker_ref),
                (normed_in, normed_ref),
                (weight_in, weight_ref),
                (cache_in, keys_ref),
            ]
        )
    ]
    for copy in copies:
        copy.start()
    for copy in copies:
        copy.wait()
    fresh = jnp.dot(
        normed_ref[...], weight_ref[...], preferred_element_type=jnp.float32
    ).astype(jnp.bfloat16)
    for j in range(n_local):
        rows = slice(j * block_rows, (j + 1) * block_rows)

        @pl.when(worker_ref[j] >= 0)
        def _():
            keys_ref[rows, :] = fresh[rows, :]


def value_kernel(
    n_frame,
    n_head,
    n_rep,
    worker_in,
    normed_in,
    weight_in,
    cache_in,
    _,
    values_t_ref,
    masks_ref,
    worker_ref,
    normed_ref,
    weight_ref,
    values_ref,
    sems,
):
    n_local = worker_ref.shape[0]
    tokens = normed_ref.shape[0]
    block_rows = tokens // n_local
    copies = [
        pltpu.make_async_copy(source, target, sems.at[i])
        for i, (source, target) in enumerate(
            [
                (worker_in, worker_ref),
                (normed_in, normed_ref),
                (weight_in, weight_ref),
                (cache_in, values_ref),
            ]
        )
    ]
    for copy in copies:
        copy.start()
    copies[0].wait()
    frame, head, rep = lax.axis_index("frame"), lax.axis_index("head"), lax.axis_index("rep")
    n_place = n_head * n_rep
    for d in range(n_place):
        target = lax.rem(head + d // n_rep, n_head) * n_rep + lax.rem(rep + d % n_rep, n_rep)
        worker = worker_ref[target * (tokens // n_place) // block_rows]
        for s in range(n_frame):
            held = (worker >= 0) & (jnp.bitwise_xor(frame, s) == worker)
            masks_ref[d * n_frame + s : d * n_frame + s + 1, :] = jnp.full(
                (1, masks_ref.shape[1]), jnp.where(held, 1.0, 0.0), jnp.float32
            )
    for copy in copies[1:]:
        copy.wait()
    fresh = jnp.dot(
        normed_ref[...], weight_ref[...], preferred_element_type=jnp.float32
    ).astype(jnp.bfloat16)
    for j in range(n_local):
        rows = slice(j * block_rows, (j + 1) * block_rows)

        @pl.when(worker_ref[j] >= 0)
        def _():
            values_ref[rows, :] = fresh[rows, :]

    for h in range(values_ref.shape[1] // HD):
        cols = slice(h * HD, (h + 1) * HD)
        values_t_ref[cols, :] = values_ref[:, cols].T


def three_terms(x):
    first = x.astype(jnp.bfloat16).astype(jnp.float32)
    rest = x - first
    second = rest.astype(jnp.bfloat16).astype(jnp.float32)
    return [first, second, rest - second]


def collect_kernel(*refs):
    *parts, _, out_ref = refs
    out_ref[...] = sum(part[...].astype(jnp.float32) for part in parts).astype(jnp.bfloat16)


def attend_kernel(count, *refs):
    keys_ref, values_t_ref = refs[count : count + 2]
    for queries_ref, out_ref in zip(refs[:count], refs[-count:]):
        attend_slot(queries_ref, keys_ref, values_t_ref, out_ref)


def attend_slot(queries_ref, keys_ref, values_t_ref, out_ref):
    width = keys_ref.shape[1]
    stats = []
    for h in range(width // HD):
        cols = slice(h * HD, (h + 1) * HD)
        scores = lax.dot_general(
            keys_ref[:, cols],
            queries_ref[:, cols],
            (((1,), (1,)), ((), ())),
            preferred_element_type=jnp.float32,
        )
        highest = jnp.max(scores, axis=0, keepdims=True)
        weights = jnp.exp(scores - highest)
        total = jnp.sum(weights, axis=0, keepdims=True)
        out_ref[cols, :] = jnp.dot(
            values_t_ref[cols, :], weights.astype(jnp.bfloat16), preferred_element_type=jnp.float32
        ).astype(jnp.bfloat16)
        stats += three_terms(highest) + three_terms(total)
    shape = (out_ref.shape[0] - width, out_ref.shape[1])
    row = lax.broadcasted_iota(jnp.int32, shape, 0)
    tail = jnp.zeros(shape, jnp.float32)
    for i, stat in enumerate(stats):
        tail = jnp.where(row == i, stat, tail)
    out_ref[width:, :] = tail.astype(jnp.bfloat16)


def combine_kernel(*refs):
    parts, out_ref = refs[:-1], refs[-1]
    width = out_ref.shape[1]
    tails = [part[width:, :].astype(jnp.float32) for part in parts]
    for h in range(width // HD):
        cols = slice(h * HD, (h + 1) * HD)

        def stat(tail, at):
            at += 6 * h
            return tail[at : at + 1, :] + tail[at + 1 : at + 2, :] + tail[at + 2 : at + 3, :]

        maxima = [stat(tail, 0) for tail in tails]
        highest = functools.reduce(jnp.maximum, maxima)
        factors = [jnp.exp(m - highest) for m in maxima]
        total = sum(stat(tail, 3) * factor for tail, factor in zip(tails, factors))
        summed = sum(
            part[cols, :].astype(jnp.float32) * factor for part, factor in zip(parts, factors)
        )
        out_ref[:, cols] = (summed / total).T.astype(jnp.bfloat16)


def select_kernel(n_frame, n_head, n_rep, *refs):
    slots, masks_ref = refs[:n_frame], refs[n_frame]
    first = len(refs) - (len(refs) - n_frame - 1 - n_head * n_rep) // 2 - n_head * n_rep
    outs = refs[first : first + n_head * n_rep]
    block_rows, width = slots[0].shape
    rows = outs[0].shape[0]
    head, rep = lax.axis_index("head"), lax.axis_index("rep")
    for d in range(n_head * n_rep):
        if rows == block_rows:
            some = slice(None)
        else:
            target = lax.rem(head + d // n_rep, n_head) * n_rep + lax.rem(rep + d % n_rep, n_rep)
            some = pl.ds(pl.multiple_of(lax.rem(target * rows, block_rows), rows), rows)
        for h in range(width // HD):
            cols = slice(h * HD, (h + 1) * HD)
            chosen = jnp.zeros((rows, HD), jnp.float32)
            for s in range(n_frame):
                mask = masks_ref[d * n_frame + s : d * n_frame + s + 1, :]
                chosen = jnp.where(mask > 0.5, slots[s][some, cols].astype(jnp.float32), chosen)
            outs[d][:, cols] = chosen.astype(jnp.bfloat16)


def project_near_kernel(*refs):
    refs, out_ref = refs[:-1], refs[-1]
    parts, weights = refs[: len(refs) // 2], refs[len(refs) // 2 :]
    for start in range(0, out_ref.shape[1], COLUMNS):
        cols = slice(start, start + COLUMNS)
        out_ref[:, cols] = sum(
            jnp.dot(part[...], weight[:, cols], preferred_element_type=jnp.float32)
            for part, weight in zip(parts, weights)
        )


def project_kernel(modulation_ref, near_ref, *refs):
    refs, (out, total_ref, sems) = refs[:-3], refs[-3:]
    parts, weights = refs[: len(refs) // 2], refs[len(refs) // 2 :]
    copies = []
    for i, start in enumerate(range(0, total_ref.shape[1], COLUMNS)):
        cols = slice(start, start + COLUMNS)
        total = near_ref[:, cols] + sum(
            jnp.dot(part[...], weight[:, cols], preferred_element_type=jnp.float32)
            for part, weight in zip(parts, weights)
        )
        total_ref[:, cols] = total * modulation_ref[2:3, cols]
        copies.append(pltpu.make_async_copy(total_ref.at[:, cols], out.at[:, cols], sems.at[i]))
        copies[-1].start()
    for copy in copies:
        copy.wait()


def params(mib):
    return pltpu.CompilerParams(vmem_limit_bytes=mib * MIB)


def cost(flops, moved, exps=0):
    return pl.CostEstimate(flops=flops, bytes_accessed=moved, transcendentals=exps)


def per_device(
    n_frame,
    n_head,
    n_rep,
    latents,
    modulation,
    key_cache,
    value_cache,
    block_worker,
    query_weight,
    key_weight,
    value_weight,
    out_weight,
):
    tokens, model = latents.shape
    n_local = block_worker.shape[0]
    block_rows = tokens // n_local
    width = query_weight.shape[1]
    n_place = n_head * n_rep
    own_rows = tokens // n_place
    tail = TAIL * -(-6 * (width // HD) // TAIL)
    half = jnp.bfloat16

    def along_frame(x, s):
        return lax.ppermute(x, "frame", [(i, i ^ s) for i in range(n_frame)])

    def along_head(x, shift):
        return lax.ppermute(x, "head", [(i, (i + shift) % n_head) for i in range(n_head)])

    def along_rep(x, shift):
        return lax.ppermute(x, "rep", [(i, (i + shift) % n_rep) for i in range(n_rep)])

    def in_frame(x, d):
        pairs = []
        for h in range(n_head):
            for r in range(n_rep):
                to = ((h + d // n_rep) % n_head) * n_rep + (r + d % n_rep) % n_rep
                pairs.append((h * n_rep + r, to))
        return lax.ppermute(x, ("head", "rep"), pairs)

    across = [along_head(out_weight, dh) for dh in range(1, n_head)]

    *slots, normed = pl.pallas_call(
        functools.partial(query_kernel, n_frame),
        out_shape=[jax.ShapeDtypeStruct((block_rows, width), half)] * n_frame
        + [jax.ShapeDtypeStruct(latents.shape, half)],
        in_specs=[HBM] * 4,
        out_specs=[VMEM] * n_frame + [HBM],
        scratch_shapes=[
            pltpu.SMEM(block_worker.shape, jnp.int32),
            pltpu.VMEM(latents.shape, half),
            pltpu.VMEM(modulation.shape, jnp.float32),
            pltpu.VMEM(query_weight.shape, half),
            pltpu.VMEM(latents.shape, half),
            pltpu.VMEM((tokens, width), half),
            pltpu.VMEM((CHUNK, model), jnp.float32),
            pltpu.VMEM((CHUNK, model), jnp.float32),
            pltpu.SemaphoreType.DMA((3 + 2 * n_local,)),
        ],
        compiler_params=params(60),
        cost_estimate=cost(2 * tokens * model * width, 2 * tokens * model + 2 * model * width),
        name="queries",
    )(block_worker, latents, modulation, query_weight)
    arrived = [along_frame(slots[s], s) for s in range(n_frame - 1, 0, -1)]

    keys = pl.pallas_call(
        key_kernel,
        out_shape=jax.ShapeDtypeStruct((tokens, width), half),
        in_specs=[HBM] * 4,
        out_specs=VMEM,
        scratch_shapes=[
            pltpu.SMEM(block_worker.shape, jnp.int32),
            pltpu.VMEM(latents.shape, half),
            pltpu.VMEM(key_weight.shape, half),
            pltpu.SemaphoreType.DMA((4,)),
        ],
        compiler_params=params(53),
        cost_estimate=cost(2 * tokens * model * width, 6 * tokens * model),
        name="keys",
    )(block_worker, normed, key_weight, key_cache)

    mine = pl.pallas_call(
        collect_kernel,
        out_shape=jax.ShapeDtypeStruct((block_rows, width), half),
        in_specs=[VMEM] * n_frame + [ANY],
        out_specs=VMEM,
        compiler_params=params(16),
        cost_estimate=cost(n_frame * block_rows * width, 2 * n_frame * block_rows * width),
        name="collect",
    )(slots[0], *arrived, keys)

    values_t, masks = pl.pallas_call(
        functools.partial(value_kernel, n_frame, n_head, n_rep),
        out_shape=[
            jax.ShapeDtypeStruct((width, tokens), half),
            jax.ShapeDtypeStruct((n_place * n_frame, HD), jnp.float32),
        ],
        in_specs=[HBM] * 4 + [ANY],
        out_specs=[VMEM] * 2,
        scratch_shapes=[
            pltpu.SMEM(block_worker.shape, jnp.int32),
            pltpu.VMEM(latents.shape, half),
            pltpu.VMEM(value_weight.shape, half),
            pltpu.VMEM(value_cache.shape, half),
            pltpu.SemaphoreType.DMA((4,)),
        ],
        compiler_params=params(53),
        cost_estimate=cost(2 * tokens * model * width, 6 * tokens * model),
        name="values",
    )(block_worker, normed, value_weight, value_cache, mine)

    def attend(queries, after=()):
        count = len(queries)
        return pl.pallas_call(
            functools.partial(attend_kernel, count),
            out_shape=[jax.ShapeDtypeStruct((width + tail, block_rows), half)] * count,
            in_specs=[VMEM] * (count + 2) + [ANY] * len(after),
            out_specs=[VMEM] * count,
            compiler_params=params(16),
            cost_estimate=cost(
                4 * tokens * block_rows * width * count,
                20 * tokens * width,
                tokens * block_rows * width // HD * count,
            ),
            name="attend",
        )(*queries, keys, values_t, *after)

    far_first = list(range(n_frame - 1, 0, -1))
    shared = [along_frame(mine, s) for s in far_first]
    own = list(attend([mine]))
    partial = []
    for start in range(0, n_frame - 1, SLOTS):
        partial += attend(shared[start : start + SLOTS], own)
    sent = [along_frame(x, s) for s, x in zip(far_first, partial)]
    attended = pl.pallas_call(
        combine_kernel,
        out_shape=jax.ShapeDtypeStruct((block_rows, width), half),
        in_specs=[VMEM] * n_frame,
        out_specs=VMEM,
        compiler_params=params(16),
        cost_estimate=cost(4 * n_frame * block_rows * width, 2 * n_frame * block_rows * width),
        name="combine",
    )(*own, *sent)
    copies = {s: along_frame(attended, s) for s in far_first}
    copies = [attended] + [copies[s] for s in range(1, n_frame)]
    pieces = pl.pallas_call(
        functools.partial(select_kernel, n_frame, n_head, n_rep),
        out_shape=[jax.ShapeDtypeStruct((own_rows, width), half)] * n_place
        + [jax.ShapeDtypeStruct(w.shape, w.dtype) for w in across],
        in_specs=[VMEM] * (n_frame + 1) + [ANY] * len(across),
        out_specs=[VMEM] * n_place + [ANY] * len(across),
        input_output_aliases={n_frame + 1 + i: n_place + i for i in range(len(across))},
        compiler_params=params(16),
        cost_estimate=cost(0, 4 * n_frame * block_rows * width),
        name="select",
    )(*copies, masks, *across)
    pieces, across = pieces[:n_place], list(pieces[n_place:])
    moved = {d: in_frame(pieces[d], d) for d in range(n_place - 1, 0, -1)}
    pieces = [pieces[0]] + [moved[d] for d in range(1, n_place)]

    weights = []
    for held in [out_weight] + across:
        weights += [held] + [along_rep(held, dr) for dr in range(1, n_rep)]
    near = pl.pallas_call(
        project_near_kernel,
        out_shape=jax.ShapeDtypeStruct((own_rows, model), jnp.float32),
        in_specs=[VMEM] * (2 * n_rep),
        out_specs=VMEM,
        compiler_params=params(16),
        cost_estimate=cost(2 * own_rows * model * width * n_rep, 4 * model * width * n_rep),
        name="project_near",
    )(*pieces[:n_rep], *weights[:n_rep])
    return pl.pallas_call(
        project_kernel,
        out_shape=jax.ShapeDtypeStruct((own_rows, model), jnp.float32),
        in_specs=[VMEM] * (2 + 2 * (n_place - n_rep)),
        out_specs=ANY,
        scratch_shapes=[
            pltpu.VMEM((own_rows, model), jnp.float32),
            pltpu.SemaphoreType.DMA((-(-model // COLUMNS),)),
        ],
        compiler_params=params(16),
        cost_estimate=cost(2 * own_rows * model * width * n_rep, 2 * model * width * n_place),
        name="project",
    )(modulation, near, *pieces[n_rep:], *weights[n_rep:])


def solution(mesh):
    in_specs = (
        P(("groups", "frame"), None),
        P("groups", None),
        P(("groups", "frame"), ("head", "rep")),
        P(("groups", "frame"), ("head", "rep")),
        P(("groups", "frame")),
        P(None, ("head", "rep")),
        P(None, ("head", "rep")),
        P(None, ("head", "rep")),
        P(("head", "rep"), None),
    )
    out_specs = P(("groups", "frame", "head", "rep"), None)
    body = functools.partial(
        per_device, mesh.shape["frame"], mesh.shape["head"], mesh.shape["rep"]
    )
    return jax.shard_map(body, mesh=mesh, in_specs=in_specs, out_specs=out_specs, check_vma=False)
```

```python
import functools

import jax
import jax.numpy as jnp
from jax import lax
from jax.experimental import pallas as pl
from jax.experimental.pallas import tpu as pltpu
from jax.sharding import PartitionSpec as P

HD = 128
EPS = 1e-06
CHUNK = 16
UNROLL = 8
COLUMNS = 512
SLOTS = 3
TAIL = 16
MIB = 1 << 20

VMEM = pl.BlockSpec(memory_space=pltpu.VMEM)
HBM = pl.BlockSpec(memory_space=pltpu.HBM)
ANY = pl.BlockSpec(memory_space=pl.ANY)


def normalize_block(latents_ref, gain_ref, shift_ref, normed_ref, start, block_rows):
    def one_chunk(c, carry):
        at = pl.multiple_of(start + c * CHUNK, CHUNK)
        floats = latents_ref[pl.ds(at, CHUNK), :].astype(jnp.float32)
        center = floats - jnp.mean(floats, axis=-1, keepdims=True)
        spread = jnp.mean(center * center, axis=-1, keepdims=True)
        normed_ref[pl.ds(at, CHUNK), :] = (
            center * lax.rsqrt(spread + EPS) * gain_ref[...] + shift_ref[...]
        ).astype(jnp.bfloat16)
        return carry

    lax.fori_loop(0, block_rows // CHUNK, one_chunk, 0, unroll=UNROLL)


def query_kernel(n_frame, worker_in, latents_in, modulation_in, weight_in, *rest):
    outs, normed_out = rest[:n_frame], rest[n_frame]
    (
        worker_ref,
        latents_ref,
        modulation_ref,
        weight_ref,
        normed_ref,
        queries_ref,
        gain_ref,
        shift_ref,
        sems,
    ) = rest[n_frame + 1 :]
    n_local = worker_ref.shape[0]
    block_rows = latents_ref.shape[0] // n_local
    frame = lax.axis_index("frame")
    blocks = [slice(j * block_rows, (j + 1) * block_rows) for j in range(n_local)]
    first = [
        pltpu.make_async_copy(worker_in, worker_ref, sems.at[0]),
        pltpu.make_async_copy(modulation_in, modulation_ref, sems.at[1]),
    ]
    each = [
        pltpu.make_async_copy(latents_in.at[rows, :], latents_ref.at[rows, :], sems.at[3 + j])
        for j, rows in enumerate(blocks)
    ]
    back = [
        pltpu.make_async_copy(
            normed_ref.at[rows, :], normed_out.at[rows, :], sems.at[3 + n_local + j]
        )
        for j, rows in enumerate(blocks)
    ]
    weight = pltpu.make_async_copy(weight_in, weight_ref, sems.at[2])
    for copy in first + each + [weight]:
        copy.start()
    for s in range(n_frame):
        outs[s][...] = jnp.zeros_like(outs[s])
    for copy in first:
        copy.wait()
    gain_ref[...] = jnp.broadcast_to(1.0 + modulation_ref[1:2, :], gain_ref.shape)
    shift_ref[...] = jnp.broadcast_to(modulation_ref[0:1, :], shift_ref.shape)
    for j in range(n_local):
        each[j].wait()

        @pl.when(worker_ref[j] >= 0)
        def _():
            normalize_block(
                latents_ref, gain_ref, shift_ref, normed_ref, j * block_rows, block_rows
            )
            back[j].start()

    weight.wait()
    queries_ref[...] = (
        jnp.dot(normed_ref[...], weight_ref[...], preferred_element_type=jnp.float32) * HD ** (-0.5)
    ).astype(jnp.bfloat16)
    for j in range(n_local):
        worker = worker_ref[j]
        for s in range(n_frame):

            @pl.when((worker >= 0) & (jnp.bitwise_xor(frame, s) == worker))
            def _():
                outs[s][...] = queries_ref[blocks[j], :]

        @pl.when(worker >= 0)
        def _():
            back[j].wait()


def key_kernel(
    worker_in, normed_in, weight_in, cache_in, keys_ref, worker_ref, normed_ref, weight_ref, sems
):
    n_local = worker_ref.shape[0]
    block_rows = normed_ref.shape[0] // n_local
    copies = [
        pltpu.make_async_copy(source, target, sems.at[i])
        for i, (source, target) in enumerate(
            [
                (worker_in, worker_ref),
                (normed_in, normed_ref),
                (weight_in, weight_ref),
                (cache_in, keys_ref),
            ]
        )
    ]
    for copy in copies:
        copy.start()
    for copy in copies:
        copy.wait()
    fresh = jnp.dot(
        normed_ref[...], weight_ref[...], preferred_element_type=jnp.float32
    ).astype(jnp.bfloat16)
    for j in range(n_local):
        rows = slice(j * block_rows, (j + 1) * block_rows)

        @pl.when(worker_ref[j] >= 0)
        def _():
            keys_ref[rows, :] = fresh[rows, :]


def value_kernel(
    n_frame,
    n_head,
    n_rep,
    worker_in,
    normed_in,
    weight_in,
    cache_in,
    _,
    values_t_ref,
    masks_ref,
    worker_ref,
    normed_ref,
    weight_ref,
    values_ref,
    sems,
):
    n_local = worker_ref.shape[0]
    tokens = normed_ref.shape[0]
    block_rows = tokens // n_local
    copies = [
        pltpu.make_async_copy(source, target, sems.at[i])
        for i, (source, target) in enumerate(
            [
                (worker_in, worker_ref),
                (normed_in, normed_ref),
                (weight_in, weight_ref),
                (cache_in, values_ref),
            ]
        )
    ]
    for copy in copies:
        copy.start()
    copies[0].wait()
    frame, head, rep = lax.axis_index("frame"), lax.axis_index("head"), lax.axis_index("rep")
    n_place = n_head * n_rep
    for d in range(n_place):
        target = lax.rem(head + d // n_rep, n_head) * n_rep + lax.rem(rep + d % n_rep, n_rep)
        worker = worker_ref[target * (tokens // n_place) // block_rows]
        for s in range(n_frame):
            held = (worker >= 0) & (jnp.bitwise_xor(frame, s) == worker)
            masks_ref[d * n_frame + s : d * n_frame + s + 1, :] = jnp.full(
                (1, masks_ref.shape[1]), jnp.where(held, 1.0, 0.0), jnp.float32
            )
    for copy in copies[1:]:
        copy.wait()
    fresh = jnp.dot(
        normed_ref[...], weight_ref[...], preferred_element_type=jnp.float32
    ).astype(jnp.bfloat16)
    for j in range(n_local):
        rows = slice(j * block_rows, (j + 1) * block_rows)

        @pl.when(worker_ref[j] >= 0)
        def _():
            values_ref[rows, :] = fresh[rows, :]

    for h in range(values_ref.shape[1] // HD):
        cols = slice(h * HD, (h + 1) * HD)
        values_t_ref[cols, :] = values_ref[:, cols].T


def three_terms(x):
    first = x.astype(jnp.bfloat16).astype(jnp.float32)
    rest = x - first
    second = rest.astype(jnp.bfloat16).astype(jnp.float32)
    return [first, second, rest - second]


def collect_kernel(*refs):
    *parts, _, out_ref = refs
    out_ref[...] = sum(part[...].astype(jnp.float32) for part in parts).astype(jnp.bfloat16)


def attend_kernel(count, *refs):
    keys_ref, values_t_ref = refs[count : count + 2]
    for queries_ref, out_ref in zip(refs[:count], refs[-count:]):
        attend_slot(queries_ref, keys_ref, values_t_ref, out_ref)


def attend_slot(queries_ref, keys_ref, values_t_ref, out_ref):
    width = keys_ref.shape[1]
    stats = []
    for h in range(width // HD):
        cols = slice(h * HD, (h + 1) * HD)
        scores = lax.dot_general(
            keys_ref[:, cols],
            queries_ref[:, cols],
            (((1,), (1,)), ((), ())),
            preferred_element_type=jnp.float32,
        )
        highest = jnp.max(scores, axis=0, keepdims=True)
        weights = jnp.exp(scores - highest)
        total = jnp.sum(weights, axis=0, keepdims=True)
        out_ref[cols, :] = jnp.dot(
            values_t_ref[cols, :], weights.astype(jnp.bfloat16), preferred_element_type=jnp.float32
        ).astype(jnp.bfloat16)
        stats += three_terms(highest) + three_terms(total)
    shape = (out_ref.shape[0] - width, out_ref.shape[1])
    row = lax.broadcasted_iota(jnp.int32, shape, 0)
    tail = jnp.zeros(shape, jnp.float32)
    for i, stat in enumerate(stats):
        tail = jnp.where(row == i, stat, tail)
    out_ref[width:, :] = tail.astype(jnp.bfloat16)


def combine_kernel(*refs):
    parts, out_ref = refs[:-1], refs[-1]
    width = out_ref.shape[1]
    tails = [part[width:, :].astype(jnp.float32) for part in parts]
    for h in range(width // HD):
        cols = slice(h * HD, (h + 1) * HD)

        def stat(tail, at):
            at += 6 * h
            return tail[at : at + 1, :] + tail[at + 1 : at + 2, :] + tail[at + 2 : at + 3, :]

        maxima = [stat(tail, 0) for tail in tails]
        highest = functools.reduce(jnp.maximum, maxima)
        factors = [jnp.exp(m - highest) for m in maxima]
        total = sum(stat(tail, 3) * factor for tail, factor in zip(tails, factors))
        summed = sum(
            part[cols, :].astype(jnp.float32) * factor for part, factor in zip(parts, factors)
        )
        out_ref[:, cols] = (summed / total).T.astype(jnp.bfloat16)


def select_kernel(n_frame, n_head, n_rep, *refs):
    slots, masks_ref = refs[:n_frame], refs[n_frame]
    first = len(refs) - (len(refs) - n_frame - 1 - n_head * n_rep) // 2 - n_head * n_rep
    outs = refs[first : first + n_head * n_rep]
    block_rows, width = slots[0].shape
    rows = outs[0].shape[0]
    head, rep = lax.axis_index("head"), lax.axis_index("rep")
    for d in range(n_head * n_rep):
        if rows == block_rows:
            some = slice(None)
        else:
            target = lax.rem(head + d // n_rep, n_head) * n_rep + lax.rem(rep + d % n_rep, n_rep)
            some = pl.ds(pl.multiple_of(lax.rem(target * rows, block_rows), rows), rows)
        for h in range(width // HD):
            cols = slice(h * HD, (h + 1) * HD)
            chosen = jnp.zeros((rows, HD), jnp.float32)
            for s in range(n_frame):
                mask = masks_ref[d * n_frame + s : d * n_frame + s + 1, :]
                chosen = jnp.where(mask > 0.5, slots[s][some, cols].astype(jnp.float32), chosen)
            outs[d][:, cols] = chosen.astype(jnp.bfloat16)


def project_near_kernel(*refs):
    refs, out_ref = refs[:-1], refs[-1]
    parts, weights = refs[: len(refs) // 2], refs[len(refs) // 2 :]
    for start in range(0, out_ref.shape[1], COLUMNS):
        cols = slice(start, start + COLUMNS)
        out_ref[:, cols] = sum(
            jnp.dot(part[...], weight[:, cols], preferred_element_type=jnp.float32)
            for part, weight in zip(parts, weights)
        )


def project_kernel(modulation_ref, near_ref, *refs):
    refs, (out, total_ref, sems) = refs[:-3], refs[-3:]
    parts, weights = refs[: len(refs) // 2], refs[len(refs) // 2 :]
    copies = []
    for i, start in enumerate(range(0, total_ref.shape[1], COLUMNS)):
        cols = slice(start, start + COLUMNS)
        total = near_ref[:, cols] + sum(
            jnp.dot(part[...], weight[:, cols], preferred_element_type=jnp.float32)
            for part, weight in zip(parts, weights)
        )
        total_ref[:, cols] = total * modulation_ref[2:3, cols]
        copies.append(pltpu.make_async_copy(total_ref.at[:, cols], out.at[:, cols], sems.at[i]))
        copies[-1].start()
    for copy in copies:
        copy.wait()


def params(mib):
    return pltpu.CompilerParams(vmem_limit_bytes=mib * MIB)


def cost(flops, moved, exps=0):
    return pl.CostEstimate(flops=flops, bytes_accessed=moved, transcendentals=exps)


def per_device(
    n_frame,
    n_head,
    n_rep,
    latents,
    modulation,
    key_cache,
    value_cache,
    block_worker,
    query_weight,
    key_weight,
    value_weight,
    out_weight,
):
    tokens, model = latents.shape
    n_local = block_worker.shape[0]
    block_rows = tokens // n_local
    width = query_weight.shape[1]
    n_place = n_head * n_rep
    own_rows = tokens // n_place
    tail = TAIL * -(-6 * (width // HD) // TAIL)
    half = jnp.bfloat16

    def along_frame(x, s):
        return lax.ppermute(x, "frame", [(i, i ^ s) for i in range(n_frame)])

    def along_head(x, shift):
        return lax.ppermute(x, "head", [(i, (i + shift) % n_head) for i in range(n_head)])

    def along_rep(x, shift):
        return lax.ppermute(x, "rep", [(i, (i + shift) % n_rep) for i in range(n_rep)])

    def in_frame(x, d):
        pairs = []
        for h in range(n_head):
            for r in range(n_rep):
                to = ((h + d // n_rep) % n_head) * n_rep + (r + d % n_rep) % n_rep
                pairs.append((h * n_rep + r, to))
        return lax.ppermute(x, ("head", "rep"), pairs)

    across = [along_head(out_weight, dh) for dh in range(1, n_head)]

    *slots, normed = pl.pallas_call(
        functools.partial(query_kernel, n_frame),
        out_shape=[jax.ShapeDtypeStruct((block_rows, width), half)] * n_frame
        + [jax.ShapeDtypeStruct(latents.shape, half)],
        in_specs=[HBM] * 4,
        out_specs=[VMEM] * n_frame + [HBM],
        scratch_shapes=[
            pltpu.SMEM(block_worker.shape, jnp.int32),
            pltpu.VMEM(latents.shape, half),
            pltpu.VMEM(modulation.shape, jnp.float32),
            pltpu.VMEM(query_weight.shape, half),
            pltpu.VMEM(latents.shape, half),
            pltpu.VMEM((tokens, width), half),
            pltpu.VMEM((CHUNK, model), jnp.float32),
            pltpu.VMEM((CHUNK, model), jnp.float32),
            pltpu.SemaphoreType.DMA((3 + 2 * n_local,)),
        ],
        compiler_params=params(60),
        cost_estimate=cost(2 * tokens * model * width, 2 * tokens * model + 2 * model * width),
        name="queries",
    )(block_worker, latents, modulation, query_weight)
    arrived = [along_frame(slots[s], s) for s in range(n_frame - 1, 0, -1)]

    keys = pl.pallas_call(
        key_kernel,
        out_shape=jax.ShapeDtypeStruct((tokens, width), half),
        in_specs=[HBM] * 4,
        out_specs=VMEM,
        scratch_shapes=[
            pltpu.SMEM(block_worker.shape, jnp.int32),
            pltpu.VMEM(latents.shape, half),
            pltpu.VMEM(key_weight.shape, half),
            pltpu.SemaphoreType.DMA((4,)),
        ],
        compiler_params=params(53),
        cost_estimate=cost(2 * tokens * model * width, 6 * tokens * model),
        name="keys",
    )(block_worker, normed, key_weight, key_cache)

    mine = pl.pallas_call(
        collect_kernel,
        out_shape=jax.ShapeDtypeStruct((block_rows, width), half),
        in_specs=[VMEM] * n_frame + [ANY],
        out_specs=VMEM,
        compiler_params=params(16),
        cost_estimate=cost(n_frame * block_rows * width, 2 * n_frame * block_rows * width),
        name="collect",
    )(slots[0], *arrived, keys)

    values_t, masks = pl.pallas_call(
        functools.partial(value_kernel, n_frame, n_head, n_rep),
        out_shape=[
            jax.ShapeDtypeStruct((width, tokens), half),
            jax.ShapeDtypeStruct((n_place * n_frame, HD), jnp.float32),
        ],
        in_specs=[HBM] * 4 + [ANY],
        out_specs=[VMEM] * 2,
        scratch_shapes=[
            pltpu.SMEM(block_worker.shape, jnp.int32),
            pltpu.VMEM(latents.shape, half),
            pltpu.VMEM(value_weight.shape, half),
            pltpu.VMEM(value_cache.shape, half),
            pltpu.SemaphoreType.DMA((4,)),
        ],
        compiler_params=params(53),
        cost_estimate=cost(2 * tokens * model * width, 6 * tokens * model),
        name="values",
    )(block_worker, normed, value_weight, value_cache, mine)

    def attend(queries, after=()):
        count = len(queries)
        return pl.pallas_call(
            functools.partial(attend_kernel, count),
            out_shape=[jax.ShapeDtypeStruct((width + tail, block_rows), half)] * count,
            in_specs=[VMEM] * (count + 2) + [ANY] * len(after),
            out_specs=[VMEM] * count,
            compiler_params=params(16),
            cost_estimate=cost(
                4 * tokens * block_rows * width * count,
                20 * tokens * width,
                tokens * block_rows * width // HD * count,
            ),
            name="attend",
        )(*queries, keys, values_t, *after)

    far_first = list(range(n_frame - 1, 0, -1))
    shared = [along_frame(mine, s) for s in far_first]
    own = list(attend([mine]))
    partial = []
    for start in range(0, n_frame - 1, SLOTS):
        partial += attend(shared[start : start + SLOTS], own)
    sent = [along_frame(x, s) for s, x in zip(far_first, partial)]
    attended = pl.pallas_call(
        combine_kernel,
        out_shape=jax.ShapeDtypeStruct((block_rows, width), half),
        in_specs=[VMEM] * n_frame,
        out_specs=VMEM,
        compiler_params=params(16),
        cost_estimate=cost(4 * n_frame * block_rows * width, 2 * n_frame * block_rows * width),
        name="combine",
    )(*own, *sent)
    copies = {s: along_frame(attended, s) for s in far_first}
    copies = [attended] + [copies[s] for s in range(1, n_frame)]
    pieces = pl.pallas_call(
        functools.partial(select_kernel, n_frame, n_head, n_rep),
        out_shape=[jax.ShapeDtypeStruct((own_rows, width), half)] * n_place
        + [jax.ShapeDtypeStruct(w.shape, w.dtype) for w in across],
        in_specs=[VMEM] * (n_frame + 1) + [ANY] * len(across),
        out_specs=[VMEM] * n_place + [ANY] * len(across),
        input_output_aliases={n_frame + 1 + i: n_place + i for i in range(len(across))},
        compiler_params=params(16),
        cost_estimate=cost(0, 4 * n_frame * block_rows * width),
        name="select",
    )(*copies, masks, *across)
    pieces, across = pieces[:n_place], list(pieces[n_place:])
    moved = {d: in_frame(pieces[d], d) for d in range(n_place - 1, 0, -1)}
    pieces = [pieces[0]] + [moved[d] for d in range(1, n_place)]

    weights = []
    for held in [out_weight] + across:
        weights += [held] + [along_rep(held, dr) for dr in range(1, n_rep)]
    near = pl.pallas_call(
        project_near_kernel,
        out_shape=jax.ShapeDtypeStruct((own_rows, model), jnp.float32),
        in_specs=[VMEM] * (2 * n_rep),
        out_specs=VMEM,
        compiler_params=params(16),
        cost_estimate=cost(2 * own_rows * model * width * n_rep, 4 * model * width * n_rep),
        name="project_near",
    )(*pieces[:n_rep], *weights[:n_rep])
    return pl.pallas_call(
        project_kernel,
        out_shape=jax.ShapeDtypeStruct((own_rows, model), jnp.float32),
        in_specs=[VMEM] * (2 + 2 * (n_place - n_rep)),
        out_specs=ANY,
        scratch_shapes=[
            pltpu.VMEM((own_rows, model), jnp.float32),
            pltpu.SemaphoreType.DMA((-(-model // COLUMNS),)),
        ],
        compiler_params=params(16),
        cost_estimate=cost(2 * own_rows * model * width * n_rep, 2 * model * width * n_place),
        name="project",
    )(modulation, near, *pieces[n_rep:], *weights[n_rep:])


def solution(mesh):
    in_specs = (
        P(("groups", "frame"), None),
        P("groups", None),
        P(("groups", "frame"), ("head", "rep")),
        P(("groups", "frame"), ("head", "rep")),
        P(("groups", "frame")),
        P(None, ("head", "rep")),
        P(None, ("head", "rep")),
        P(None, ("head", "rep")),
        P(("head", "rep"), None),
    )
    out_specs = P(("groups", "frame", "head", "rep"), None)
    body = functools.partial(
        per_device, mesh.shape["frame"], mesh.shape["head"], mesh.shape["rep"]
    )
    return jax.shard_map(body, mesh=mesh, in_specs=in_specs, out_specs=out_specs, check_vma=False)
```

```python
import functools

import jax
import jax.numpy as jnp
from jax import lax
from jax.experimental import pallas as pl
from jax.experimental.pallas import tpu as pltpu
from jax.sharding import PartitionSpec as P

HD = 128
EPS = 1e-06
CHUNK = 16
UNROLL = 8
COLUMNS = 512
SLOTS = 3
TAIL = 16
MIB = 1 << 20

VMEM = pl.BlockSpec(memory_space=pltpu.VMEM)
HBM = pl.BlockSpec(memory_space=pltpu.HBM)
ANY = pl.BlockSpec(memory_space=pl.ANY)


def normalize_block(latents_ref, gain_ref, shift_ref, normed_ref, start, block_rows):
    def one_chunk(c, carry):
        at = pl.multiple_of(start + c * CHUNK, CHUNK)
        floats = latents_ref[pl.ds(at, CHUNK), :].astype(jnp.float32)
        center = floats - jnp.mean(floats, axis=-1, keepdims=True)
        spread = jnp.mean(center * center, axis=-1, keepdims=True)
        normed_ref[pl.ds(at, CHUNK), :] = (
            center * lax.rsqrt(spread + EPS) * gain_ref[...] + shift_ref[...]
        ).astype(jnp.bfloat16)
        return carry

    lax.fori_loop(0, block_rows // CHUNK, one_chunk, 0, unroll=UNROLL)


def query_kernel(n_frame, worker_in, latents_in, modulation_in, weight_in, *rest):
    outs, normed_out = rest[:n_frame], rest[n_frame]
    (
        worker_ref,
        latents_ref,
        modulation_ref,
        weight_ref,
        normed_ref,
        queries_ref,
        gain_ref,
        shift_ref,
        sems,
    ) = rest[n_frame + 1 :]
    n_local = worker_ref.shape[0]
    block_rows = latents_ref.shape[0] // n_local
    frame = lax.axis_index("frame")
    blocks = [slice(j * block_rows, (j + 1) * block_rows) for j in range(n_local)]
    first = [
        pltpu.make_async_copy(worker_in, worker_ref, sems.at[0]),
        pltpu.make_async_copy(modulation_in, modulation_ref, sems.at[1]),
    ]
    each = [
        pltpu.make_async_copy(latents_in.at[rows, :], latents_ref.at[rows, :], sems.at[3 + j])
        for j, rows in enumerate(blocks)
    ]
    back = [
        pltpu.make_async_copy(
            normed_ref.at[rows, :], normed_out.at[rows, :], sems.at[3 + n_local + j]
        )
        for j, rows in enumerate(blocks)
    ]
    weight = pltpu.make_async_copy(weight_in, weight_ref, sems.at[2])
    for copy in first + each + [weight]:
        copy.start()
    for s in range(n_frame):
        outs[s][...] = jnp.zeros_like(outs[s])
    for copy in first:
        copy.wait()
    gain_ref[...] = jnp.broadcast_to(1.0 + modulation_ref[1:2, :], gain_ref.shape)
    shift_ref[...] = jnp.broadcast_to(modulation_ref[0:1, :], shift_ref.shape)
    for j in range(n_local):
        each[j].wait()

        @pl.when(worker_ref[j] >= 0)
        def _():
            normalize_block(
                latents_ref, gain_ref, shift_ref, normed_ref, j * block_rows, block_rows
            )
            back[j].start()

    weight.wait()

    @pl.when(functools.reduce(jnp.maximum, [worker_ref[j] for j in range(n_local)]) >= 0)
    def _():
        queries_ref[...] = (
            jnp.dot(normed_ref[...], weight_ref[...], preferred_element_type=jnp.float32)
            * HD ** (-0.5)
        ).astype(jnp.bfloat16)

    for j in range(n_local):
        worker = worker_ref[j]
        for s in range(n_frame):

            @pl.when((worker >= 0) & (jnp.bitwise_xor(frame, s) == worker))
            def _():
                outs[s][...] = queries_ref[blocks[j], :]

        @pl.when(worker >= 0)
        def _():
            back[j].wait()


def key_kernel(
    worker_in, normed_in, weight_in, cache_in, keys_ref, worker_ref, normed_ref, weight_ref, sems
):
    n_local = worker_ref.shape[0]
    block_rows = normed_ref.shape[0] // n_local
    copies = [
        pltpu.make_async_copy(source, target, sems.at[i])
        for i, (source, target) in enumerate(
            [
                (worker_in, worker_ref),
                (normed_in, normed_ref),
                (weight_in, weight_ref),
                (cache_in, keys_ref),
            ]
        )
    ]
    for copy in copies:
        copy.start()
    for copy in copies:
        copy.wait()
    fresh = jnp.dot(
        normed_ref[...], weight_ref[...], preferred_element_type=jnp.float32
    ).astype(jnp.bfloat16)
    for j in range(n_local):
        rows = slice(j * block_rows, (j + 1) * block_rows)

        @pl.when(worker_ref[j] >= 0)
        def _():
            keys_ref[rows, :] = fresh[rows, :]


def value_kernel(
    n_frame,
    n_head,
    n_rep,
    worker_in,
    normed_in,
    weight_in,
    cache_in,
    _,
    values_t_ref,
    masks_ref,
    worker_ref,
    normed_ref,
    weight_ref,
    values_ref,
    sems,
):
    n_local = worker_ref.shape[0]
    tokens = normed_ref.shape[0]
    block_rows = tokens // n_local
    copies = [
        pltpu.make_async_copy(source, target, sems.at[i])
        for i, (source, target) in enumerate(
            [
                (worker_in, worker_ref),
                (normed_in, normed_ref),
                (weight_in, weight_ref),
                (cache_in, values_ref),
            ]
        )
    ]
    for copy in copies:
        copy.start()
    copies[0].wait()
    frame, head, rep = lax.axis_index("frame"), lax.axis_index("head"), lax.axis_index("rep")
    n_place = n_head * n_rep
    for d in range(n_place):
        target = lax.rem(head + d // n_rep, n_head) * n_rep + lax.rem(rep + d % n_rep, n_rep)
        worker = worker_ref[target * (tokens // n_place) // block_rows]
        for s in range(n_frame):
            held = (worker >= 0) & (jnp.bitwise_xor(frame, s) == worker)
            masks_ref[d * n_frame + s : d * n_frame + s + 1, :] = jnp.full(
                (1, masks_ref.shape[1]), jnp.where(held, 1.0, 0.0), jnp.float32
            )
    for copy in copies[1:]:
        copy.wait()
    fresh = jnp.dot(
        normed_ref[...], weight_ref[...], preferred_element_type=jnp.float32
    ).astype(jnp.bfloat16)
    for j in range(n_local):
        rows = slice(j * block_rows, (j + 1) * block_rows)

        @pl.when(worker_ref[j] >= 0)
        def _():
            values_ref[rows, :] = fresh[rows, :]

    for h in range(values_ref.shape[1] // HD):
        cols = slice(h * HD, (h + 1) * HD)
        values_t_ref[cols, :] = values_ref[:, cols].T


def three_terms(x):
    first = x.astype(jnp.bfloat16).astype(jnp.float32)
    rest = x - first
    second = rest.astype(jnp.bfloat16).astype(jnp.float32)
    return [first, second, rest - second]


def collect_kernel(*refs):
    *parts, _, out_ref = refs
    out_ref[...] = sum(part[...].astype(jnp.float32) for part in parts).astype(jnp.bfloat16)


def attend_kernel(count, *refs):
    keys_ref, values_t_ref = refs[count : count + 2]
    for queries_ref, out_ref in zip(refs[:count], refs[-count:]):
        attend_slot(queries_ref, keys_ref, values_t_ref, out_ref)


def attend_slot(queries_ref, keys_ref, values_t_ref, out_ref):
    width = keys_ref.shape[1]
    stats = []
    for h in range(width // HD):
        cols = slice(h * HD, (h + 1) * HD)
        scores = lax.dot_general(
            keys_ref[:, cols],
            queries_ref[:, cols],
            (((1,), (1,)), ((), ())),
            preferred_element_type=jnp.float32,
        )
        highest = jnp.max(scores, axis=0, keepdims=True)
        weights = jnp.exp(scores - highest)
        total = jnp.sum(weights, axis=0, keepdims=True)
        out_ref[cols, :] = jnp.dot(
            values_t_ref[cols, :], weights.astype(jnp.bfloat16), preferred_element_type=jnp.float32
        ).astype(jnp.bfloat16)
        stats += three_terms(highest) + three_terms(total)
    shape = (out_ref.shape[0] - width, out_ref.shape[1])
    row = lax.broadcasted_iota(jnp.int32, shape, 0)
    tail = jnp.zeros(shape, jnp.float32)
    for i, stat in enumerate(stats):
        tail = jnp.where(row == i, stat, tail)
    out_ref[width:, :] = tail.astype(jnp.bfloat16)


def combine_kernel(*refs):
    parts, out_ref = refs[:-1], refs[-1]
    width = out_ref.shape[1]
    tails = [part[width:, :].astype(jnp.float32) for part in parts]
    for h in range(width // HD):
        cols = slice(h * HD, (h + 1) * HD)

        def stat(tail, at):
            at += 6 * h
            return tail[at : at + 1, :] + tail[at + 1 : at + 2, :] + tail[at + 2 : at + 3, :]

        maxima = [stat(tail, 0) for tail in tails]
        highest = functools.reduce(jnp.maximum, maxima)
        factors = [jnp.exp(m - highest) for m in maxima]
        total = sum(stat(tail, 3) * factor for tail, factor in zip(tails, factors))
        summed = sum(
            part[cols, :].astype(jnp.float32) * factor for part, factor in zip(parts, factors)
        )
        out_ref[:, cols] = (summed / total).T.astype(jnp.bfloat16)


def select_kernel(n_frame, n_head, n_rep, *refs):
    slots, masks_ref = refs[:n_frame], refs[n_frame]
    first = len(refs) - (len(refs) - n_frame - 1 - n_head * n_rep) // 2 - n_head * n_rep
    outs = refs[first : first + n_head * n_rep]
    block_rows, width = slots[0].shape
    rows = outs[0].shape[0]
    head, rep = lax.axis_index("head"), lax.axis_index("rep")
    for d in range(n_head * n_rep):
        if rows == block_rows:
            some = slice(None)
        else:
            target = lax.rem(head + d // n_rep, n_head) * n_rep + lax.rem(rep + d % n_rep, n_rep)
            some = pl.ds(pl.multiple_of(lax.rem(target * rows, block_rows), rows), rows)
        for h in range(width // HD):
            cols = slice(h * HD, (h + 1) * HD)
            chosen = jnp.zeros((rows, HD), jnp.float32)
            for s in range(n_frame):
                mask = masks_ref[d * n_frame + s : d * n_frame + s + 1, :]
                chosen = jnp.where(mask > 0.5, slots[s][some, cols].astype(jnp.float32), chosen)
            outs[d][:, cols] = chosen.astype(jnp.bfloat16)


def project_near_kernel(*refs):
    refs, out_ref = refs[:-1], refs[-1]
    parts, weights = refs[: len(refs) // 2], refs[len(refs) // 2 :]
    for start in range(0, out_ref.shape[1], COLUMNS):
        cols = slice(start, start + COLUMNS)
        out_ref[:, cols] = sum(
            jnp.dot(part[...], weight[:, cols], preferred_element_type=jnp.float32)
            for part, weight in zip(parts, weights)
        )


def project_kernel(modulation_ref, near_ref, *refs):
    refs, (out, total_ref, sems) = refs[:-3], refs[-3:]
    parts, weights = refs[: len(refs) // 2], refs[len(refs) // 2 :]
    copies = []
    for i, start in enumerate(range(0, total_ref.shape[1], COLUMNS)):
        cols = slice(start, start + COLUMNS)
        total = near_ref[:, cols] + sum(
            jnp.dot(part[...], weight[:, cols], preferred_element_type=jnp.float32)
            for part, weight in zip(parts, weights)
        )
        total_ref[:, cols] = total * modulation_ref[2:3, cols]
        copies.append(pltpu.make_async_copy(total_ref.at[:, cols], out.at[:, cols], sems.at[i]))
        copies[-1].start()
    for copy in copies:
        copy.wait()


def params(mib):
    return pltpu.CompilerParams(vmem_limit_bytes=mib * MIB)


def cost(flops, moved, exps=0):
    return pl.CostEstimate(flops=flops, bytes_accessed=moved, transcendentals=exps)


def per_device(
    n_frame,
    n_head,
    n_rep,
    latents,
    modulation,
    key_cache,
    value_cache,
    block_worker,
    query_weight,
    key_weight,
    value_weight,
    out_weight,
):
    tokens, model = latents.shape
    n_local = block_worker.shape[0]
    block_rows = tokens // n_local
    width = query_weight.shape[1]
    n_place = n_head * n_rep
    own_rows = tokens // n_place
    tail = TAIL * -(-6 * (width // HD) // TAIL)
    half = jnp.bfloat16

    def along_frame(x, s):
        return lax.ppermute(x, "frame", [(i, i ^ s) for i in range(n_frame)])

    def along_head(x, shift):
        return lax.ppermute(x, "head", [(i, (i + shift) % n_head) for i in range(n_head)])

    def along_rep(x, shift):
        return lax.ppermute(x, "rep", [(i, (i + shift) % n_rep) for i in range(n_rep)])

    def in_frame(x, d):
        pairs = []
        for h in range(n_head):
            for r in range(n_rep):
                to = ((h + d // n_rep) % n_head) * n_rep + (r + d % n_rep) % n_rep
                pairs.append((h * n_rep + r, to))
        return lax.ppermute(x, ("head", "rep"), pairs)


    *slots, normed = pl.pallas_call(
        functools.partial(query_kernel, n_frame),
        out_shape=[jax.ShapeDtypeStruct((block_rows, width), half)] * n_frame
        + [jax.ShapeDtypeStruct(latents.shape, half)],
        in_specs=[HBM] * 4,
        out_specs=[VMEM] * n_frame + [HBM],
        scratch_shapes=[
            pltpu.SMEM(block_worker.shape, jnp.int32),
            pltpu.VMEM(latents.shape, half),
            pltpu.VMEM(modulation.shape, jnp.float32),
            pltpu.VMEM(query_weight.shape, half),
            pltpu.VMEM(latents.shape, half),
            pltpu.VMEM((tokens, width), half),
            pltpu.VMEM((CHUNK, model), jnp.float32),
            pltpu.VMEM((CHUNK, model), jnp.float32),
            pltpu.SemaphoreType.DMA((3 + 2 * n_local,)),
        ],
        compiler_params=params(60),
        cost_estimate=cost(2 * tokens * model * width, 2 * tokens * model + 2 * model * width),
        name="queries",
    )(block_worker, latents, modulation, query_weight)
    later_weight, normed = lax.optimization_barrier((out_weight, normed))
    across = [along_head(later_weight, dh) for dh in range(1, n_head)]
    arrived = [along_frame(slots[s], s) for s in range(n_frame - 1, 0, -1)]

    keys = pl.pallas_call(
        key_kernel,
        out_shape=jax.ShapeDtypeStruct((tokens, width), half),
        in_specs=[HBM] * 4,
        out_specs=VMEM,
        scratch_shapes=[
            pltpu.SMEM(block_worker.shape, jnp.int32),
            pltpu.VMEM(latents.shape, half),
            pltpu.VMEM(key_weight.shape, half),
            pltpu.SemaphoreType.DMA((4,)),
        ],
        compiler_params=params(53),
        cost_estimate=cost(2 * tokens * model * width, 6 * tokens * model),
        name="keys",
    )(block_worker, normed, key_weight, key_cache)

    mine = pl.pallas_call(
        collect_kernel,
        out_shape=jax.ShapeDtypeStruct((block_rows, width), half),
        in_specs=[VMEM] * n_frame + [ANY],
        out_specs=VMEM,
        compiler_params=params(16),
        cost_estimate=cost(n_frame * block_rows * width, 2 * n_frame * block_rows * width),
        name="collect",
    )(slots[0], *arrived, keys)

    values_t, masks = pl.pallas_call(
        functools.partial(value_kernel, n_frame, n_head, n_rep),
        out_shape=[
            jax.ShapeDtypeStruct((width, tokens), half),
            jax.ShapeDtypeStruct((n_place * n_frame, HD), jnp.float32),
        ],
        in_specs=[HBM] * 4 + [ANY],
        out_specs=[VMEM] * 2,
        scratch_shapes=[
            pltpu.SMEM(block_worker.shape, jnp.int32),
            pltpu.VMEM(latents.shape, half),
            pltpu.VMEM(value_weight.shape, half),
            pltpu.VMEM(value_cache.shape, half),
            pltpu.SemaphoreType.DMA((4,)),
        ],
        compiler_params=params(53),
        cost_estimate=cost(2 * tokens * model * width, 6 * tokens * model),
        name="values",
    )(block_worker, normed, value_weight, value_cache, mine)

    def attend(queries, after=()):
        count = len(queries)
        return pl.pallas_call(
            functools.partial(attend_kernel, count),
            out_shape=[jax.ShapeDtypeStruct((width + tail, block_rows), half)] * count,
            in_specs=[VMEM] * (count + 2) + [ANY] * len(after),
            out_specs=[VMEM] * count,
            compiler_params=params(16),
            cost_estimate=cost(
                4 * tokens * block_rows * width * count,
                20 * tokens * width,
                tokens * block_rows * width // HD * count,
            ),
            name="attend",
        )(*queries, keys, values_t, *after)

    far_first = list(range(n_frame - 1, 0, -1))
    shared = [along_frame(mine, s) for s in reversed(far_first)]
    own = list(attend([mine]))
    partial = []
    for start in range(0, n_frame - 1, SLOTS):
        partial += attend(shared[start : start + SLOTS], own)
    sent = [along_frame(x, s) for s, x in zip(reversed(far_first), partial)][::-1]
    attended = pl.pallas_call(
        combine_kernel,
        out_shape=jax.ShapeDtypeStruct((block_rows, width), half),
        in_specs=[VMEM] * n_frame,
        out_specs=VMEM,
        compiler_params=params(16),
        cost_estimate=cost(4 * n_frame * block_rows * width, 2 * n_frame * block_rows * width),
        name="combine",
    )(*own, *sent)
    copies = {s: along_frame(attended, s) for s in far_first}
    copies = [attended] + [copies[s] for s in range(1, n_frame)]
    pieces = pl.pallas_call(
        functools.partial(select_kernel, n_frame, n_head, n_rep),
        out_shape=[jax.ShapeDtypeStruct((own_rows, width), half)] * n_place
        + [jax.ShapeDtypeStruct(w.shape, w.dtype) for w in across],
        in_specs=[VMEM] * (n_frame + 1) + [ANY] * len(across),
        out_specs=[VMEM] * n_place + [ANY] * len(across),
        input_output_aliases={n_frame + 1 + i: n_place + i for i in range(len(across))},
        compiler_params=params(16),
        cost_estimate=cost(0, 4 * n_frame * block_rows * width),
        name="select",
    )(*copies, masks, *across)
    pieces, across = pieces[:n_place], list(pieces[n_place:])
    moved = {d: in_frame(pieces[d], d) for d in range(n_place - 1, 0, -1)}
    pieces = [pieces[0]] + [moved[d] for d in range(1, n_place)]

    weights = []
    for held in [out_weight] + across:
        weights += [held] + [along_rep(held, dr) for dr in range(1, n_rep)]
    near = pl.pallas_call(
        project_near_kernel,
        out_shape=jax.ShapeDtypeStruct((own_rows, model), jnp.float32),
        in_specs=[VMEM] * (2 * n_rep),
        out_specs=VMEM,
        compiler_params=params(16),
        cost_estimate=cost(2 * own_rows * model * width * n_rep, 4 * model * width * n_rep),
        name="project_near",
    )(*pieces[:n_rep], *weights[:n_rep])
    return pl.pallas_call(
        project_kernel,
        out_shape=jax.ShapeDtypeStruct((own_rows, model), jnp.float32),
        in_specs=[VMEM] * (2 + 2 * (n_place - n_rep)),
        out_specs=ANY,
        scratch_shapes=[
            pltpu.VMEM((own_rows, model), jnp.float32),
            pltpu.SemaphoreType.DMA((-(-model // COLUMNS),)),
        ],
        compiler_params=params(16),
        cost_estimate=cost(2 * own_rows * model * width * n_rep, 2 * model * width * n_place),
        name="project",
    )(modulation, near, *pieces[n_rep:], *weights[n_rep:])


def solution(mesh):
    in_specs = (
        P(("groups", "frame"), None),
        P("groups", None),
        P(("groups", "frame"), ("head", "rep")),
        P(("groups", "frame"), ("head", "rep")),
        P(("groups", "frame")),
        P(None, ("head", "rep")),
        P(None, ("head", "rep")),
        P(None, ("head", "rep")),
        P(("head", "rep"), None),
    )
    out_specs = P(("groups", "frame", "head", "rep"), None)
    body = functools.partial(
        per_device, mesh.shape["frame"], mesh.shape["head"], mesh.shape["rep"]
    )
    return jax.shard_map(body, mesh=mesh, in_specs=in_specs, out_specs=out_specs, check_vma=False)
```

```python
import functools

import jax
import jax.numpy as jnp
from jax import lax
from jax.experimental import pallas as pl
from jax.experimental.pallas import tpu as pltpu
from jax.sharding import PartitionSpec as P

HD = 128
EPS = 1e-06
CHUNK = 16
UNROLL = 8
COLUMNS = 512
SLOTS = 3
TAIL = 16
MIB = 1 << 20

VMEM = pl.BlockSpec(memory_space=pltpu.VMEM)
HBM = pl.BlockSpec(memory_space=pltpu.HBM)
ANY = pl.BlockSpec(memory_space=pl.ANY)


def normalize_block(latents_ref, gain_ref, shift_ref, normed_ref, start, block_rows):
    def one_chunk(c, carry):
        at = pl.multiple_of(start + c * CHUNK, CHUNK)
        floats = latents_ref[pl.ds(at, CHUNK), :].astype(jnp.float32)
        center = floats - jnp.mean(floats, axis=-1, keepdims=True)
        spread = jnp.mean(center * center, axis=-1, keepdims=True)
        normed_ref[pl.ds(at, CHUNK), :] = (
            center * lax.rsqrt(spread + EPS) * gain_ref[...] + shift_ref[...]
        ).astype(jnp.bfloat16)
        return carry

    lax.fori_loop(0, block_rows // CHUNK, one_chunk, 0, unroll=UNROLL)


def query_kernel(n_frame, worker_in, latents_in, modulation_in, weight_in, *rest):
    outs, normed_out = rest[:n_frame], rest[n_frame]
    (
        worker_ref,
        latents_ref,
        modulation_ref,
        weight_ref,
        normed_ref,
        queries_ref,
        gain_ref,
        shift_ref,
        sems,
    ) = rest[n_frame + 1 :]
    n_local = worker_ref.shape[0]
    block_rows = latents_ref.shape[0] // n_local
    frame = lax.axis_index("frame")
    blocks = [slice(j * block_rows, (j + 1) * block_rows) for j in range(n_local)]
    first = [
        pltpu.make_async_copy(worker_in, worker_ref, sems.at[0]),
        pltpu.make_async_copy(modulation_in, modulation_ref, sems.at[1]),
    ]
    each = [
        pltpu.make_async_copy(latents_in.at[rows, :], latents_ref.at[rows, :], sems.at[3 + j])
        for j, rows in enumerate(blocks)
    ]
    back = [
        pltpu.make_async_copy(
            normed_ref.at[rows, :], normed_out.at[rows, :], sems.at[3 + n_local + j]
        )
        for j, rows in enumerate(blocks)
    ]
    weight = pltpu.make_async_copy(weight_in, weight_ref, sems.at[2])
    for copy in first + each + [weight]:
        copy.start()
    for s in range(n_frame):
        outs[s][...] = jnp.zeros_like(outs[s])
    for copy in first:
        copy.wait()
    gain_ref[...] = jnp.broadcast_to(1.0 + modulation_ref[1:2, :], gain_ref.shape)
    shift_ref[...] = jnp.broadcast_to(modulation_ref[0:1, :], shift_ref.shape)
    for j in range(n_local):
        each[j].wait()

        @pl.when(worker_ref[j] >= 0)
        def _():
            normalize_block(
                latents_ref, gain_ref, shift_ref, normed_ref, j * block_rows, block_rows
            )
            back[j].start()

    weight.wait()

    @pl.when(functools.reduce(jnp.maximum, [worker_ref[j] for j in range(n_local)]) >= 0)
    def _():
        queries_ref[...] = (
            jnp.dot(normed_ref[...], weight_ref[...], preferred_element_type=jnp.float32)
            * HD ** (-0.5)
        ).astype(jnp.bfloat16)

    for j in range(n_local):
        worker = worker_ref[j]
        for s in range(n_frame):

            @pl.when((worker >= 0) & (jnp.bitwise_xor(frame, s) == worker))
            def _():
                outs[s][...] = queries_ref[blocks[j], :]

        @pl.when(worker >= 0)
        def _():
            back[j].wait()


def key_kernel(
    worker_in, normed_in, weight_in, cache_in, keys_ref, worker_ref, normed_ref, weight_ref, sems
):
    n_local = worker_ref.shape[0]
    block_rows = normed_ref.shape[0] // n_local
    copies = [
        pltpu.make_async_copy(source, target, sems.at[i])
        for i, (source, target) in enumerate(
            [
                (worker_in, worker_ref),
                (normed_in, normed_ref),
                (weight_in, weight_ref),
                (cache_in, keys_ref),
            ]
        )
    ]
    for copy in copies:
        copy.start()
    for copy in copies:
        copy.wait()
    fresh = jnp.dot(
        normed_ref[...], weight_ref[...], preferred_element_type=jnp.float32
    ).astype(jnp.bfloat16)
    for j in range(n_local):
        rows = slice(j * block_rows, (j + 1) * block_rows)

        @pl.when(worker_ref[j] >= 0)
        def _():
            keys_ref[rows, :] = fresh[rows, :]


def value_kernel(
    n_frame,
    n_head,
    n_rep,
    worker_in,
    normed_in,
    weight_in,
    cache_in,
    _,
    values_t_ref,
    masks_ref,
    worker_ref,
    normed_ref,
    weight_ref,
    values_ref,
    sems,
):
    n_local = worker_ref.shape[0]
    tokens = normed_ref.shape[0]
    block_rows = tokens // n_local
    copies = [
        pltpu.make_async_copy(source, target, sems.at[i])
        for i, (source, target) in enumerate(
            [
                (worker_in, worker_ref),
                (normed_in, normed_ref),
                (weight_in, weight_ref),
                (cache_in, values_ref),
            ]
        )
    ]
    for copy in copies:
        copy.start()
    copies[0].wait()
    frame, head, rep = lax.axis_index("frame"), lax.axis_index("head"), lax.axis_index("rep")
    n_place = n_head * n_rep
    for d in range(n_place):
        target = lax.rem(head + d // n_rep, n_head) * n_rep + lax.rem(rep + d % n_rep, n_rep)
        worker = worker_ref[target * (tokens // n_place) // block_rows]
        for s in range(n_frame):
            held = (worker >= 0) & (jnp.bitwise_xor(frame, s) == worker)
            masks_ref[d * n_frame + s : d * n_frame + s + 1, :] = jnp.full(
                (1, masks_ref.shape[1]), jnp.where(held, 1.0, 0.0), jnp.float32
            )
    for copy in copies[1:]:
        copy.wait()
    fresh = jnp.dot(
        normed_ref[...], weight_ref[...], preferred_element_type=jnp.float32
    ).astype(jnp.bfloat16)
    for j in range(n_local):
        rows = slice(j * block_rows, (j + 1) * block_rows)

        @pl.when(worker_ref[j] >= 0)
        def _():
            values_ref[rows, :] = fresh[rows, :]

    for h in range(values_ref.shape[1] // HD):
        cols = slice(h * HD, (h + 1) * HD)
        values_t_ref[cols, :] = values_ref[:, cols].T


def three_terms(x):
    first = x.astype(jnp.bfloat16).astype(jnp.float32)
    rest = x - first
    second = rest.astype(jnp.bfloat16).astype(jnp.float32)
    return [first, second, rest - second]


def collect_kernel(*refs):
    *parts, _, out_ref = refs
    out_ref[...] = sum(part[...].astype(jnp.float32) for part in parts).astype(jnp.bfloat16)


def attend_kernel(count, *refs):
    keys_ref, values_t_ref = refs[count : count + 2]
    for queries_ref, out_ref in zip(refs[:count], refs[-count:]):
        attend_slot(queries_ref, keys_ref, values_t_ref, out_ref)


def attend_slot(queries_ref, keys_ref, values_t_ref, out_ref):
    width = keys_ref.shape[1]
    stats = []
    for h in range(width // HD):
        cols = slice(h * HD, (h + 1) * HD)
        scores = lax.dot_general(
            keys_ref[:, cols],
            queries_ref[:, cols],
            (((1,), (1,)), ((), ())),
            preferred_element_type=jnp.float32,
        )
        highest = jnp.max(scores, axis=0, keepdims=True)
        weights = jnp.exp(scores - highest)
        total = jnp.sum(weights, axis=0, keepdims=True)
        out_ref[cols, :] = jnp.dot(
            values_t_ref[cols, :], weights.astype(jnp.bfloat16), preferred_element_type=jnp.float32
        ).astype(jnp.bfloat16)
        stats += three_terms(highest) + three_terms(total)
    shape = (out_ref.shape[0] - width, out_ref.shape[1])
    row = lax.broadcasted_iota(jnp.int32, shape, 0)
    tail = jnp.zeros(shape, jnp.float32)
    for i, stat in enumerate(stats):
        tail = jnp.where(row == i, stat, tail)
    out_ref[width:, :] = tail.astype(jnp.bfloat16)


def combine_kernel(*refs):
    parts, out_ref = refs[:-1], refs[-1]
    width = out_ref.shape[1]
    tails = [part[width:, :].astype(jnp.float32) for part in parts]
    for h in range(width // HD):
        cols = slice(h * HD, (h + 1) * HD)

        def stat(tail, at):
            at += 6 * h
            return tail[at : at + 1, :] + tail[at + 1 : at + 2, :] + tail[at + 2 : at + 3, :]

        maxima = [stat(tail, 0) for tail in tails]
        highest = functools.reduce(jnp.maximum, maxima)
        factors = [jnp.exp(m - highest) for m in maxima]
        total = sum(stat(tail, 3) * factor for tail, factor in zip(tails, factors))
        summed = sum(
            part[cols, :].astype(jnp.float32) * factor for part, factor in zip(parts, factors)
        )
        out_ref[:, cols] = (summed / total).T.astype(jnp.bfloat16)


def select_kernel(n_frame, n_head, n_rep, *refs):
    slots, masks_ref = refs[:n_frame], refs[n_frame]
    first = len(refs) - (len(refs) - n_frame - 1 - n_head * n_rep) // 2 - n_head * n_rep
    outs = refs[first : first + n_head * n_rep]
    block_rows, width = slots[0].shape
    rows = outs[0].shape[0]
    head, rep = lax.axis_index("head"), lax.axis_index("rep")
    for d in range(n_head * n_rep):
        if rows == block_rows:
            some = slice(None)
        else:
            target = lax.rem(head + d // n_rep, n_head) * n_rep + lax.rem(rep + d % n_rep, n_rep)
            some = pl.ds(pl.multiple_of(lax.rem(target * rows, block_rows), rows), rows)
        for h in range(width // HD):
            cols = slice(h * HD, (h + 1) * HD)
            chosen = jnp.zeros((rows, HD), jnp.float32)
            for s in range(n_frame):
                mask = masks_ref[d * n_frame + s : d * n_frame + s + 1, :]
                chosen = jnp.where(mask > 0.5, slots[s][some, cols].astype(jnp.float32), chosen)
            outs[d][:, cols] = chosen.astype(jnp.bfloat16)


def project_kernel(modulation_ref, *refs):
    refs, (out, total_ref, sems) = refs[:-3], refs[-3:]
    parts, weights = refs[: len(refs) // 2], refs[len(refs) // 2 :]
    copies = []
    for i, start in enumerate(range(0, total_ref.shape[1], COLUMNS)):
        cols = slice(start, start + COLUMNS)
        total = sum(
            jnp.dot(part[...], weight[:, cols], preferred_element_type=jnp.float32)
            for part, weight in zip(parts, weights)
        )
        total_ref[:, cols] = total * modulation_ref[2:3, cols]
        copies.append(pltpu.make_async_copy(total_ref.at[:, cols], out.at[:, cols], sems.at[i]))
        copies[-1].start()
    for copy in copies:
        copy.wait()


def params(mib):
    return pltpu.CompilerParams(vmem_limit_bytes=mib * MIB)


def cost(flops, moved, exps=0):
    return pl.CostEstimate(flops=flops, bytes_accessed=moved, transcendentals=exps)


def per_device(
    n_frame,
    n_head,
    n_rep,
    latents,
    modulation,
    key_cache,
    value_cache,
    block_worker,
    query_weight,
    key_weight,
    value_weight,
    out_weight,
):
    tokens, model = latents.shape
    n_local = block_worker.shape[0]
    block_rows = tokens // n_local
    width = query_weight.shape[1]
    n_place = n_head * n_rep
    own_rows = tokens // n_place
    tail = TAIL * -(-6 * (width // HD) // TAIL)
    half = jnp.bfloat16

    def along_frame(x, s):
        return lax.ppermute(x, "frame", [(i, i ^ s) for i in range(n_frame)])

    def along_head(x, shift):
        return lax.ppermute(x, "head", [(i, (i + shift) % n_head) for i in range(n_head)])

    def along_rep(x, shift):
        return lax.ppermute(x, "rep", [(i, (i + shift) % n_rep) for i in range(n_rep)])

    def in_frame(x, d):
        pairs = []
        for h in range(n_head):
            for r in range(n_rep):
                to = ((h + d // n_rep) % n_head) * n_rep + (r + d % n_rep) % n_rep
                pairs.append((h * n_rep + r, to))
        return lax.ppermute(x, ("head", "rep"), pairs)


    *slots, normed = pl.pallas_call(
        functools.partial(query_kernel, n_frame),
        out_shape=[jax.ShapeDtypeStruct((block_rows, width), half)] * n_frame
        + [jax.ShapeDtypeStruct(latents.shape, half)],
        in_specs=[HBM] * 4,
        out_specs=[VMEM] * n_frame + [HBM],
        scratch_shapes=[
            pltpu.SMEM(block_worker.shape, jnp.int32),
            pltpu.VMEM(latents.shape, half),
            pltpu.VMEM(modulation.shape, jnp.float32),
            pltpu.VMEM(query_weight.shape, half),
            pltpu.VMEM(latents.shape, half),
            pltpu.VMEM((tokens, width), half),
            pltpu.VMEM((CHUNK, model), jnp.float32),
            pltpu.VMEM((CHUNK, model), jnp.float32),
            pltpu.SemaphoreType.DMA((3 + 2 * n_local,)),
        ],
        compiler_params=params(60),
        cost_estimate=cost(2 * tokens * model * width, 2 * tokens * model + 2 * model * width),
        name="queries",
    )(block_worker, latents, modulation, query_weight)
    later_weight, normed = lax.optimization_barrier((out_weight, normed))
    across = [along_head(later_weight, dh) for dh in range(1, n_head)]
    arrived = [along_frame(slots[s], s) for s in range(n_frame - 1, 0, -1)]

    keys = pl.pallas_call(
        key_kernel,
        out_shape=jax.ShapeDtypeStruct((tokens, width), half),
        in_specs=[HBM] * 4,
        out_specs=VMEM,
        scratch_shapes=[
            pltpu.SMEM(block_worker.shape, jnp.int32),
            pltpu.VMEM(latents.shape, half),
            pltpu.VMEM(key_weight.shape, half),
            pltpu.SemaphoreType.DMA((4,)),
        ],
        compiler_params=params(53),
        cost_estimate=cost(2 * tokens * model * width, 6 * tokens * model),
        name="keys",
    )(block_worker, normed, key_weight, key_cache)

    mine = pl.pallas_call(
        collect_kernel,
        out_shape=jax.ShapeDtypeStruct((block_rows, width), half),
        in_specs=[VMEM] * n_frame + [ANY],
        out_specs=VMEM,
        compiler_params=params(16),
        cost_estimate=cost(n_frame * block_rows * width, 2 * n_frame * block_rows * width),
        name="collect",
    )(slots[0], *arrived, keys)

    values_t, masks = pl.pallas_call(
        functools.partial(value_kernel, n_frame, n_head, n_rep),
        out_shape=[
            jax.ShapeDtypeStruct((width, tokens), half),
            jax.ShapeDtypeStruct((n_place * n_frame, HD), jnp.float32),
        ],
        in_specs=[HBM] * 4 + [ANY],
        out_specs=[VMEM] * 2,
        scratch_shapes=[
            pltpu.SMEM(block_worker.shape, jnp.int32),
            pltpu.VMEM(latents.shape, half),
            pltpu.VMEM(value_weight.shape, half),
            pltpu.VMEM(value_cache.shape, half),
            pltpu.SemaphoreType.DMA((4,)),
        ],
        compiler_params=params(53),
        cost_estimate=cost(2 * tokens * model * width, 6 * tokens * model),
        name="values",
    )(block_worker, normed, value_weight, value_cache, mine)

    def attend(queries, after=()):
        count = len(queries)
        return pl.pallas_call(
            functools.partial(attend_kernel, count),
            out_shape=[jax.ShapeDtypeStruct((width + tail, block_rows), half)] * count,
            in_specs=[VMEM] * (count + 2) + [ANY] * len(after),
            out_specs=[VMEM] * count,
            compiler_params=params(16),
            cost_estimate=cost(
                4 * tokens * block_rows * width * count,
                20 * tokens * width,
                tokens * block_rows * width // HD * count,
            ),
            name="attend",
        )(*queries, keys, values_t, *after)

    far_first = list(range(n_frame - 1, 0, -1))
    shared = [along_frame(mine, s) for s in reversed(far_first)]
    own = list(attend([mine]))
    partial = []
    for start in range(0, n_frame - 1, SLOTS):
        partial += attend(shared[start : start + SLOTS], own)
    sent = [along_frame(x, s) for s, x in zip(reversed(far_first), partial)][::-1]
    attended = pl.pallas_call(
        combine_kernel,
        out_shape=jax.ShapeDtypeStruct((block_rows, width), half),
        in_specs=[VMEM] * n_frame,
        out_specs=VMEM,
        compiler_params=params(16),
        cost_estimate=cost(4 * n_frame * block_rows * width, 2 * n_frame * block_rows * width),
        name="combine",
    )(*own, *sent)
    copies = {s: along_frame(attended, s) for s in far_first}
    copies = [attended] + [copies[s] for s in range(1, n_frame)]
    pieces = pl.pallas_call(
        functools.partial(select_kernel, n_frame, n_head, n_rep),
        out_shape=[jax.ShapeDtypeStruct((own_rows, width), half)] * n_place
        + [jax.ShapeDtypeStruct(w.shape, w.dtype) for w in across],
        in_specs=[VMEM] * (n_frame + 1) + [ANY] * len(across),
        out_specs=[VMEM] * n_place + [ANY] * len(across),
        input_output_aliases={n_frame + 1 + i: n_place + i for i in range(len(across))},
        compiler_params=params(16),
        cost_estimate=cost(0, 4 * n_frame * block_rows * width),
        name="select",
    )(*copies, masks, *across)
    pieces, across = pieces[:n_place], list(pieces[n_place:])
    moved = {d: in_frame(pieces[d], d) for d in range(1, n_place)}
    pieces = [pieces[0]] + [moved[d] for d in range(1, n_place)]

    weights = []
    for held in [out_weight] + across:
        weights += [held] + [along_rep(held, dr) for dr in range(1, n_rep)]
    return pl.pallas_call(
        project_kernel,
        out_shape=jax.ShapeDtypeStruct((own_rows, model), jnp.float32),
        in_specs=[VMEM] * (1 + 2 * n_place),
        out_specs=ANY,
        scratch_shapes=[
            pltpu.VMEM((own_rows, model), jnp.float32),
            pltpu.SemaphoreType.DMA((-(-model // COLUMNS),)),
        ],
        compiler_params=params(16),
        cost_estimate=cost(2 * own_rows * model * width * n_place, 2 * model * width * n_place),
        name="project",
    )(modulation, *pieces[::-1], *weights[::-1])


def solution(mesh):
    in_specs = (
        P(("groups", "frame"), None),
        P("groups", None),
        P(("groups", "frame"), ("head", "rep")),
        P(("groups", "frame"), ("head", "rep")),
        P(("groups", "frame")),
        P(None, ("head", "rep")),
        P(None, ("head", "rep")),
        P(None, ("head", "rep")),
        P(("head", "rep"), None),
    )
    out_specs = P(("groups", "frame", "head", "rep"), None)
    body = functools.partial(
        per_device, mesh.shape["frame"], mesh.shape["head"], mesh.shape["rep"]
    )
    return jax.shard_map(body, mesh=mesh, in_specs=in_specs, out_specs=out_specs, check_vma=False)
```

```python
import functools

import jax
import jax.numpy as jnp
from jax import lax
from jax.experimental import pallas as pl
from jax.experimental.pallas import tpu as pltpu
from jax.sharding import PartitionSpec as P

HD = 128
EPS = 1e-06
CHUNK = 16
UNROLL = 8
COLUMNS = 512
SLOTS = 3
TAIL = 16
MIB = 1 << 20

VMEM = pl.BlockSpec(memory_space=pltpu.VMEM)
HBM = pl.BlockSpec(memory_space=pltpu.HBM)
ANY = pl.BlockSpec(memory_space=pl.ANY)


def normalize_block(latents_ref, gain_ref, shift_ref, normed_ref, start, block_rows):
    def one_chunk(c, carry):
        at = pl.multiple_of(start + c * CHUNK, CHUNK)
        floats = latents_ref[pl.ds(at, CHUNK), :].astype(jnp.float32)
        center = floats - jnp.mean(floats, axis=-1, keepdims=True)
        spread = jnp.mean(center * center, axis=-1, keepdims=True)
        normed_ref[pl.ds(at, CHUNK), :] = (
            center * lax.rsqrt(spread + EPS) * gain_ref[...] + shift_ref[...]
        ).astype(jnp.bfloat16)
        return carry

    lax.fori_loop(0, block_rows // CHUNK, one_chunk, 0, unroll=UNROLL)


def query_kernel(n_frame, worker_in, latents_in, modulation_in, weight_in, *rest):
    outs, normed_out = rest[:n_frame], rest[n_frame]
    (
        worker_ref,
        latents_ref,
        modulation_ref,
        weight_ref,
        normed_ref,
        queries_ref,
        gain_ref,
        shift_ref,
        sems,
    ) = rest[n_frame + 1 :]
    n_local = worker_ref.shape[0]
    block_rows = latents_ref.shape[0] // n_local
    frame = lax.axis_index("frame")
    blocks = [slice(j * block_rows, (j + 1) * block_rows) for j in range(n_local)]
    first = [
        pltpu.make_async_copy(worker_in, worker_ref, sems.at[0]),
        pltpu.make_async_copy(modulation_in, modulation_ref, sems.at[1]),
    ]
    each = [
        pltpu.make_async_copy(latents_in.at[rows, :], latents_ref.at[rows, :], sems.at[3 + j])
        for j, rows in enumerate(blocks)
    ]
    back = [
        pltpu.make_async_copy(
            normed_ref.at[rows, :], normed_out.at[rows, :], sems.at[3 + n_local + j]
        )
        for j, rows in enumerate(blocks)
    ]
    weight = pltpu.make_async_copy(weight_in, weight_ref, sems.at[2])
    for copy in first + each:
        copy.start()
    for s in range(n_frame):
        outs[s][...] = jnp.zeros_like(outs[s])
    for copy in first:
        copy.wait()
    gain_ref[...] = jnp.broadcast_to(1.0 + modulation_ref[1:2, :], gain_ref.shape)
    shift_ref[...] = jnp.broadcast_to(modulation_ref[0:1, :], shift_ref.shape)
    for j in range(n_local):
        each[j].wait()
        if j == 0:
            weight.start()

        @pl.when(worker_ref[j] >= 0)
        def _():
            normalize_block(
                latents_ref, gain_ref, shift_ref, normed_ref, j * block_rows, block_rows
            )
            back[j].start()

    weight.wait()

    @pl.when(functools.reduce(jnp.maximum, [worker_ref[j] for j in range(n_local)]) >= 0)
    def _():
        queries_ref[...] = (
            jnp.dot(normed_ref[...], weight_ref[...], preferred_element_type=jnp.float32)
            * HD ** (-0.5)
        ).astype(jnp.bfloat16)

    for j in range(n_local):
        worker = worker_ref[j]
        for s in range(n_frame):

            @pl.when((worker >= 0) & (jnp.bitwise_xor(frame, s) == worker))
            def _():
                outs[s][...] = queries_ref[blocks[j], :]

        @pl.when(worker >= 0)
        def _():
            back[j].wait()


def key_kernel(
    worker_in, normed_in, weight_in, cache_in, keys_ref, worker_ref, normed_ref, weight_ref, sems
):
    n_local = worker_ref.shape[0]
    block_rows = normed_ref.shape[0] // n_local
    copies = [
        pltpu.make_async_copy(source, target, sems.at[i])
        for i, (source, target) in enumerate(
            [
                (worker_in, worker_ref),
                (normed_in, normed_ref),
                (weight_in, weight_ref),
                (cache_in, keys_ref),
            ]
        )
    ]
    for copy in copies:
        copy.start()
    for copy in copies:
        copy.wait()
    fresh = jnp.dot(
        normed_ref[...], weight_ref[...], preferred_element_type=jnp.float32
    ).astype(jnp.bfloat16)
    for j in range(n_local):
        rows = slice(j * block_rows, (j + 1) * block_rows)

        @pl.when(worker_ref[j] >= 0)
        def _():
            keys_ref[rows, :] = fresh[rows, :]


def value_kernel(
    n_frame,
    n_head,
    n_rep,
    worker_in,
    normed_in,
    weight_in,
    cache_in,
    _,
    values_t_ref,
    masks_ref,
    worker_ref,
    normed_ref,
    weight_ref,
    values_ref,
    sems,
):
    n_local = worker_ref.shape[0]
    tokens = normed_ref.shape[0]
    block_rows = tokens // n_local
    copies = [
        pltpu.make_async_copy(source, target, sems.at[i])
        for i, (source, target) in enumerate(
            [
                (worker_in, worker_ref),
                (normed_in, normed_ref),
                (weight_in, weight_ref),
                (cache_in, values_ref),
            ]
        )
    ]
    for copy in copies:
        copy.start()
    copies[0].wait()
    frame, head, rep = lax.axis_index("frame"), lax.axis_index("head"), lax.axis_index("rep")
    n_place = n_head * n_rep
    for d in range(n_place):
        target = lax.rem(head + d // n_rep, n_head) * n_rep + lax.rem(rep + d % n_rep, n_rep)
        worker = worker_ref[target * (tokens // n_place) // block_rows]
        for s in range(n_frame):
            held = (worker >= 0) & (jnp.bitwise_xor(frame, s) == worker)
            masks_ref[d * n_frame + s : d * n_frame + s + 1, :] = jnp.full(
                (1, masks_ref.shape[1]), jnp.where(held, 1.0, 0.0), jnp.float32
            )
    for copy in copies[1:]:
        copy.wait()
    fresh = jnp.dot(
        normed_ref[...], weight_ref[...], preferred_element_type=jnp.float32
    ).astype(jnp.bfloat16)
    for j in range(n_local):
        rows = slice(j * block_rows, (j + 1) * block_rows)

        @pl.when(worker_ref[j] >= 0)
        def _():
            values_ref[rows, :] = fresh[rows, :]

    for h in range(values_ref.shape[1] // HD):
        cols = slice(h * HD, (h + 1) * HD)
        values_t_ref[cols, :] = values_ref[:, cols].T


def three_terms(x):
    first = x.astype(jnp.bfloat16).astype(jnp.float32)
    rest = x - first
    second = rest.astype(jnp.bfloat16).astype(jnp.float32)
    return [first, second, rest - second]


def collect_kernel(*refs):
    *parts, _, out_ref = refs
    out_ref[...] = sum(part[...].astype(jnp.float32) for part in parts).astype(jnp.bfloat16)


def attend_kernel(count, *refs):
    keys_ref, values_t_ref = refs[count : count + 2]
    for queries_ref, out_ref in zip(refs[:count], refs[-count:]):
        attend_slot(queries_ref, keys_ref, values_t_ref, out_ref)


def attend_slot(queries_ref, keys_ref, values_t_ref, out_ref):
    width = keys_ref.shape[1]
    stats = []
    for h in range(width // HD):
        cols = slice(h * HD, (h + 1) * HD)
        scores = lax.dot_general(
            keys_ref[:, cols],
            queries_ref[:, cols],
            (((1,), (1,)), ((), ())),
            preferred_element_type=jnp.float32,
        )
        highest = jnp.max(scores, axis=0, keepdims=True)
        weights = jnp.exp(scores - highest)
        total = jnp.sum(weights, axis=0, keepdims=True)
        out_ref[cols, :] = jnp.dot(
            values_t_ref[cols, :], weights.astype(jnp.bfloat16), preferred_element_type=jnp.float32
        ).astype(jnp.bfloat16)
        stats += three_terms(highest) + three_terms(total)
    shape = (out_ref.shape[0] - width, out_ref.shape[1])
    row = lax.broadcasted_iota(jnp.int32, shape, 0)
    tail = jnp.zeros(shape, jnp.float32)
    for i, stat in enumerate(stats):
        tail = jnp.where(row == i, stat, tail)
    out_ref[width:, :] = tail.astype(jnp.bfloat16)


def combine_kernel(*refs):
    parts, out_ref = refs[:-1], refs[-1]
    width = out_ref.shape[1]
    tails = [part[width:, :].astype(jnp.float32) for part in parts]
    for h in range(width // HD):
        cols = slice(h * HD, (h + 1) * HD)

        def stat(tail, at):
            at += 6 * h
            return tail[at : at + 1, :] + tail[at + 1 : at + 2, :] + tail[at + 2 : at + 3, :]

        maxima = [stat(tail, 0) for tail in tails]
        highest = functools.reduce(jnp.maximum, maxima)
        factors = [jnp.exp(m - highest) for m in maxima]
        total = sum(stat(tail, 3) * factor for tail, factor in zip(tails, factors))
        summed = sum(
            part[cols, :].astype(jnp.float32) * factor for part, factor in zip(parts, factors)
        )
        out_ref[:, cols] = (summed / total).T.astype(jnp.bfloat16)


def select_kernel(n_frame, n_head, n_rep, *refs):
    slots, masks_ref = refs[:n_frame], refs[n_frame]
    first = len(refs) - (len(refs) - n_frame - 1 - n_head * n_rep) // 2 - n_head * n_rep
    outs = refs[first : first + n_head * n_rep]
    block_rows, width = slots[0].shape
    rows = outs[0].shape[0]
    head, rep = lax.axis_index("head"), lax.axis_index("rep")
    for d in range(n_head * n_rep):
        if rows == block_rows:
            some = slice(None)
        else:
            target = lax.rem(head + d // n_rep, n_head) * n_rep + lax.rem(rep + d % n_rep, n_rep)
            some = pl.ds(pl.multiple_of(lax.rem(target * rows, block_rows), rows), rows)
        for h in range(width // HD):
            cols = slice(h * HD, (h + 1) * HD)
            chosen = jnp.zeros((rows, HD), jnp.float32)
            for s in range(n_frame):
                mask = masks_ref[d * n_frame + s : d * n_frame + s + 1, :]
                chosen = jnp.where(mask > 0.5, slots[s][some, cols].astype(jnp.float32), chosen)
            outs[d][:, cols] = chosen.astype(jnp.bfloat16)


def project_own_kernel(part_ref, weight_ref, out_ref):
    for start in range(0, out_ref.shape[1], COLUMNS):
        cols = slice(start, start + COLUMNS)
        out_ref[:, cols] = jnp.dot(
            part_ref[...], weight_ref[:, cols], preferred_element_type=jnp.float32
        )


def project_kernel(modulation_ref, own_ref, *refs):
    refs, (out, total_ref, sems) = refs[:-3], refs[-3:]
    parts, weights = refs[: len(refs) // 2], refs[len(refs) // 2 :]
    copies = []
    for i, start in enumerate(range(0, total_ref.shape[1], COLUMNS)):
        cols = slice(start, start + COLUMNS)
        total = own_ref[:, cols] + sum(
            jnp.dot(part[...], weight[:, cols], preferred_element_type=jnp.float32)
            for part, weight in zip(parts, weights)
        )
        total_ref[:, cols] = total * modulation_ref[2:3, cols]
        copies.append(pltpu.make_async_copy(total_ref.at[:, cols], out.at[:, cols], sems.at[i]))
        copies[-1].start()
    for copy in copies:
        copy.wait()


def params(mib):
    return pltpu.CompilerParams(vmem_limit_bytes=mib * MIB)


def cost(flops, moved, exps=0):
    return pl.CostEstimate(flops=flops, bytes_accessed=moved, transcendentals=exps)


def per_device(
    n_frame,
    n_head,
    n_rep,
    latents,
    modulation,
    key_cache,
    value_cache,
    block_worker,
    query_weight,
    key_weight,
    value_weight,
    out_weight,
):
    tokens, model = latents.shape
    n_local = block_worker.shape[0]
    block_rows = tokens // n_local
    width = query_weight.shape[1]
    n_place = n_head * n_rep
    own_rows = tokens // n_place
    tail = TAIL * -(-6 * (width // HD) // TAIL)
    half = jnp.bfloat16

    def along_frame(x, s):
        return lax.ppermute(x, "frame", [(i, i ^ s) for i in range(n_frame)])

    def along_head(x, shift):
        return lax.ppermute(x, "head", [(i, (i + shift) % n_head) for i in range(n_head)])

    def along_rep(x, shift):
        return lax.ppermute(x, "rep", [(i, (i + shift) % n_rep) for i in range(n_rep)])

    def in_frame(x, d):
        pairs = []
        for h in range(n_head):
            for r in range(n_rep):
                to = ((h + d // n_rep) % n_head) * n_rep + (r + d % n_rep) % n_rep
                pairs.append((h * n_rep + r, to))
        return lax.ppermute(x, ("head", "rep"), pairs)


    *slots, normed = pl.pallas_call(
        functools.partial(query_kernel, n_frame),
        out_shape=[jax.ShapeDtypeStruct((block_rows, width), half)] * n_frame
        + [jax.ShapeDtypeStruct(latents.shape, half)],
        in_specs=[HBM] * 4,
        out_specs=[VMEM] * n_frame + [HBM],
        scratch_shapes=[
            pltpu.SMEM(block_worker.shape, jnp.int32),
            pltpu.VMEM(latents.shape, half),
            pltpu.VMEM(modulation.shape, jnp.float32),
            pltpu.VMEM(query_weight.shape, half),
            pltpu.VMEM(latents.shape, half),
            pltpu.VMEM((tokens, width), half),
            pltpu.VMEM((CHUNK, model), jnp.float32),
            pltpu.VMEM((CHUNK, model), jnp.float32),
            pltpu.SemaphoreType.DMA((3 + 2 * n_local,)),
        ],
        compiler_params=params(60),
        cost_estimate=cost(2 * tokens * model * width, 2 * tokens * model + 2 * model * width),
        name="queries",
    )(block_worker, latents, modulation, query_weight)
    later_weight, normed = lax.optimization_barrier((out_weight, normed))
    across = [along_head(later_weight, dh) for dh in range(1, n_head)]
    arrived = [along_frame(slots[s], s) for s in range(n_frame - 1, 0, -1)]

    keys = pl.pallas_call(
        key_kernel,
        out_shape=jax.ShapeDtypeStruct((tokens, width), half),
        in_specs=[HBM] * 4,
        out_specs=VMEM,
        scratch_shapes=[
            pltpu.SMEM(block_worker.shape, jnp.int32),
            pltpu.VMEM(latents.shape, half),
            pltpu.VMEM(key_weight.shape, half),
            pltpu.SemaphoreType.DMA((4,)),
        ],
        compiler_params=params(53),
        cost_estimate=cost(2 * tokens * model * width, 6 * tokens * model),
        name="keys",
    )(block_worker, normed, key_weight, key_cache)

    mine = pl.pallas_call(
        collect_kernel,
        out_shape=jax.ShapeDtypeStruct((block_rows, width), half),
        in_specs=[VMEM] * n_frame + [ANY],
        out_specs=VMEM,
        compiler_params=params(16),
        cost_estimate=cost(n_frame * block_rows * width, 2 * n_frame * block_rows * width),
        name="collect",
    )(slots[0], *arrived, keys)

    values_t, masks = pl.pallas_call(
        functools.partial(value_kernel, n_frame, n_head, n_rep),
        out_shape=[
            jax.ShapeDtypeStruct((width, tokens), half),
            jax.ShapeDtypeStruct((n_place * n_frame, HD), jnp.float32),
        ],
        in_specs=[HBM] * 4 + [ANY],
        out_specs=[VMEM] * 2,
        scratch_shapes=[
            pltpu.SMEM(block_worker.shape, jnp.int32),
            pltpu.VMEM(latents.shape, half),
            pltpu.VMEM(value_weight.shape, half),
            pltpu.VMEM(value_cache.shape, half),
            pltpu.SemaphoreType.DMA((4,)),
        ],
        compiler_params=params(53),
        cost_estimate=cost(2 * tokens * model * width, 6 * tokens * model),
        name="values",
    )(block_worker, normed, value_weight, value_cache, mine)

    def attend(queries, after=()):
        count = len(queries)
        return pl.pallas_call(
            functools.partial(attend_kernel, count),
            out_shape=[jax.ShapeDtypeStruct((width + tail, block_rows), half)] * count,
            in_specs=[VMEM] * (count + 2) + [ANY] * len(after),
            out_specs=[VMEM] * count,
            compiler_params=params(16),
            cost_estimate=cost(
                4 * tokens * block_rows * width * count,
                20 * tokens * width,
                tokens * block_rows * width // HD * count,
            ),
            name="attend",
        )(*queries, keys, values_t, *after)

    far_first = list(range(n_frame - 1, 0, -1))
    shared = [along_frame(mine, s) for s in reversed(far_first)]
    own = list(attend([mine]))
    partial = []
    for start in range(0, n_frame - 1, SLOTS):
        partial += attend(shared[start : start + SLOTS], own)
    sent = [along_frame(x, s) for s, x in zip(reversed(far_first), partial)][::-1]
    attended = pl.pallas_call(
        combine_kernel,
        out_shape=jax.ShapeDtypeStruct((block_rows, width), half),
        in_specs=[VMEM] * n_frame,
        out_specs=VMEM,
        compiler_params=params(16),
        cost_estimate=cost(4 * n_frame * block_rows * width, 2 * n_frame * block_rows * width),
        name="combine",
    )(*own, *sent)
    copies = {s: along_frame(attended, s) for s in far_first}
    copies = [attended] + [copies[s] for s in range(1, n_frame)]
    pieces = pl.pallas_call(
        functools.partial(select_kernel, n_frame, n_head, n_rep),
        out_shape=[jax.ShapeDtypeStruct((own_rows, width), half)] * n_place
        + [jax.ShapeDtypeStruct(w.shape, w.dtype) for w in across],
        in_specs=[VMEM] * (n_frame + 1) + [ANY] * len(across),
        out_specs=[VMEM] * n_place + [ANY] * len(across),
        input_output_aliases={n_frame + 1 + i: n_place + i for i in range(len(across))},
        compiler_params=params(16),
        cost_estimate=cost(0, 4 * n_frame * block_rows * width),
        name="select",
    )(*copies, masks, *across)
    pieces, across = pieces[:n_place], list(pieces[n_place:])
    moved = {d: in_frame(pieces[d], d) for d in range(1, n_place)}
    pieces = [pieces[0]] + [moved[d] for d in range(1, n_place)]

    weights = []
    for held in [out_weight] + across:
        weights += [held] + [along_rep(held, dr) for dr in range(1, n_rep)]
    own = pl.pallas_call(
        project_own_kernel,
        out_shape=jax.ShapeDtypeStruct((own_rows, model), jnp.float32),
        in_specs=[VMEM] * 2,
        out_specs=VMEM,
        compiler_params=params(16),
        cost_estimate=cost(2 * own_rows * model * width, 4 * model * width),
        name="project_own",
    )(pieces[0], weights[0])
    return pl.pallas_call(
        project_kernel,
        out_shape=jax.ShapeDtypeStruct((own_rows, model), jnp.float32),
        in_specs=[VMEM] * (2 * n_place),
        out_specs=ANY,
        scratch_shapes=[
            pltpu.VMEM((own_rows, model), jnp.float32),
            pltpu.SemaphoreType.DMA((-(-model // COLUMNS),)),
        ],
        compiler_params=params(16),
        cost_estimate=cost(2 * own_rows * model * width * n_place, 2 * model * width * n_place),
        name="project",
    )(modulation, own, *pieces[:0:-1], *weights[:0:-1])


def solution(mesh):
    in_specs = (
        P(("groups", "frame"), None),
        P("groups", None),
        P(("groups", "frame"), ("head", "rep")),
        P(("groups", "frame"), ("head", "rep")),
        P(("groups", "frame")),
        P(None, ("head", "rep")),
        P(None, ("head", "rep")),
        P(None, ("head", "rep")),
        P(("head", "rep"), None),
    )
    out_specs = P(("groups", "frame", "head", "rep"), None)
    body = functools.partial(
        per_device, mesh.shape["frame"], mesh.shape["head"], mesh.shape["rep"]
    )
    return jax.shard_map(body, mesh=mesh, in_specs=in_specs, out_specs=out_specs, check_vma=False)
```

```python
import functools

import jax
import jax.numpy as jnp
from jax import lax
from jax.experimental import pallas as pl
from jax.experimental.pallas import tpu as pltpu
from jax.sharding import PartitionSpec as P

HD = 128
EPS = 1e-06
CHUNK = 16
UNROLL = 8
COLUMNS = 512
SLOTS = 3
TAIL = 16
MIB = 1 << 20

VMEM = pl.BlockSpec(memory_space=pltpu.VMEM)
HBM = pl.BlockSpec(memory_space=pltpu.HBM)
ANY = pl.BlockSpec(memory_space=pl.ANY)


def normalize_block(latents_ref, gain_ref, shift_ref, normed_ref, start, block_rows):
    def one_chunk(c, carry):
        at = pl.multiple_of(start + c * CHUNK, CHUNK)
        floats = latents_ref[pl.ds(at, CHUNK), :].astype(jnp.float32)
        center = floats - jnp.mean(floats, axis=-1, keepdims=True)
        spread = jnp.mean(center * center, axis=-1, keepdims=True)
        normed_ref[pl.ds(at, CHUNK), :] = (
            center * lax.rsqrt(spread + EPS) * gain_ref[...] + shift_ref[...]
        ).astype(jnp.bfloat16)
        return carry

    lax.fori_loop(0, block_rows // CHUNK, one_chunk, 0, unroll=UNROLL)


def query_kernel(n_frame, worker_in, latents_in, modulation_in, weight_in, *rest):
    outs, normed_out = rest[:n_frame], rest[n_frame]
    (
        worker_ref,
        latents_ref,
        modulation_ref,
        weight_ref,
        normed_ref,
        queries_ref,
        gain_ref,
        shift_ref,
        sems,
    ) = rest[n_frame + 1 :]
    n_local = worker_ref.shape[0]
    block_rows = latents_ref.shape[0] // n_local
    frame = lax.axis_index("frame")
    blocks = [slice(j * block_rows, (j + 1) * block_rows) for j in range(n_local)]
    first = [
        pltpu.make_async_copy(worker_in, worker_ref, sems.at[0]),
        pltpu.make_async_copy(modulation_in, modulation_ref, sems.at[1]),
    ]
    each = [
        pltpu.make_async_copy(latents_in.at[rows, :], latents_ref.at[rows, :], sems.at[3 + j])
        for j, rows in enumerate(blocks)
    ]
    back = [
        pltpu.make_async_copy(
            normed_ref.at[rows, :], normed_out.at[rows, :], sems.at[3 + n_local + j]
        )
        for j, rows in enumerate(blocks)
    ]
    weight = pltpu.make_async_copy(weight_in, weight_ref, sems.at[2])
    for copy in first + each + [weight]:
        copy.start()
    for s in range(n_frame):
        outs[s][...] = jnp.zeros_like(outs[s])
    for copy in first:
        copy.wait()
    gain_ref[...] = jnp.broadcast_to(1.0 + modulation_ref[1:2, :], gain_ref.shape)
    shift_ref[...] = jnp.broadcast_to(modulation_ref[0:1, :], shift_ref.shape)
    for j in range(n_local):
        each[j].wait()

        @pl.when(worker_ref[j] >= 0)
        def _():
            normalize_block(
                latents_ref, gain_ref, shift_ref, normed_ref, j * block_rows, block_rows
            )
            back[j].start()

    weight.wait()

    @pl.when(functools.reduce(jnp.maximum, [worker_ref[j] for j in range(n_local)]) >= 0)
    def _():
        queries_ref[...] = (
            jnp.dot(normed_ref[...], weight_ref[...], preferred_element_type=jnp.float32)
            * HD ** (-0.5)
        ).astype(jnp.bfloat16)

    for j in range(n_local):
        worker = worker_ref[j]
        for s in range(n_frame):

            @pl.when((worker >= 0) & (jnp.bitwise_xor(frame, s) == worker))
            def _():
                outs[s][...] = queries_ref[blocks[j], :]

        @pl.when(worker >= 0)
        def _():
            back[j].wait()


def key_kernel(
    worker_in, normed_in, weight_in, cache_in, keys_ref, worker_ref, normed_ref, weight_ref, sems
):
    n_local = worker_ref.shape[0]
    block_rows = normed_ref.shape[0] // n_local
    copies = [
        pltpu.make_async_copy(source, target, sems.at[i])
        for i, (source, target) in enumerate(
            [
                (worker_in, worker_ref),
                (normed_in, normed_ref),
                (weight_in, weight_ref),
                (cache_in, keys_ref),
            ]
        )
    ]
    for copy in copies:
        copy.start()
    for copy in copies:
        copy.wait()
    fresh = jnp.dot(
        normed_ref[...], weight_ref[...], preferred_element_type=jnp.float32
    ).astype(jnp.bfloat16)
    for j in range(n_local):
        rows = slice(j * block_rows, (j + 1) * block_rows)

        @pl.when(worker_ref[j] >= 0)
        def _():
            keys_ref[rows, :] = fresh[rows, :]


def value_kernel(
    n_frame,
    n_head,
    n_rep,
    worker_in,
    normed_in,
    weight_in,
    cache_in,
    _,
    values_t_ref,
    masks_ref,
    worker_ref,
    normed_ref,
    weight_ref,
    values_ref,
    sems,
):
    n_local = worker_ref.shape[0]
    tokens = normed_ref.shape[0]
    block_rows = tokens // n_local
    copies = [
        pltpu.make_async_copy(source, target, sems.at[i])
        for i, (source, target) in enumerate(
            [
                (worker_in, worker_ref),
                (normed_in, normed_ref),
                (weight_in, weight_ref),
                (cache_in, values_ref),
            ]
        )
    ]
    for copy in copies:
        copy.start()
    copies[0].wait()
    frame, head, rep = lax.axis_index("frame"), lax.axis_index("head"), lax.axis_index("rep")
    n_place = n_head * n_rep
    for d in range(n_place):
        target = lax.rem(head + d // n_rep, n_head) * n_rep + lax.rem(rep + d % n_rep, n_rep)
        worker = worker_ref[target * (tokens // n_place) // block_rows]
        for s in range(n_frame):
            held = (worker >= 0) & (jnp.bitwise_xor(frame, s) == worker)
            masks_ref[d * n_frame + s : d * n_frame + s + 1, :] = jnp.full(
                (1, masks_ref.shape[1]), jnp.where(held, 1.0, 0.0), jnp.float32
            )
    for copy in copies[1:]:
        copy.wait()
    fresh = jnp.dot(
        normed_ref[...], weight_ref[...], preferred_element_type=jnp.float32
    ).astype(jnp.bfloat16)
    for j in range(n_local):
        rows = slice(j * block_rows, (j + 1) * block_rows)

        @pl.when(worker_ref[j] >= 0)
        def _():
            values_ref[rows, :] = fresh[rows, :]

    for h in range(values_ref.shape[1] // HD):
        cols = slice(h * HD, (h + 1) * HD)
        values_t_ref[cols, :] = values_ref[:, cols].T


def three_terms(x):
    first = x.astype(jnp.bfloat16).astype(jnp.float32)
    rest = x - first
    second = rest.astype(jnp.bfloat16).astype(jnp.float32)
    return [first, second, rest - second]


def collect_kernel(*refs):
    *parts, _, out_ref = refs
    out_ref[...] = sum(part[...].astype(jnp.float32) for part in parts).astype(jnp.bfloat16)


def attend_kernel(count, *refs):
    keys_ref, values_t_ref = refs[count : count + 2]
    for queries_ref, out_ref in zip(refs[:count], refs[-count:]):
        attend_slot(queries_ref, keys_ref, values_t_ref, out_ref)


def attend_slot(queries_ref, keys_ref, values_t_ref, out_ref):
    width = keys_ref.shape[1]
    stats = []
    for h in range(width // HD):
        cols = slice(h * HD, (h + 1) * HD)
        scores = lax.dot_general(
            keys_ref[:, cols],
            queries_ref[:, cols],
            (((1,), (1,)), ((), ())),
            preferred_element_type=jnp.float32,
        )
        highest = jnp.max(scores, axis=0, keepdims=True)
        weights = jnp.exp(scores - highest)
        total = jnp.sum(weights, axis=0, keepdims=True)
        out_ref[cols, :] = jnp.dot(
            values_t_ref[cols, :], weights.astype(jnp.bfloat16), preferred_element_type=jnp.float32
        ).astype(jnp.bfloat16)
        stats += three_terms(highest) + three_terms(total)
    shape = (out_ref.shape[0] - width, out_ref.shape[1])
    row = lax.broadcasted_iota(jnp.int32, shape, 0)
    tail = jnp.zeros(shape, jnp.float32)
    for i, stat in enumerate(stats):
        tail = jnp.where(row == i, stat, tail)
    out_ref[width:, :] = tail.astype(jnp.bfloat16)


def combine_kernel(*refs):
    parts, out_ref = refs[:-1], refs[-1]
    width = out_ref.shape[1]
    tails = [part[width:, :].astype(jnp.float32) for part in parts]
    for h in range(width // HD):
        cols = slice(h * HD, (h + 1) * HD)

        def stat(tail, at):
            at += 6 * h
            return tail[at : at + 1, :] + tail[at + 1 : at + 2, :] + tail[at + 2 : at + 3, :]

        maxima = [stat(tail, 0) for tail in tails]
        highest = functools.reduce(jnp.maximum, maxima)
        factors = [jnp.exp(m - highest) for m in maxima]
        total = sum(stat(tail, 3) * factor for tail, factor in zip(tails, factors))
        summed = sum(
            part[cols, :].astype(jnp.float32) * factor for part, factor in zip(parts, factors)
        )
        out_ref[:, cols] = (summed / total).T.astype(jnp.bfloat16)


def select_kernel(n_frame, n_head, n_rep, *refs):
    slots, masks_ref = refs[:n_frame], refs[n_frame]
    first = len(refs) - (len(refs) - n_frame - 1 - n_head * n_rep) // 2 - n_head * n_rep
    outs = refs[first : first + n_head * n_rep]
    block_rows, width = slots[0].shape
    rows = outs[0].shape[0]
    head, rep = lax.axis_index("head"), lax.axis_index("rep")
    for d in range(n_head * n_rep):
        if rows == block_rows:
            some = slice(None)
        else:
            target = lax.rem(head + d // n_rep, n_head) * n_rep + lax.rem(rep + d % n_rep, n_rep)
            some = pl.ds(pl.multiple_of(lax.rem(target * rows, block_rows), rows), rows)
        for h in range(width // HD):
            cols = slice(h * HD, (h + 1) * HD)
            chosen = jnp.zeros((rows, HD), jnp.float32)
            for s in range(n_frame):
                mask = masks_ref[d * n_frame + s : d * n_frame + s + 1, :]
                chosen = jnp.where(mask > 0.5, slots[s][some, cols].astype(jnp.float32), chosen)
            outs[d][:, cols] = chosen.astype(jnp.bfloat16)


def project_own_kernel(part_ref, weight_ref, out_ref):
    for start in range(0, out_ref.shape[1], COLUMNS):
        cols = slice(start, start + COLUMNS)
        out_ref[:, cols] = jnp.dot(
            part_ref[...], weight_ref[:, cols], preferred_element_type=jnp.float32
        )


def project_kernel(modulation_ref, own_ref, *refs):
    refs, (out, total_ref, sems) = refs[:-3], refs[-3:]
    parts, weights = refs[: len(refs) // 2], refs[len(refs) // 2 :]
    copies = []
    for i, start in enumerate(range(0, total_ref.shape[1], COLUMNS)):
        cols = slice(start, start + COLUMNS)
        total = own_ref[:, cols] + sum(
            jnp.dot(part[...], weight[:, cols], preferred_element_type=jnp.float32)
            for part, weight in zip(parts, weights)
        )
        total_ref[:, cols] = total * modulation_ref[2:3, cols]
        copies.append(pltpu.make_async_copy(total_ref.at[:, cols], out.at[:, cols], sems.at[i]))
        copies[-1].start()
    for copy in copies:
        copy.wait()


def params(mib):
    return pltpu.CompilerParams(vmem_limit_bytes=mib * MIB)


def cost(flops, moved, exps=0):
    return pl.CostEstimate(flops=flops, bytes_accessed=moved, transcendentals=exps)


def per_device(
    n_frame,
    n_head,
    n_rep,
    latents,
    modulation,
    key_cache,
    value_cache,
    block_worker,
    query_weight,
    key_weight,
    value_weight,
    out_weight,
):
    tokens, model = latents.shape
    n_local = block_worker.shape[0]
    block_rows = tokens // n_local
    width = query_weight.shape[1]
    n_place = n_head * n_rep
    own_rows = tokens // n_place
    tail = TAIL * -(-6 * (width // HD) // TAIL)
    half = jnp.bfloat16

    def along_frame(x, s):
        return lax.ppermute(x, "frame", [(i, i ^ s) for i in range(n_frame)])

    def along_head(x, shift):
        return lax.ppermute(x, "head", [(i, (i + shift) % n_head) for i in range(n_head)])

    def along_rep(x, shift):
        return lax.ppermute(x, "rep", [(i, (i + shift) % n_rep) for i in range(n_rep)])

    def in_frame(x, d):
        pairs = []
        for h in range(n_head):
            for r in range(n_rep):
                to = ((h + d // n_rep) % n_head) * n_rep + (r + d % n_rep) % n_rep
                pairs.append((h * n_rep + r, to))
        return lax.ppermute(x, ("head", "rep"), pairs)


    *slots, normed = pl.pallas_call(
        functools.partial(query_kernel, n_frame),
        out_shape=[jax.ShapeDtypeStruct((block_rows, width), half)] * n_frame
        + [jax.ShapeDtypeStruct(latents.shape, half)],
        in_specs=[HBM] * 4,
        out_specs=[VMEM] * n_frame + [HBM],
        scratch_shapes=[
            pltpu.SMEM(block_worker.shape, jnp.int32),
            pltpu.VMEM(latents.shape, half),
            pltpu.VMEM(modulation.shape, jnp.float32),
            pltpu.VMEM(query_weight.shape, half),
            pltpu.VMEM(latents.shape, half),
            pltpu.VMEM((tokens, width), half),
            pltpu.VMEM((CHUNK, model), jnp.float32),
            pltpu.VMEM((CHUNK, model), jnp.float32),
            pltpu.SemaphoreType.DMA((3 + 2 * n_local,)),
        ],
        compiler_params=params(60),
        cost_estimate=cost(2 * tokens * model * width, 2 * tokens * model + 2 * model * width),
        name="queries",
    )(block_worker, latents, modulation, query_weight)
    later_weight, normed = lax.optimization_barrier((out_weight, normed))
    across = [along_head(later_weight, dh) for dh in range(1, n_head)]
    arrived = [along_frame(slots[s], s) for s in range(n_frame - 1, 0, -1)]

    keys = pl.pallas_call(
        key_kernel,
        out_shape=jax.ShapeDtypeStruct((tokens, width), half),
        in_specs=[HBM] * 4,
        out_specs=VMEM,
        scratch_shapes=[
            pltpu.SMEM(block_worker.shape, jnp.int32),
            pltpu.VMEM(latents.shape, half),
            pltpu.VMEM(key_weight.shape, half),
            pltpu.SemaphoreType.DMA((4,)),
        ],
        compiler_params=params(53),
        cost_estimate=cost(2 * tokens * model * width, 6 * tokens * model),
        name="keys",
    )(block_worker, normed, key_weight, key_cache)

    mine = pl.pallas_call(
        collect_kernel,
        out_shape=jax.ShapeDtypeStruct((block_rows, width), half),
        in_specs=[VMEM] * n_frame + [ANY],
        out_specs=VMEM,
        compiler_params=params(16),
        cost_estimate=cost(n_frame * block_rows * width, 2 * n_frame * block_rows * width),
        name="collect",
    )(slots[0], *arrived, keys)

    values_t, masks = pl.pallas_call(
        functools.partial(value_kernel, n_frame, n_head, n_rep),
        out_shape=[
            jax.ShapeDtypeStruct((width, tokens), half),
            jax.ShapeDtypeStruct((n_place * n_frame, HD), jnp.float32),
        ],
        in_specs=[HBM] * 4 + [ANY],
        out_specs=[VMEM] * 2,
        scratch_shapes=[
            pltpu.SMEM(block_worker.shape, jnp.int32),
            pltpu.VMEM(latents.shape, half),
            pltpu.VMEM(value_weight.shape, half),
            pltpu.VMEM(value_cache.shape, half),
            pltpu.SemaphoreType.DMA((4,)),
        ],
        compiler_params=params(53),
        cost_estimate=cost(2 * tokens * model * width, 6 * tokens * model),
        name="values",
    )(block_worker, normed, value_weight, value_cache, mine)

    def attend(queries, after=()):
        count = len(queries)
        return pl.pallas_call(
            functools.partial(attend_kernel, count),
            out_shape=[jax.ShapeDtypeStruct((width + tail, block_rows), half)] * count,
            in_specs=[VMEM] * (count + 2) + [ANY] * len(after),
            out_specs=[VMEM] * count,
            compiler_params=params(16),
            cost_estimate=cost(
                4 * tokens * block_rows * width * count,
                20 * tokens * width,
                tokens * block_rows * width // HD * count,
            ),
            name="attend",
        )(*queries, keys, values_t, *after)

    far_first = list(range(n_frame - 1, 0, -1))
    shared = [along_frame(mine, s) for s in reversed(far_first)]
    own = list(attend([mine]))
    partial = []
    for start in range(0, n_frame - 1, SLOTS):
        partial += attend(shared[start : start + SLOTS], own)
    sent = [along_frame(x, s) for s, x in zip(reversed(far_first), partial)][::-1]
    attended = pl.pallas_call(
        combine_kernel,
        out_shape=jax.ShapeDtypeStruct((block_rows, width), half),
        in_specs=[VMEM] * n_frame,
        out_specs=VMEM,
        compiler_params=params(16),
        cost_estimate=cost(4 * n_frame * block_rows * width, 2 * n_frame * block_rows * width),
        name="combine",
    )(*own, *sent)
    copies = {s: along_frame(attended, s) for s in far_first}
    copies = [attended] + [copies[s] for s in range(1, n_frame)]
    pieces = pl.pallas_call(
        functools.partial(select_kernel, n_frame, n_head, n_rep),
        out_shape=[jax.ShapeDtypeStruct((own_rows, width), half)] * n_place
        + [jax.ShapeDtypeStruct(w.shape, w.dtype) for w in across],
        in_specs=[VMEM] * (n_frame + 1) + [ANY] * len(across),
        out_specs=[VMEM] * n_place + [ANY] * len(across),
        input_output_aliases={n_frame + 1 + i: n_place + i for i in range(len(across))},
        compiler_params=params(16),
        cost_estimate=cost(0, 4 * n_frame * block_rows * width),
        name="select",
    )(*copies, masks, *across)
    pieces, across = pieces[:n_place], list(pieces[n_place:])
    moved = {d: in_frame(pieces[d], d) for d in range(1, n_place)}
    pieces = [pieces[0]] + [moved[d] for d in range(1, n_place)]

    weights = []
    for held in [out_weight] + across:
        weights += [held] + [along_rep(held, dr) for dr in range(1, n_rep)]
    own = pl.pallas_call(
        project_own_kernel,
        out_shape=jax.ShapeDtypeStruct((own_rows, model), jnp.float32),
        in_specs=[VMEM] * 2,
        out_specs=VMEM,
        compiler_params=params(16),
        cost_estimate=cost(2 * own_rows * model * width, 4 * model * width),
        name="project_own",
    )(pieces[0], weights[0])
    return pl.pallas_call(
        project_kernel,
        out_shape=jax.ShapeDtypeStruct((own_rows, model), jnp.float32),
        in_specs=[VMEM] * (2 * n_place),
        out_specs=ANY,
        scratch_shapes=[
            pltpu.VMEM((own_rows, model), jnp.float32),
            pltpu.SemaphoreType.DMA((-(-model // COLUMNS),)),
        ],
        compiler_params=params(16),
        cost_estimate=cost(2 * own_rows * model * width * n_place, 2 * model * width * n_place),
        name="project",
    )(modulation, own, *pieces[:0:-1], *weights[:0:-1])


def solution(mesh):
    in_specs = (
        P(("groups", "frame"), None),
        P("groups", None),
        P(("groups", "frame"), ("head", "rep")),
        P(("groups", "frame"), ("head", "rep")),
        P(("groups", "frame")),
        P(None, ("head", "rep")),
        P(None, ("head", "rep")),
        P(None, ("head", "rep")),
        P(("head", "rep"), None),
    )
    out_specs = P(("groups", "frame", "head", "rep"), None)
    body = functools.partial(
        per_device, mesh.shape["frame"], mesh.shape["head"], mesh.shape["rep"]
    )
    return jax.shard_map(body, mesh=mesh, in_specs=in_specs, out_specs=out_specs, check_vma=False)
```
